256 devices in a mesh: lon: 32 (over y, x, core), lat: 8 (over z).
Axes of the slice: x: 4, y: 4, z: 8, core: 2. Of those that a mesh axis runs over, the one named last changes fastest.
Arguments:
- potential_warmth: float32 [12, 128, 4096], P(None, 'lat', 'lon'), may hold values from -6 to 6
- salt_anomaly_value: float32 [12, 128, 4096], P(None, 'lat', 'lon'), may hold values from -6 to 6
- zonal_current_speed: float32 [12, 128, 4096], P(None, 'lat', 'lon'), may hold values from -1.8 to 1.8
- meridional_current_speed: float32 [12, 128, 4096], P(None, 'lat', 'lon'), may hold values from -1.8 to 1.8
- block_water_flag: int32 [8, 32], P('lat', 'lon'), may hold values 0 or 1
- water_point_flag: int32 [128, 4096], P('lat', 'lon'), may hold values 0 or 1
- wet_layer_count: int32 [128, 4096], P('lat', 'lon'), may hold values from 4 to 12
Outputs:
- temp_next: float32 [12, 128, 4096], P(None, 'lat', 'lon')
- salt_next: float32 [12, 128, 4096], P(None, 'lat', 'lon')
The draws below stay inside these ranges and needn't reach their ends.
Inputs may be any that keep to these rules, and one draw needn't show every extreme that they name: `block_water_flag`: one entry a tile.
All inputs are finite; a program needn't handle non-finite values. No bound on the sum of `block_water_flag` or of `water_point_flag` on one device may be relied on, other than what follows from the above.
Results may differ from the reference program's by a relative error of at most 0.0003.
Values sent between devices are 32-bit elements; how exact they have to be, the bound alone decides.
A program may use at most 64 MiB of HBM per device.

```python
import jax
import jax.numpy as jnp

VERTICAL_LAYERS = 12
CI = 128
CJ = 16
MESH_LONGITUDES = 4096
MESH_LATITUDES = 128
TILES_LON = 32
TILES_LAT = 8
N_LAT = 8


def place_ends(array, key, smallest, high):
    place = [jax.random.randint(jax.random.fold_in(key, axis), (), 0, length) for axis, length in enumerate(array.shape)]
    widest = array.shape.index(max(array.shape))
    neighbour = place[:widest] + [(place[widest] + 1) % array.shape[widest]] + place[widest + 1:]
    return array.at[tuple(place)].set(smallest).at[tuple(neighbour)].set(high)


def block_levels(rng, shape, cuts, low, high):
    gain = 1.0
    for position, blocks in cuts:
        steps = jax.random.uniform(jax.random.fold_in(jax.random.fold_in(rng, 6), position), (blocks,), jnp.float32, low / len(cuts), high / len(cuts))
        gain = gain * jnp.repeat(jnp.exp(steps), shape[position] // blocks).reshape((-1,) + (1,) * (len(shape) - 1 - position))
    return gain


def centred(key, dims, deviation, bound, cuts=(), kind=jnp.bfloat16):
    drawn = deviation * jax.random.normal(key, dims, jnp.float32)
    if cuts:
        drawn = drawn * block_levels(key, dims, cuts, -0.22, 0.18)
    return jnp.clip(drawn, -bound, bound).astype(kind)


def setup_inputs(seed: int = 0) -> dict:
    keys = jax.random.split(jax.random.key(seed), 8)
    return {
        "potential_warmth": centred(keys[0], (VERTICAL_LAYERS, MESH_LATITUDES, MESH_LONGITUDES), 1.0, 6.0, ((1, 8), (2, 32)), jnp.float32),
        "salt_anomaly_value": centred(keys[1], (VERTICAL_LAYERS, MESH_LATITUDES, MESH_LONGITUDES), 1.0, 6.0, ((1, 8), (2, 32)), jnp.float32),
        "zonal_current_speed": centred(keys[2], (VERTICAL_LAYERS, MESH_LATITUDES, MESH_LONGITUDES), 0.45, 1.8, ((1, 8), (2, 32)), jnp.float32),
        "meridional_current_speed": centred(keys[3], (VERTICAL_LAYERS, MESH_LATITUDES, MESH_LONGITUDES), 0.45, 1.8, ((1, 8), (2, 32)), jnp.float32),
        "block_water_flag": place_ends((jax.random.randint(keys[4], (TILES_LAT, TILES_LON), 0, 4) < 3).astype(jnp.int32), jax.random.fold_in(keys[4], 1), 0, 1),
        "water_point_flag": place_ends((jax.random.randint(keys[5], (MESH_LATITUDES, MESH_LONGITUDES), 0, 5) < 4).astype(jnp.int32), jax.random.fold_in(keys[5], 1), 0, 1),
        "wet_layer_count": place_ends(jax.random.randint(keys[6], (MESH_LATITUDES, MESH_LONGITUDES), VERTICAL_LAYERS // 3, VERTICAL_LAYERS + 1), jax.random.fold_in(keys[6], 1), VERTICAL_LAYERS // 3, VERTICAL_LAYERS).astype(jnp.int32),
    }


time_step = 0.5
diffusivity = 0.1
strat_floor = 0.5
slope_limit = 2.0
thermal_coef = 0.2
haline_coef = 0.8

def trim_rim(grid_field, depth_cut):
    if depth_cut == 0:
        return grid_field
    return grid_field[:, depth_cut:grid_field.shape[1] - depth_cut, depth_cut:grid_field.shape[2] - depth_cut]

def positive_part(values):
    return jnp.maximum(values, 0.0)

def flux_div(flux_east, flux_north):
    return flux_east[:, 1:-1, 1:] - flux_east[:, 1:-1, :-1] + (flux_north[:, 1:, 1:-1] - flux_north[:, :-1, 1:-1])

def vert_div(flux_top):
    below = jnp.concatenate([flux_top[1:], jnp.zeros_like(flux_top[:1])], 0)
    return flux_top - below

def geometry(statics, layer_pile):
    u_cell = statics[:layer_pile]
    v_cell = statics[layer_pile:2 * layer_pile]
    floor_level = statics[2 * layer_pile]
    level_index = jnp.arange(layer_pile).astype(statics.dtype)[:, None, None]
    wet_mask = (level_index < floor_level[None]).astype(statics.dtype)
    u_face = 0.5 * (u_cell[:, :, :-1] + u_cell[:, :, 1:]) * wet_mask[:, :, :-1] * wet_mask[:, :, 1:]
    v_face = 0.5 * (v_cell[:, :-1, :] + v_cell[:, 1:, :]) * wet_mask[:, :-1, :] * wet_mask[:, 1:, :]
    divergence = flux_div(u_face, v_face)
    w_top = -jnp.cumsum(divergence[::-1], 0)[::-1]
    return (trim_rim(wet_mask, 1), u_face[:, 1:-1, :], v_face[:, :, 1:-1], w_top)

def extreme_near(values, wet_mask, chooser):
    center = trim_rim(values, 1)
    center_wet = trim_rim(wet_mask, 1)
    result = center
    near_list = ((values[:, 1:-1, 2:], wet_mask[:, 1:-1, 2:]), (values[:, 1:-1, :-2], wet_mask[:, 1:-1, :-2]), (values[:, 2:, 1:-1], wet_mask[:, 2:, 1:-1]), (values[:, :-2, 1:-1], wet_mask[:, :-2, 1:-1]))
    for near_vals, near_wet in near_list:
        result = chooser(result, jnp.where(near_wet > 0, near_vals, center))
    zero_row = jnp.zeros_like(center_wet[:1])
    above_vals = jnp.concatenate([center[:1], center[:-1]], 0)
    above_wet = jnp.concatenate([zero_row, center_wet[:-1]], 0)
    below_vals = jnp.concatenate([center[1:], center[-1:]], 0)
    below_wet = jnp.concatenate([center_wet[1:], zero_row], 0)
    result = chooser(result, jnp.where(above_wet > 0, above_vals, center))
    result = chooser(result, jnp.where(below_wet > 0, below_vals, center))
    return result

def limit_ratio(supply, headroom):
    return jnp.where(supply > headroom, headroom / jnp.where(supply > headroom, supply, 1.0), 1.0)

def advect(tracer, wet_mask, u_face, v_face, w_top):
    east_vel = u_face[:, :, 1:-1]
    north_vel = v_face[:, 1:-1, :]
    west_val = tracer[:, :, :-1]
    east_val = tracer[:, :, 1:]
    low_east = positive_part(east_vel) * west_val + jnp.minimum(east_vel, 0.0) * east_val
    anti_east = east_vel * 0.5 * (west_val + east_val) - low_east
    south_val = tracer[:, :-1, :]
    north_val = tracer[:, 1:, :]
    low_north = positive_part(north_vel) * south_val + jnp.minimum(north_vel, 0.0) * north_val
    anti_north = north_vel * 0.5 * (south_val + north_val) - low_north
    rise_vel = w_top[1:]
    upper_val = tracer[:-1]
    lower_val = tracer[1:]
    low_rise = positive_part(rise_vel) * lower_val + jnp.minimum(rise_vel, 0.0) * upper_val
    anti_rise = rise_vel * 0.5 * (upper_val + lower_val) - low_rise
    low_top = jnp.concatenate([w_top[:1] * tracer[:1], low_rise], 0)
    wet_one = trim_rim(wet_mask, 1)
    inner_val = trim_rim(tracer, 1)
    low_order = (inner_val - time_step * (flux_div(low_east, low_north) + trim_rim(vert_div(low_top), 1))) * wet_one
    upper_bound = extreme_near(jnp.maximum(inner_val, low_order), wet_one, jnp.maximum)
    lower_bound = extreme_near(jnp.minimum(inner_val, low_order), wet_one, jnp.minimum)
    face_east = anti_east[:, 1:-1, 1:]
    face_west = anti_east[:, 1:-1, :-1]
    face_north = anti_north[:, 1:, 1:-1]
    face_south = anti_north[:, :-1, 1:-1]
    face_top = trim_rim(jnp.concatenate([jnp.zeros_like(anti_rise[:1]), anti_rise], 0), 1)
    face_bottom = jnp.concatenate([face_top[1:], jnp.zeros_like(face_top[:1])], 0)
    gain_in = positive_part(face_west) + positive_part(-face_east) + positive_part(face_south) + positive_part(-face_north) + positive_part(face_bottom) + positive_part(-face_top)
    gain_out = positive_part(face_east) + positive_part(-face_west) + positive_part(face_north) + positive_part(-face_south) + positive_part(face_top) + positive_part(-face_bottom)
    low_two = trim_rim(low_order, 1)
    ratio_in = limit_ratio(trim_rim(gain_in, 1), (upper_bound - low_two) / time_step)
    ratio_out = limit_ratio(trim_rim(gain_out, 1), (low_two - lower_bound) / time_step)
    anti_x2 = anti_east[:, 2:-2, 2:-2]
    limit_east = jnp.where(anti_x2 >= 0, jnp.minimum(ratio_in[:, :, 1:], ratio_out[:, :, :-1]), jnp.minimum(ratio_in[:, :, :-1], ratio_out[:, :, 1:]))
    anti_y2 = anti_north[:, 2:-2, 2:-2]
    limit_north = jnp.where(anti_y2 >= 0, jnp.minimum(ratio_in[:, 1:, :], ratio_out[:, :-1, :]), jnp.minimum(ratio_in[:, :-1, :], ratio_out[:, 1:, :]))
    anti_z2 = trim_rim(anti_rise, 2)
    limit_rise = jnp.where(anti_z2 >= 0, jnp.minimum(ratio_in[:-1], ratio_out[1:]), jnp.minimum(ratio_in[1:], ratio_out[:-1]))
    limited_top = jnp.concatenate([jnp.zeros_like(anti_z2[:1]), limit_rise * anti_z2], 0)
    update = flux_div(limit_east * anti_x2, limit_north * anti_y2) + trim_rim(vert_div(limited_top), 1)
    return (trim_rim(low_order, 2) - time_step * update) * trim_rim(wet_mask, 3)

def vert_grad(grid_field, pair_wet, zero_row):
    return jnp.concatenate([zero_row, (grid_field[:-1] - grid_field[1:]) * pair_wet, zero_row], 0)

def pick_east(full_faces):
    top_faces = full_faces[:-1]
    bottom_faces = full_faces[1:]
    return [top_faces[:, :, :-1], bottom_faces[:, :, :-1], top_faces[:, :, 1:], bottom_faces[:, :, 1:]]

def pick_north(full_faces):
    top_faces = full_faces[:-1]
    bottom_faces = full_faces[1:]
    return [top_faces[:, :-1, :], bottom_faces[:, :-1, :], top_faces[:, 1:, :], bottom_faces[:, 1:, :]]

def stack_faces(part_vals, on_top):
    zero_row = jnp.zeros_like(part_vals[:1])
    if on_top:
        return jnp.concatenate([part_vals, zero_row], 0)
    return jnp.concatenate([zero_row, part_vals], 0)

def diffuse(scalar_quantities, wet_mask):
    temp_field, salt_field = scalar_quantities
    density = haline_coef * salt_field - thermal_coef * temp_field
    pair_east = wet_mask[:, :, :-1] * wet_mask[:, :, 1:]
    pair_north = wet_mask[:, :-1, :] * wet_mask[:, 1:, :]
    pair_rise = wet_mask[:-1] * wet_mask[1:]
    zero_row = jnp.zeros_like(wet_mask[:1])
    face_wet = jnp.concatenate([zero_row, pair_rise, zero_row], 0)
    rho_rise = vert_grad(density, pair_rise, zero_row)
    rho_east = (density[:, :, 1:] - density[:, :, :-1]) * pair_east
    rho_north = (density[:, 1:, :] - density[:, :-1, :]) * pair_north
    triads_east = []
    for rise_part, wet_part in zip(pick_east(rho_rise), pick_east(face_wet)):
        present = pair_east * wet_part
        slope_val = jnp.clip(rho_east / jnp.maximum(-rise_part, strat_floor), -slope_limit, slope_limit) * present
        triads_east.append((present, slope_val))
    triads_north = []
    for rise_part, wet_part in zip(pick_north(rho_rise), pick_north(face_wet)):
        present = pair_north * wet_part
        slope_val = jnp.clip(rho_north / jnp.maximum(-rise_part, strat_floor), -slope_limit, slope_limit) * present
        triads_north.append((present, slope_val))
    scale_flux = -diffusivity * 0.25
    results = []
    for tracer in scalar_quantities:
        grad_rise = vert_grad(tracer, pair_rise, zero_row)
        grad_east = (tracer[:, :, 1:] - tracer[:, :, :-1]) * pair_east
        grad_north = (tracer[:, 1:, :] - tracer[:, :-1, :]) * pair_north
        flux_east = jnp.zeros_like(grad_east)
        flux_north = jnp.zeros_like(grad_north)
        rise_total = jnp.zeros_like(trim_rim(face_wet, 1))
        for slot_index, ((present, slope_val), rise_part) in enumerate(zip(triads_east, pick_east(grad_rise))):
            flux_east = flux_east + present * (grad_east + slope_val * rise_part)
            rise_vals = present * (slope_val * grad_east + slope_val * slope_val * rise_part)
            cell_vals = rise_vals[:, 1:-1, 1:] if slot_index < 2 else rise_vals[:, 1:-1, :-1]
            rise_total = rise_total + stack_faces(cell_vals, slot_index % 2 == 0)
        for slot_index, ((present, slope_val), rise_part) in enumerate(zip(triads_north, pick_north(grad_rise))):
            flux_north = flux_north + present * (grad_north + slope_val * rise_part)
            rise_vals = present * (slope_val * grad_north + slope_val * slope_val * rise_part)
            cell_vals = rise_vals[:, 1:, 1:-1] if slot_index < 2 else rise_vals[:, :-1, 1:-1]
            rise_total = rise_total + stack_faces(cell_vals, slot_index % 2 == 0)
        rise_flux = scale_flux * rise_total
        update = flux_div(scale_flux * flux_east, scale_flux * flux_north) + (rise_flux[:-1] - rise_flux[1:])
        results.append((trim_rim(tracer, 1) - time_step * update) * trim_rim(wet_mask, 1))
    return results

def enlarge_whole_mesh(grid_field, width, sign_flip):
    wide_field = jnp.concatenate([grid_field[:, :, -width:], grid_field, grid_field[:, :, :width]], 2)
    north_rows = wide_field[:, -width:, :][:, ::-1, ::-1] * sign_flip
    south_rows = jnp.zeros_like(wide_field[:, :width, :])
    return jnp.concatenate([south_rows, wide_field, north_rows], 1)

def reference(potential_warmth, salt_anomaly_value, zonal_current_speed, meridional_current_speed, block_water_flag, water_point_flag, wet_layer_count):
    layer_pile = potential_warmth.shape[0]
    tile_cells = jnp.repeat(jnp.repeat(block_water_flag, CJ, 0), CI, 1)
    floor_level = (wet_layer_count * water_point_flag * tile_cells).astype(jnp.float32)
    statics = jnp.concatenate([zonal_current_speed, meridional_current_speed, floor_level[None]], 0)
    sign_flip = jnp.concatenate([-jnp.ones((2 * layer_pile, 1, 1), jnp.float32), jnp.ones((1, 1, 1), jnp.float32)], 0)
    stat_pad = enlarge_whole_mesh(statics, 4, sign_flip)
    haloed_scalar = enlarge_whole_mesh(jnp.concatenate([potential_warmth, salt_anomaly_value], 0), 3, 1.0)
    first_pass = []
    wet_bands = []
    for band_index in range(N_LAT):
        row_start = band_index * CJ
        wet_mask, u_face, v_face, w_top = geometry(stat_pad[:, row_start:row_start + CJ + 8], layer_pile)
        tile_rows = haloed_scalar[:, row_start:row_start + CJ + 6]
        first_pass.append(jnp.concatenate([advect(tile_rows[:layer_pile], wet_mask, u_face, v_face, w_top), advect(tile_rows[layer_pile:], wet_mask, u_face, v_face, w_top)], 0))
        wet_bands.append(trim_rim(wet_mask, 2))
    advected = jnp.concatenate(first_pass, 1)
    refilled = enlarge_whole_mesh(advected, 1, 1.0)
    temp_bands = []
    salt_bands = []
    for band_index in range(N_LAT):
        row_start = band_index * CJ
        tile_rows = refilled[:, row_start:row_start + CJ + 2]
        new_temp, new_salt = diffuse([tile_rows[:layer_pile], tile_rows[layer_pile:]], wet_bands[band_index])
        temp_bands.append(new_temp)
        salt_bands.append(new_salt)
    return (jnp.concatenate(temp_bands, 1), jnp.concatenate(salt_bands, 1))
```

```python
import functools

import jax
import jax.numpy as jnp
from jax import lax
from jax.experimental import pallas as pl
from jax.experimental.pallas import tpu as pltpu
from jax.sharding import PartitionSpec as P

time_step = 0.5
diffusivity = 0.1
strat_floor = 0.5
slope_limit = 2.0
thermal_coef = 0.2
haline_coef = 0.8

MESH = pl.DeviceIdType.MESH
INF = float("inf")
TINY = 1e-37
FACE_SCALE = 0.25 * time_step
DIFF_SCALE = 0.25 * time_step * diffusivity

EAST, WEST, NORTH, SOUTH, NE, NW, SE, SW = range(8)


def east_of(x):
    return pltpu.roll(x, x.shape[1] - 1, 1)


def west_of(x):
    return pltpu.roll(x, 1, 1)


def south_of(x):
    return pltpu.roll(x, 1, 0)


def stage_flux(z, wins):
    nk = z["u"].shape[0]
    stat = []
    for r0, n, _, _ in wins:
        f = z["f"][r0 : r0 + n, :]
        f_e = jnp.minimum(f, east_of(f))
        f_n = jnp.minimum(f, z["f"][r0 + 1 : r0 + 1 + n, :])
        stat.append((f, f_e, f_n))

    def body(i, carry):
        k = nk - 1 - i
        kk = k.astype(jnp.float32)
        up_k = jnp.maximum(k - 1, 0)
        out = []
        for (r0, n, lo, hi), (f, f_e, f_n), (w_old, bottoms) in zip(wins, stat, carry):
            u = z["u"][k, r0 : r0 + n, :]
            u_e = jnp.where(kk < f_e, FACE_SCALE * (u + east_of(u)), 0.0)
            v = z["v"][k, r0 : r0 + n, :]
            v_n = jnp.where(kk < f_n, FACE_SCALE * (v + z["v"][k, r0 + 1 : r0 + 1 + n, :]), 0.0)
            w = w_old - (u_e - west_of(u_e) + v_n - south_of(v_n))
            abs_u, abs_v, abs_w = jnp.abs(u_e), jnp.abs(v_n), jnp.abs(w)
            wet = kk < f
            tops = []
            for m, t in enumerate(z["t"]):
                c = t[k, r0 : r0 + n, :]
                e = east_of(c)
                nn = t[k, r0 + 1 : r0 + 1 + n, :]
                up = t[up_k, r0 : r0 + n, :]
                a_e = abs_u * (e - c)
                l_e = u_e * (c + e) - a_e
                a_n = abs_v * (nn - c)
                l_n = v_n * (c + nn) - a_n
                a_t = abs_w * (up - c)
                l_t = w * (c + up) - a_t
                low = c - ((l_e - west_of(l_e)) + (l_n - south_of(l_n)) + (l_t - bottoms[m]))
                low = jnp.where(wet, low, 0.0)
                big = jnp.where(wet, jnp.maximum(c, low), -INF)
                small = jnp.where(wet, jnp.minimum(c, low), INF)
                for name, val in (("ax", a_e), ("ay", a_n), ("az", a_t), ("low", low), ("mx", big), ("mn", small)):
                    z[name][m][k, r0 + lo : r0 + hi, :] = val[lo:hi]
                tops.append(l_t)
            out.append((w, tuple(tops)))
        return tuple(out)

    zero = [jnp.zeros((n, 128), jnp.float32) for _, n, _, _ in wins]
    lax.fori_loop(0, nk, body, tuple((x, tuple(x for _ in z["t"])) for x in zero))


def stage_ratio(z, wins):
    nk = z["u"].shape[0]

    def body(i, carry):
        k = nk - 1 - i
        up_k, down_k = jnp.maximum(k - 1, 0), jnp.minimum(k + 1, nk - 1)
        out = []
        for (r0, n, lo, hi), bottoms in zip(wins, carry):
            tops = []
            for m in range(len(z["t"])):
                def near(ref, pick):
                    c = ref[k, r0 : r0 + n, :]
                    horizontal = pick(pick(east_of(c), west_of(c)), pick(ref[k, r0 + 1 : r0 + 1 + n, :], ref[k, r0 - 1 : r0 - 1 + n, :]))
                    return pick(pick(c, horizontal), pick(ref[up_k, r0 : r0 + n, :], ref[down_k, r0 : r0 + n, :]))

                big, small = near(z["mx"][m], jnp.maximum), near(z["mn"][m], jnp.minimum)
                low = z["low"][m][k, r0 : r0 + n, :]
                a_e = z["ax"][m][k, r0 : r0 + n, :]
                a_w = west_of(a_e)
                a_n = z["ay"][m][k, r0 : r0 + n, :]
                a_s = z["ay"][m][k, r0 - 1 : r0 - 1 + n, :]
                a_t, a_b = z["az"][m][k, r0 : r0 + n, :], bottoms[m]
                p_in, p_out = 0.0, 0.0
                for inward, outward in ((a_w, a_e), (a_s, a_n), (a_b, a_t)):
                    p_in = p_in + (jnp.maximum(inward, 0.0) - jnp.minimum(outward, 0.0))
                    p_out = p_out + (jnp.maximum(outward, 0.0) - jnp.minimum(inward, 0.0))
                r_in = jnp.clip((big - low) * pl.reciprocal(jnp.maximum(p_in, TINY)), 0.0, 1.0)
                r_out = jnp.clip((low - small) * pl.reciprocal(jnp.maximum(p_out, TINY)), 0.0, 1.0)
                z["rin"][m][k, r0 + lo : r0 + hi, :] = r_in[lo:hi]
                z["rout"][m][k, r0 + lo : r0 + hi, :] = r_out[lo:hi]
                tops.append(a_t)
            out.append(tuple(tops))
        return tuple(out)

    lax.fori_loop(0, nk, body, tuple(tuple(jnp.zeros((n, 128), jnp.float32) for _ in z["t"]) for _, n, _, _ in wins))


def stage_limit(z, wins):
    nk = z["u"].shape[0]
    stat = [z["f"][r0 : r0 + n, :] for r0, n, _, _ in wins]

    def body(i, carry):
        k = nk - 1 - i
        kk = k.astype(jnp.float32)
        up_k = jnp.maximum(k - 1, 0)
        out = []
        for (r0, n, lo, hi), f, bottoms in zip(wins, stat, carry):
            tops = []
            for m in range(len(z["t"])):
                r_in, r_out = z["rin"][m][k, r0 : r0 + n, :], z["rout"][m][k, r0 : r0 + n, :]

                def limited(anti, far_in, far_out):
                    return anti * jnp.where(anti >= 0, jnp.minimum(far_in, r_out), jnp.minimum(r_in, far_out))

                f_e = limited(z["ax"][m][k, r0 : r0 + n, :], east_of(r_in), east_of(r_out))
                f_n = limited(
                    z["ay"][m][k, r0 : r0 + n, :],
                    z["rin"][m][k, r0 + 1 : r0 + 1 + n, :],
                    z["rout"][m][k, r0 + 1 : r0 + 1 + n, :],
                )
                f_t = limited(
                    z["az"][m][k, r0 : r0 + n, :],
                    z["rin"][m][up_k, r0 : r0 + n, :],
                    z["rout"][m][up_k, r0 : r0 + n, :],
                )
                low = z["low"][m][k, r0 : r0 + n, :]
                new = low - ((f_e - west_of(f_e)) + (f_n - south_of(f_n)) + (f_t - bottoms[m]))
                new = jnp.where(kk < f, new, 0.0)
                z["adv"][m][k, r0 + lo : r0 + hi, :] = new[lo:hi]
                tops.append(f_t)
            out.append(tuple(tops))
        return tuple(out)

    lax.fori_loop(0, nk, body, tuple(tuple(jnp.zeros((n, 128), jnp.float32) for _ in z["t"]) for _, n, _, _ in wins))


def clip_slope(x):
    return jnp.clip(x, -slope_limit, slope_limit)


def stage_diffuse(z, wins, emit):
    nk = z["u"].shape[0]
    dens = z["density"]
    nt = len(z["t"])
    stat = []
    for r0, n, _, _ in wins:
        f = z["f"][r0 : r0 + n, :]
        far_e, far_n = east_of(f), z["f"][r0 + 1 : r0 + 1 + n, :]
        stat.append((f, far_e, far_n, jnp.minimum(f, far_e), jnp.minimum(f, far_n)))

    def inverse(grads):
        return pl.reciprocal(jnp.maximum(-dens(grads), strat_floor))

    def body(i, carry):
        k = nk - 1 - i
        kk = k.astype(jnp.float32)
        up_k = jnp.maximum(k - 1, 0)
        below_k = jnp.minimum(k + 1, nk - 1)
        not_top = (k >= 1).astype(jnp.float32)
        out = []
        for wi, ((r0, n, _, _), (f, far_e, far_n, f_e, f_n), old) in enumerate(zip(wins, stat, carry)):
            here = [a[k, r0 : r0 + n, :] for a in z["adv"]]
            north = [a[k, r0 + 1 : r0 + 1 + n, :] for a in z["adv"]]
            gz = [jnp.where(kk < f, a[up_k, r0 : r0 + n, :] - c, 0.0) for a, c in zip(z["adv"], here)]
            gz_n = [jnp.where(kk < far_n, a[up_k, r0 + 1 : r0 + 1 + n, :] - c, 0.0) for a, c in zip(z["adv"], north)]
            gz_e = [east_of(g) for g in gz]
            inv, inv_n = inverse(gz), inverse(gz_n)
            inv_e = east_of(inv)
            gx = [jnp.where(kk < f_e, east_of(c) - c, 0.0) for c in here]
            gy = [jnp.where(kk < f_n, b - c, 0.0) for b, c in zip(north, here)]
            rx, ry = dens(gx), dens(gy)
            (o_inv, o_inv_e, o_inv_n, o_gz, o_gz_e, o_gz_n, o_part, o_top) = old
            low_here, low_e, low_n = kk + 1.0 < f, kk + 1.0 < far_e, kk + 1.0 < far_n
            s_x = [clip_slope(rx * q) for q in (inv, inv_e, o_inv, o_inv_e)]
            s_y = [clip_slope(ry * q) for q in (inv, inv_n, o_inv, o_inv_n)]
            parts, tops = [], []
            for m in range(nt):
                gx_top, gy_top = gx[m] * not_top, gy[m] * not_top
                hx = (
                    gx_top + s_x[0] * gz[m],
                    gx_top + s_x[1] * gz_e[m],
                    jnp.where(low_here, gx[m], 0.0) + s_x[2] * o_gz[m],
                    jnp.where(low_e, gx[m], 0.0) + s_x[3] * o_gz_e[m],
                )
                hy = (
                    gy_top + s_y[0] * gz[m],
                    gy_top + s_y[1] * gz_n[m],
                    jnp.where(low_here, gy[m], 0.0) + s_y[2] * o_gz[m],
                    jnp.where(low_n, gy[m], 0.0) + s_y[3] * o_gz_n[m],
                )
                flux_e = (hx[0] + hx[1]) + (hx[2] + hx[3])
                flux_n = (hy[0] + hy[1]) + (hy[2] + hy[3])
                top = (s_x[0] * hx[0] + west_of(s_x[1] * hx[1])) + (s_y[0] * hy[0] + south_of(s_y[1] * hy[1]))
                bottom = (s_x[2] * hx[2] + west_of(s_x[3] * hx[3])) + (s_y[2] * hy[2] + south_of(s_y[3] * hy[3]))
                rise = o_top[m] + bottom
                done = jnp.where(kk + 1.0 < f, o_part[m] + DIFF_SCALE * rise, 0.0)
                emit(below_k, wi, m, done)
                parts.append(here[m] + DIFF_SCALE * ((flux_e - west_of(flux_e)) + (flux_n - south_of(flux_n)) - rise))
                tops.append(top)
            out.append((inv, inv_e, inv_n, tuple(gz), tuple(gz_e), tuple(gz_n), tuple(parts), tuple(tops)))
        return tuple(out)

    start = []
    for _, n, _, _ in wins:
        x = jnp.zeros((n, 128), jnp.float32)
        xs = tuple(x for _ in range(nt))
        start.append((x, x, x, xs, xs, xs, xs, xs))
    last = lax.fori_loop(0, nk, body, tuple(start))
    for wi, ((f, *_), old) in enumerate(zip(stat, last)):
        for m in range(nt):
            emit(0, wi, m, jnp.where(0.0 < f, old[6][m] + DIFF_SCALE * old[7][m], 0.0))


def lane_iota(rows):
    return lax.broadcasted_iota(jnp.int32, (rows, 128), 1)


def kernel(
    t_hbm, s_hbm, u_hbm, v_hbm, flag_ref, point_ref, count_ref,
    t_out, s_out,
    tr, u, v, floor, low, mx, mn, ax, ay, az, rin, rout, adv,
    e_tr, e_u, e_v, e_floor, e_low, e_mx, e_mn, e_ax, e_ay, e_az, e_rin, e_rout, e_adv, e_res,
    row_out, row_in, strip_out, fold_out, strip_in, corner_in,
    load_sem, send_sem, recv_sem,
):
    n_lon, n_lat = lax.axis_size("lon"), lax.axis_size("lat")
    lon, lat = lax.axis_index("lon"), lax.axis_index("lat")
    nk = u.shape[0]
    half = nk // 2
    east, west = lax.rem(lon + 1, n_lon), lax.rem(lon + n_lon - 1, n_lon)
    at_north, at_south = lat == n_lat - 1, lat == 0
    fold_mid = n_lon - 1 - lon
    fold_ne = lax.rem(2 * n_lon - 2 - lon, n_lon)
    fold_nw = lax.rem(n_lon - lon, n_lon)

    side = [(EAST, (east, lat)), (WEST, (west, lat))]
    north = [(NORTH, (lon, lat + 1)), (NE, (east, lat + 1)), (NW, (west, lat + 1))]
    south = [(SOUTH, (lon, lat - 1)), (SE, (east, lat - 1)), (SW, (west, lat - 1))]
    folded = [(NORTH, (fold_mid, lat)), (NE, (fold_ne, lat)), (NW, (fold_nw, lat))]
    ne_self, nw_self = fold_ne == lon, fold_nw == lon
    not_self = {NORTH: True, NE: jnp.logical_not(ne_self), NW: jnp.logical_not(nw_self)}

    barrier = pltpu.get_barrier_semaphore()

    def greet(where):
        pl.semaphore_signal(barrier, inc=1, device_id=where, device_id_type=MESH)

    for _, where in side:
        greet(where)

    @pl.when(jnp.logical_not(at_south))
    def _():
        for _, where in south:
            greet(where)

    @pl.when(jnp.logical_not(at_north))
    def _():
        for _, where in north:
            greet(where)

    @pl.when(at_north)
    def _():
        greet(folded[0][1])

        @pl.when(jnp.logical_not(ne_self))
        def _():
            greet(folded[1][1])

        @pl.when(jnp.logical_not(nw_self))
        def _():
            greet(folded[2][1])

    loads = [
        pltpu.make_async_copy(src, dst.at[:, 8:24, :], load_sem.at[i])
        for i, (src, dst) in enumerate(((t_hbm, tr.at[0]), (s_hbm, tr.at[1]), (u_hbm, u), (v_hbm, v)))
    ]
    for copy in loads:
        copy.start()
    floor[8:24, :] = (count_ref[...] * point_ref[...] * flag_ref[...]).astype(jnp.float32)
    for copy in loads:
        copy.wait()

    fields = ((tr.at[0], tr.at[1]), (u, v))
    for g, (a, b) in enumerate(fields):
        for k in range(nk):
            row_out[1, g * nk + k, 0:4, :] = a[k, 8:12, :]
            row_out[1, g * nk + k, 4:8, :] = b[k, 8:12, :]
    row_out[1, 2 * nk, 0:4, :] = floor[8:12, :]

    @pl.when(jnp.logical_not(at_north))
    def _():
        for g, (a, b) in enumerate(fields):
            for k in range(nk):
                row_out[0, g * nk + k, 0:4, :] = a[k, 20:24, :]
                row_out[0, g * nk + k, 4:8, :] = b[k, 20:24, :]
        row_out[0, 2 * nk, 0:4, :] = floor[20:24, :]

    lane8, sub8 = lane_iota(8), lax.broadcasted_iota(jnp.int32, (8, 128), 0)

    @pl.when(at_north)
    def _():
        def turned(x):
            x = jnp.take_along_axis(x, 127 - lane8, axis=1)
            return jnp.take_along_axis(x, 7 - sub8, axis=0)

        for g, (a, b) in enumerate(fields):
            sign = 1.0 if g == 0 else -1.0
            for k in range(nk):
                row_out[0, g * nk + k, 0:4, :] = sign * turned(a[k, 16:24, :])[0:4]
                row_out[0, g * nk + k, 4:8, :] = sign * turned(b[k, 16:24, :])[0:4]
        row_out[0, 2 * nk, 0:4, :] = turned(floor[16:24, :])[0:4]

    p = lax.rem(lane8, 64)
    shift = jnp.where(p < 12, 116, jnp.where(p < 16, -12, jnp.where(p < 20, 108, -20)))
    strip_idx = lax.rem(p + shift + 128, 128)
    first = lane8 < 64

    def strip_tile(row):
        def gather(x):
            return jnp.take_along_axis(x, strip_idx, axis=1)

        rows = slice(row, row + 8)
        for k in range(nk):
            e_tr[k, rows, :] = jnp.where(first, gather(tr[0, k, rows, :]), gather(tr[1, k, rows, :]))
            e_u[k, rows, :] = gather(u[k, rows, :])
            e_v[k, rows, :] = gather(v[k, rows, :])
        e_floor[rows, :] = gather(floor[rows, :])

    q = lax.rem(lane8, 32)
    q_t = jnp.logical_and(q >= 12, q < 20)
    q_u = jnp.logical_and(q >= 20, q < 28)
    p32 = lax.rem(lane8 + 124, 64) < 32
    for row in (8, 16):
        strip_tile(row)
        rows = slice(row, row + 8)
        for k in range(half):
            def packed(level):
                return jnp.where(
                    q_t, e_tr[level, rows, :],
                    jnp.where(q_u, pltpu.roll(e_u[level, rows, :], 8, 1), pltpu.roll(e_v[level, rows, :], 16, 1)),
                )

            strip_out[k, row - 8 : row, :] = jnp.where(p32, packed(k), pltpu.roll(packed(k + half), 32, 1))
        strip_out[half, row - 8 : row, :] = e_floor[rows, :]

    @pl.when(at_north)
    def _():
        group_idx = lax.rem(lane8 + 7 - 2 * lax.rem(lane8 + 4, 8) + 128, 128)
        sign = jnp.where(q_t, 1.0, -1.0)
        for k in range(half + 1):
            x = jnp.take_along_axis(strip_out[k, 8:16, :], group_idx, axis=1)
            x = jnp.take_along_axis(x, 7 - sub8, axis=0)
            fold_out[k] = x if k == half else x * sign

    n_north = jnp.where(at_north, 3 - ne_self.astype(jnp.int32) - nw_self.astype(jnp.int32), 3)
    pl.semaphore_wait(barrier, 2 + n_north + jnp.where(at_south, 0, 3))

    def send(src, dst, role, slot, where):
        return pltpu.make_async_remote_copy(
            src_ref=src, dst_ref=dst, send_sem=send_sem.at[role], recv_sem=recv_sem.at[slot],
            device_id=where, device_id_type=MESH,
        )

    corner = {NE: 0, NW: 1, SE: 2, SW: 3}

    def to_rows(role, slot, where):
        return send(row_out.at[0 if role == NORTH else 1], row_in.at[0 if slot == NORTH else 1], role, slot, where)

    def to_corner(role, slot, where, fold=False):
        src = fold_out if fold else strip_out.at[:, 8:16, :] if role in (NE, NW) else strip_out.at[:, 0:8, :]
        return send(src, corner_in.at[corner[slot]], role, slot, where)

    side_sends = [
        send(strip_out, strip_in.at[0], WEST, EAST, (west, lat)),
        send(strip_out, strip_in.at[1], EAST, WEST, (east, lat)),
    ]
    north_sends = [
        to_rows(NORTH, SOUTH, north[0][1]),
        to_corner(NE, SW, north[1][1]),
        to_corner(NW, SE, north[2][1]),
    ]
    south_sends = [
        to_rows(SOUTH, NORTH, south[0][1]),
        to_corner(SE, NW, south[1][1]),
        to_corner(SW, NE, south[2][1]),
    ]
    fold_sends = [
        to_rows(NORTH, NORTH, folded[0][1]),
        to_corner(NE, NE, folded[1][1], True),
        to_corner(NW, NW, folded[2][1], True),
    ]
    ne_local = pltpu.make_async_copy(fold_out, corner_in.at[corner[NE]], send_sem.at[NE])
    nw_local = pltpu.make_async_copy(fold_out, corner_in.at[corner[NW]], send_sem.at[NW])

    @pl.when(jnp.logical_not(at_south))
    def _():
        for copy in south_sends:
            copy.start()

    @pl.when(jnp.logical_not(at_north))
    def _():
        for copy in north_sends:
            copy.start()

    @pl.when(at_north)
    def _():
        fold_sends[0].start()
        for copy, local, own in ((fold_sends[1], ne_local, ne_self), (fold_sends[2], nw_local, nw_self)):
            @pl.when(own)
            def _():
                local.start()

            @pl.when(jnp.logical_not(own))
            def _():
                copy.start()

    for copy in side_sends:
        copy.start()

    main = dict(
        t=[tr.at[0], tr.at[1]], u=u, v=v, f=floor,
        density=lambda pair: haline_coef * pair[1] - thermal_coef * pair[0],
    )
    names = dict(low=low, mx=mx, mn=mn, ax=ax, ay=ay, az=az, rin=rin, rout=rout, adv=adv)
    main.update({name: [ref.at[0], ref.at[1]] for name, ref in names.items()})

    outs = (t_out, s_out)

    stage_flux(main, [(8, 16, 0, 16)])
    stage_ratio(main, [(8, 16, 0, 16)])
    stage_limit(main, [(8, 16, 0, 16)])

    def emit_inner(k, wi, m, val):
        outs[m][k, 4:12, :] = val[4:12]

    stage_diffuse(main, [(8, 16, 4, 12)], emit_inner)

    @pl.when(at_south)
    def _():
        row_in[1] = jnp.zeros(row_in.shape[1:], jnp.float32)
        corner_in[corner[SE]] = jnp.zeros(corner_in.shape[1:], jnp.float32)
        corner_in[corner[SW]] = jnp.zeros(corner_in.shape[1:], jnp.float32)

    @pl.when(jnp.logical_not(at_south))
    def _():
        for copy in north_sends:
            copy.wait_recv()
        for copy in south_sends:
            copy.wait_send()

    @pl.when(jnp.logical_not(at_north))
    def _():
        for copy in south_sends:
            copy.wait_recv()
        for copy in north_sends:
            copy.wait_send()

    @pl.when(at_north)
    def _():
        fold_sends[0].wait()
        for copy, local, own in ((fold_sends[1], ne_local, ne_self), (fold_sends[2], nw_local, nw_self)):
            @pl.when(own)
            def _():
                local.wait()

            @pl.when(jnp.logical_not(own))
            def _():
                copy.wait()

    for copy in side_sends:
        copy.wait()

    for slot, row in ((1, 4), (0, 24)):
        for g, (a, b) in enumerate(fields):
            for k in range(nk):
                a[k, row : row + 4, :] = row_in[slot, g * nk + k, 0:4, :]
                b[k, row : row + 4, :] = row_in[slot, g * nk + k, 4:8, :]
        floor[row : row + 4, :] = row_in[slot, 2 * nk, 0:4, :]

    strip_tile(0)
    strip_tile(24)
    halo = jnp.logical_and(p >= 12, p < 20)
    from_east = lax.rem(lane8, 8) >= 4
    for row, east_ref, west_ref, at in (
        (0, corner_in.at[corner[SE]], corner_in.at[corner[SW]], 0),
        (8, strip_in.at[0], strip_in.at[1], 0),
        (16, strip_in.at[0], strip_in.at[1], 8),
        (24, corner_in.at[corner[NE]], corner_in.at[corner[NW]], 0),
    ):
        rows = slice(row, row + 8)
        for k in range(half + 1):
            x = jnp.where(from_east, east_ref[k, at : at + 8, :], west_ref[k, at : at + 8, :])
            if k == half:
                e_floor[rows, :] = jnp.where(halo, x, e_floor[rows, :])
                continue
            for level, y in ((k, x), (k + half, pltpu.roll(x, 96, 1))):
                e_tr[level, rows, :] = jnp.where(halo, y, e_tr[level, rows, :])
                e_u[level, rows, :] = jnp.where(halo, pltpu.roll(y, 120, 1), e_u[level, rows, :])
                e_v[level, rows, :] = jnp.where(halo, pltpu.roll(y, 112, 1), e_v[level, rows, :])

    stage_flux(main, [(4, 8, 1, 5), (20, 8, 3, 7)])
    stage_ratio(main, [(4, 8, 2, 6), (20, 8, 2, 6)])
    stage_limit(main, [(4, 8, 3, 7), (20, 8, 1, 5)])

    def emit_outer(k, wi, m, val):
        if wi == 0:
            outs[m][k, 0:4, :] = val[4:8]
        else:
            outs[m][k, 12:16, :] = val[4:8]

    stage_diffuse(main, [(4, 8, 4, 8), (16, 8, 4, 8)], emit_outer)

    def strip_density(one):
        x = one[0]
        low_half = lane_iota(x.shape[0]) < 64
        own = jnp.where(low_half, -thermal_coef, haline_coef)
        other = jnp.where(low_half, haline_coef, -thermal_coef)
        return own * x + other * pltpu.roll(x, 64, 1)

    strips = dict(t=[e_tr], u=e_u, v=e_v, f=e_floor, density=strip_density)
    names = dict(low=e_low, mx=e_mx, mn=e_mn, ax=e_ax, ay=e_ay, az=e_az, rin=e_rin, rout=e_rout, adv=e_adv)
    strips.update({name: [ref] for name, ref in names.items()})
    stage_flux(strips, [(4, 24, 0, 24)])
    stage_ratio(strips, [(4, 24, 0, 24)])
    stage_limit(strips, [(4, 24, 0, 24)])

    def emit_strip(k, wi, m, val):
        e_res[k] = val[4:20]

    stage_diffuse(strips, [(4, 24, 4, 20)], emit_strip)

    lane16 = lane_iota(16)
    rim = jnp.logical_or(lane16 < 4, lane16 >= 124)
    for m in range(2):
        back = jnp.where(lane16 < 4, lane16 + 20, jnp.where(lane16 >= 124, lane16 - 116, 0)) + 64 * m
        for k in range(nk):
            outs[m][k] = jnp.where(rim, jnp.take_along_axis(e_res[k], back, axis=1), outs[m][k])


def on_device(t, s, u, v, flag, point, count):
    nk = t.shape[0]
    f32 = jnp.float32
    vm = lambda *shape: pltpu.VMEM(shape, f32)
    big = lambda: vm(2, nk, 32, 128)
    one = lambda: vm(nk, 32, 128)
    whole = pl.BlockSpec(memory_space=pltpu.VMEM)
    hbm = pl.BlockSpec(memory_space=pl.ANY)
    return pl.pallas_call(
        kernel,
        out_shape=(jax.ShapeDtypeStruct(t.shape, f32), jax.ShapeDtypeStruct(s.shape, f32)),
        in_specs=[hbm] * 4 + [whole] * 3,
        out_specs=(whole, whole),
        scratch_shapes=[
            big(), one(), one(), vm(32, 128),
            *[big() for _ in range(9)],
            one(), one(), one(), vm(32, 128),
            *[one() for _ in range(9)],
            vm(nk, 16, 128),
            vm(2, 2 * nk + 1, 8, 128), vm(2, 2 * nk + 1, 8, 128),
            vm(nk // 2 + 1, 16, 128), vm(nk // 2 + 1, 8, 128),
            vm(2, nk // 2 + 1, 16, 128), vm(4, nk // 2 + 1, 8, 128),
            pltpu.SemaphoreType.DMA((4,)), pltpu.SemaphoreType.DMA((8,)), pltpu.SemaphoreType.DMA((8,)),
        ],
        compiler_params=pltpu.CompilerParams(
            collective_id=0, has_side_effects=True, vmem_limit_bytes=32 * 1024 * 1024
        ),
    )(t, s, u, v, flag, point, count)


def solution(mesh):
    grid = P(None, "lat", "lon")
    flat = P("lat", "lon")
    return jax.shard_map(
        on_device, mesh=mesh, in_specs=(grid,) * 4 + (flat,) * 3, out_specs=(grid, grid), check_vma=False
    )
```

```python
import functools

import jax
import jax.numpy as jnp
from jax import lax
from jax.experimental import pallas as pl
from jax.experimental.pallas import tpu as pltpu
from jax.sharding import PartitionSpec as P

time_step = 0.5
diffusivity = 0.1
strat_floor = 0.5
slope_limit = 2.0
thermal_coef = 0.2
haline_coef = 0.8

MESH = pl.DeviceIdType.MESH
INF = float("inf")
TINY = 1e-37
FACE_SCALE = 0.25 * time_step
DIFF_SCALE = 0.25 * time_step * diffusivity

EAST, WEST, NORTH, SOUTH, NE, NW, SE, SW = range(8)


def east_of(x):
    return pltpu.roll(x, x.shape[1] - 1, 1)


def west_of(x):
    return pltpu.roll(x, 1, 1)


def south_of(x):
    return pltpu.roll(x, 1, 0)


def stage_flux(z, wins):
    nk = z["u"].shape[0]
    stat = []
    for r0, n, _, _ in wins:
        f = z["f"][r0 : r0 + n, :]
        f_e = jnp.minimum(f, east_of(f))
        f_n = jnp.minimum(f, z["f"][r0 + 1 : r0 + 1 + n, :])
        stat.append((f, f_e, f_n))

    def body(i, carry):
        k = nk - 1 - i
        kk = k.astype(jnp.float32)
        up_k = jnp.maximum(k - 1, 0)
        out = []
        for (r0, n, lo, hi), (f, f_e, f_n), (w_old, bottoms) in zip(wins, stat, carry):
            u = z["u"][k, r0 : r0 + n, :]
            u_e = jnp.where(kk < f_e, FACE_SCALE * (u + east_of(u)), 0.0)
            v = z["v"][k, r0 : r0 + n, :]
            v_n = jnp.where(kk < f_n, FACE_SCALE * (v + z["v"][k, r0 + 1 : r0 + 1 + n, :]), 0.0)
            w = w_old - (u_e - west_of(u_e) + v_n - south_of(v_n))
            abs_u, abs_v, abs_w = jnp.abs(u_e), jnp.abs(v_n), jnp.abs(w)
            wet = kk < f
            tops = []
            for m, t in enumerate(z["t"]):
                c = t[k, r0 : r0 + n, :]
                e = east_of(c)
                nn = t[k, r0 + 1 : r0 + 1 + n, :]
                up = t[up_k, r0 : r0 + n, :]
                a_e = abs_u * (e - c)
                l_e = u_e * (c + e) - a_e
                a_n = abs_v * (nn - c)
                l_n = v_n * (c + nn) - a_n
                a_t = abs_w * (up - c)
                l_t = w * (c + up) - a_t
                low = c - ((l_e - west_of(l_e)) + (l_n - south_of(l_n)) + (l_t - bottoms[m]))
                low = jnp.where(wet, low, 0.0)
                big = jnp.where(wet, jnp.maximum(c, low), -INF)
                small = jnp.where(wet, jnp.minimum(c, low), INF)
                for name, val in (("ax", a_e), ("ay", a_n), ("az", a_t), ("low", low), ("mx", big), ("mn", small)):
                    z[name][m][k, r0 + lo : r0 + hi, :] = val[lo:hi]
                tops.append(l_t)
            out.append((w, tuple(tops)))
        return tuple(out)

    zero = [jnp.zeros((n, 128), jnp.float32) for _, n, _, _ in wins]
    lax.fori_loop(0, nk, body, tuple((x, tuple(x for _ in z["t"])) for x in zero), unroll=nk)


def stage_ratio(z, wins):
    nk = z["u"].shape[0]

    def body(i, carry):
        k = nk - 1 - i
        up_k, down_k = jnp.maximum(k - 1, 0), jnp.minimum(k + 1, nk - 1)
        out = []
        for (r0, n, lo, hi), bottoms in zip(wins, carry):
            tops = []
            for m in range(len(z["t"])):
                def near(ref, pick):
                    c = ref[k, r0 : r0 + n, :]
                    horizontal = pick(pick(east_of(c), west_of(c)), pick(ref[k, r0 + 1 : r0 + 1 + n, :], ref[k, r0 - 1 : r0 - 1 + n, :]))
                    return pick(pick(c, horizontal), pick(ref[up_k, r0 : r0 + n, :], ref[down_k, r0 : r0 + n, :]))

                big, small = near(z["mx"][m], jnp.maximum), near(z["mn"][m], jnp.minimum)
                low = z["low"][m][k, r0 : r0 + n, :]
                a_e = z["ax"][m][k, r0 : r0 + n, :]
                a_w = west_of(a_e)
                a_n = z["ay"][m][k, r0 : r0 + n, :]
                a_s = z["ay"][m][k, r0 - 1 : r0 - 1 + n, :]
                a_t, a_b = z["az"][m][k, r0 : r0 + n, :], bottoms[m]
                p_in, p_out = 0.0, 0.0
                for inward, outward in ((a_w, a_e), (a_s, a_n), (a_b, a_t)):
                    p_in = p_in + (jnp.maximum(inward, 0.0) - jnp.minimum(outward, 0.0))
                    p_out = p_out + (jnp.maximum(outward, 0.0) - jnp.minimum(inward, 0.0))
                r_in = jnp.clip((big - low) * pl.reciprocal(jnp.maximum(p_in, TINY)), 0.0, 1.0)
                r_out = jnp.clip((low - small) * pl.reciprocal(jnp.maximum(p_out, TINY)), 0.0, 1.0)
                z["rin"][m][k, r0 + lo : r0 + hi, :] = r_in[lo:hi]
                z["rout"][m][k, r0 + lo : r0 + hi, :] = r_out[lo:hi]
                tops.append(a_t)
            out.append(tuple(tops))
        return tuple(out)

    lax.fori_loop(0, nk, body, tuple(tuple(jnp.zeros((n, 128), jnp.float32) for _ in z["t"]) for _, n, _, _ in wins), unroll=nk)


def stage_limit(z, wins):
    nk = z["u"].shape[0]
    stat = [z["f"][r0 : r0 + n, :] for r0, n, _, _ in wins]

    def body(i, carry):
        k = nk - 1 - i
        kk = k.astype(jnp.float32)
        up_k = jnp.maximum(k - 1, 0)
        out = []
        for (r0, n, lo, hi), f, bottoms in zip(wins, stat, carry):
            tops = []
            for m in range(len(z["t"])):
                r_in, r_out = z["rin"][m][k, r0 : r0 + n, :], z["rout"][m][k, r0 : r0 + n, :]

                def limited(anti, far_in, far_out):
                    return anti * jnp.where(anti >= 0, jnp.minimum(far_in, r_out), jnp.minimum(r_in, far_out))

                f_e = limited(z["ax"][m][k, r0 : r0 + n, :], east_of(r_in), east_of(r_out))
                f_n = limited(
                    z["ay"][m][k, r0 : r0 + n, :],
                    z["rin"][m][k, r0 + 1 : r0 + 1 + n, :],
                    z["rout"][m][k, r0 + 1 : r0 + 1 + n, :],
                )
                f_t = limited(
                    z["az"][m][k, r0 : r0 + n, :],
                    z["rin"][m][up_k, r0 : r0 + n, :],
                    z["rout"][m][up_k, r0 : r0 + n, :],
                )
                low = z["low"][m][k, r0 : r0 + n, :]
                new = low - ((f_e - west_of(f_e)) + (f_n - south_of(f_n)) + (f_t - bottoms[m]))
                new = jnp.where(kk < f, new, 0.0)
                z["adv"][m][k, r0 + lo : r0 + hi, :] = new[lo:hi]
                tops.append(f_t)
            out.append(tuple(tops))
        return tuple(out)

    lax.fori_loop(0, nk, body, tuple(tuple(jnp.zeros((n, 128), jnp.float32) for _ in z["t"]) for _, n, _, _ in wins), unroll=nk)


def clip_slope(x):
    return jnp.clip(x, -slope_limit, slope_limit)


def stage_diffuse(z, wins, emit):
    nk = z["u"].shape[0]
    dens = z["density"]
    nt = len(z["t"])
    stat = []
    for r0, n, _, _ in wins:
        f = z["f"][r0 : r0 + n, :]
        far_e, far_n = east_of(f), z["f"][r0 + 1 : r0 + 1 + n, :]
        stat.append((f, far_e, far_n, jnp.minimum(f, far_e), jnp.minimum(f, far_n)))

    def inverse(grads):
        return pl.reciprocal(jnp.maximum(-dens(grads), strat_floor))

    def body(i, carry):
        k = nk - 1 - i
        kk = k.astype(jnp.float32)
        up_k = jnp.maximum(k - 1, 0)
        below_k = jnp.minimum(k + 1, nk - 1)
        not_top = (k >= 1).astype(jnp.float32)
        out = []
        for wi, ((r0, n, _, _), (f, far_e, far_n, f_e, f_n), old) in enumerate(zip(wins, stat, carry)):
            here = [a[k, r0 : r0 + n, :] for a in z["adv"]]
            north = [a[k, r0 + 1 : r0 + 1 + n, :] for a in z["adv"]]
            gz = [jnp.where(kk < f, a[up_k, r0 : r0 + n, :] - c, 0.0) for a, c in zip(z["adv"], here)]
            gz_n = [jnp.where(kk < far_n, a[up_k, r0 + 1 : r0 + 1 + n, :] - c, 0.0) for a, c in zip(z["adv"], north)]
            gz_e = [east_of(g) for g in gz]
            inv, inv_n = inverse(gz), inverse(gz_n)
            inv_e = east_of(inv)
            gx = [jnp.where(kk < f_e, east_of(c) - c, 0.0) for c in here]
            gy = [jnp.where(kk < f_n, b - c, 0.0) for b, c in zip(north, here)]
            rx, ry = dens(gx), dens(gy)
            (o_inv, o_inv_e, o_inv_n, o_gz, o_gz_e, o_gz_n, o_part, o_top) = old
            low_here, low_e, low_n = kk + 1.0 < f, kk + 1.0 < far_e, kk + 1.0 < far_n
            s_x = [clip_slope(rx * q) for q in (inv, inv_e, o_inv, o_inv_e)]
            s_y = [clip_slope(ry * q) for q in (inv, inv_n, o_inv, o_inv_n)]
            parts, tops = [], []
            for m in range(nt):
                gx_top, gy_top = gx[m] * not_top, gy[m] * not_top
                hx = (
                    gx_top + s_x[0] * gz[m],
                    gx_top + s_x[1] * gz_e[m],
                    jnp.where(low_here, gx[m], 0.0) + s_x[2] * o_gz[m],
                    jnp.where(low_e, gx[m], 0.0) + s_x[3] * o_gz_e[m],
                )
                hy = (
                    gy_top + s_y[0] * gz[m],
                    gy_top + s_y[1] * gz_n[m],
                    jnp.where(low_here, gy[m], 0.0) + s_y[2] * o_gz[m],
                    jnp.where(low_n, gy[m], 0.0) + s_y[3] * o_gz_n[m],
                )
                flux_e = (hx[0] + hx[1]) + (hx[2] + hx[3])
                flux_n = (hy[0] + hy[1]) + (hy[2] + hy[3])
                top = (s_x[0] * hx[0] + west_of(s_x[1] * hx[1])) + (s_y[0] * hy[0] + south_of(s_y[1] * hy[1]))
                bottom = (s_x[2] * hx[2] + west_of(s_x[3] * hx[3])) + (s_y[2] * hy[2] + south_of(s_y[3] * hy[3]))
                rise = o_top[m] + bottom
                done = jnp.where(kk + 1.0 < f, o_part[m] + DIFF_SCALE * rise, 0.0)
                emit(below_k, wi, m, done)
                parts.append(here[m] + DIFF_SCALE * ((flux_e - west_of(flux_e)) + (flux_n - south_of(flux_n)) - rise))
                tops.append(top)
            out.append((inv, inv_e, inv_n, tuple(gz), tuple(gz_e), tuple(gz_n), tuple(parts), tuple(tops)))
        return tuple(out)

    start = []
    for _, n, _, _ in wins:
        x = jnp.zeros((n, 128), jnp.float32)
        xs = tuple(x for _ in range(nt))
        start.append((x, x, x, xs, xs, xs, xs, xs))
    last = lax.fori_loop(0, nk, body, tuple(start), unroll=nk // 2)
    for wi, ((f, *_), old) in enumerate(zip(stat, last)):
        for m in range(nt):
            emit(0, wi, m, jnp.where(0.0 < f, old[6][m] + DIFF_SCALE * old[7][m], 0.0))


def lane_iota(rows):
    return lax.broadcasted_iota(jnp.int32, (rows, 128), 1)


def kernel(
    t_hbm, s_hbm, u_hbm, v_hbm, flag_hbm, point_hbm, count_hbm,
    t_out, s_out, e_res,
    flag_ref, point_ref, count_ref, tr, u, v, floor, low, mx, mn, ax, ay, az, rin, rout, adv,
    e_tr, e_u, e_v, e_floor, e_low, e_mx, e_mn, e_ax, e_ay, e_az, e_rin, e_rout, e_adv,
    row_out, row_in, strip_out, fold_out, strip_in, corner_in,
    load_sem, send_sem, recv_sem,
):
    n_lon, n_lat = lax.axis_size("lon"), lax.axis_size("lat")
    lon, lat = lax.axis_index("lon"), lax.axis_index("lat")
    nk = u.shape[0]
    half = nk // 2
    east, west = lax.rem(lon + 1, n_lon), lax.rem(lon + n_lon - 1, n_lon)
    at_north, at_south = lat == n_lat - 1, lat == 0
    fold_mid = n_lon - 1 - lon
    fold_ne = lax.rem(2 * n_lon - 2 - lon, n_lon)
    fold_nw = lax.rem(n_lon - lon, n_lon)

    side = [(EAST, (east, lat)), (WEST, (west, lat))]
    north = [(NORTH, (lon, lat + 1)), (NE, (east, lat + 1)), (NW, (west, lat + 1))]
    south = [(SOUTH, (lon, lat - 1)), (SE, (east, lat - 1)), (SW, (west, lat - 1))]
    folded = [(NORTH, (fold_mid, lat)), (NE, (fold_ne, lat)), (NW, (fold_nw, lat))]
    ne_self, nw_self = fold_ne == lon, fold_nw == lon
    not_self = {NORTH: True, NE: jnp.logical_not(ne_self), NW: jnp.logical_not(nw_self)}

    barrier = pltpu.get_barrier_semaphore()

    def greet(where):
        pl.semaphore_signal(barrier, inc=1, device_id=where, device_id_type=MESH)

    for _, where in side:
        greet(where)

    @pl.when(jnp.logical_not(at_south))
    def _():
        for _, where in south:
            greet(where)

    @pl.when(jnp.logical_not(at_north))
    def _():
        for _, where in north:
            greet(where)

    @pl.when(at_north)
    def _():
        greet(folded[0][1])

        @pl.when(jnp.logical_not(ne_self))
        def _():
            greet(folded[1][1])

        @pl.when(jnp.logical_not(nw_self))
        def _():
            greet(folded[2][1])

    loads = [
        pltpu.make_async_copy(src, dst.at[:, 8:24, :], load_sem.at[i])
        for i, (src, dst) in enumerate(((t_hbm, tr.at[0]), (s_hbm, tr.at[1]), (u_hbm, u), (v_hbm, v)))
    ]
    loads += [
        pltpu.make_async_copy(src, dst, load_sem.at[4 + i])
        for i, (src, dst) in enumerate(((flag_hbm, flag_ref), (point_hbm, point_ref), (count_hbm, count_ref)))
    ]
    for copy in loads:
        copy.start()
    for copy in loads:
        copy.wait()
    floor[8:24, :] = (count_ref[...] * point_ref[...] * flag_ref[...]).astype(jnp.float32)

    fields = ((tr.at[0], tr.at[1]), (u, v))
    for g, (a, b) in enumerate(fields):
        for k in range(nk):
            row_out[1, g * nk + k, 0:4, :] = a[k, 8:12, :]
            row_out[1, g * nk + k, 4:8, :] = b[k, 8:12, :]
    row_out[1, 2 * nk, 0:4, :] = floor[8:12, :]

    @pl.when(jnp.logical_not(at_north))
    def _():
        for g, (a, b) in enumerate(fields):
            for k in range(nk):
                row_out[0, g * nk + k, 0:4, :] = a[k, 20:24, :]
                row_out[0, g * nk + k, 4:8, :] = b[k, 20:24, :]
        row_out[0, 2 * nk, 0:4, :] = floor[20:24, :]

    lane8, sub8 = lane_iota(8), lax.broadcasted_iota(jnp.int32, (8, 128), 0)

    @pl.when(at_north)
    def _():
        def turned(x):
            x = jnp.take_along_axis(x, 127 - lane8, axis=1)
            return jnp.take_along_axis(x, 7 - sub8, axis=0)

        for g, (a, b) in enumerate(fields):
            sign = 1.0 if g == 0 else -1.0
            for k in range(nk):
                row_out[0, g * nk + k, 0:4, :] = sign * turned(a[k, 16:24, :])[0:4]
                row_out[0, g * nk + k, 4:8, :] = sign * turned(b[k, 16:24, :])[0:4]
        row_out[0, 2 * nk, 0:4, :] = turned(floor[16:24, :])[0:4]

    p = lax.rem(lane8, 64)
    shift = jnp.where(p < 12, 116, jnp.where(p < 16, -12, jnp.where(p < 20, 108, -20)))
    strip_idx = lax.rem(p + shift + 128, 128)
    first = lane8 < 64

    def strip_tile(row):
        def gather(x):
            return jnp.take_along_axis(x, strip_idx, axis=1)

        rows = slice(row, row + 8)
        for k in range(nk):
            e_tr[k, rows, :] = jnp.where(first, gather(tr[0, k, rows, :]), gather(tr[1, k, rows, :]))
            e_u[k, rows, :] = gather(u[k, rows, :])
            e_v[k, rows, :] = gather(v[k, rows, :])
        e_floor[rows, :] = gather(floor[rows, :])

    q = lax.rem(lane8, 32)
    q_t = jnp.logical_and(q >= 12, q < 20)
    q_u = jnp.logical_and(q >= 20, q < 28)
    p32 = lax.rem(lane8 + 124, 64) < 32
    for row in (8, 16):
        strip_tile(row)
        rows = slice(row, row + 8)
        for k in range(half):
            def packed(level):
                return jnp.where(
                    q_t, e_tr[level, rows, :],
                    jnp.where(q_u, pltpu.roll(e_u[level, rows, :], 8, 1), pltpu.roll(e_v[level, rows, :], 16, 1)),
                )

            strip_out[k, row - 8 : row, :] = jnp.where(p32, packed(k), pltpu.roll(packed(k + half), 32, 1))
        strip_out[half, row - 8 : row, :] = e_floor[rows, :]

    @pl.when(at_north)
    def _():
        group_idx = lax.rem(lane8 + 7 - 2 * lax.rem(lane8 + 4, 8) + 128, 128)
        sign = jnp.where(q_t, 1.0, -1.0)
        for k in range(half + 1):
            x = jnp.take_along_axis(strip_out[k, 8:16, :], group_idx, axis=1)
            x = jnp.take_along_axis(x, 7 - sub8, axis=0)
            fold_out[k] = x if k == half else x * sign

    n_north = jnp.where(at_north, 3 - ne_self.astype(jnp.int32) - nw_self.astype(jnp.int32), 3)
    pl.semaphore_wait(barrier, 2 + n_north + jnp.where(at_south, 0, 3))

    def send(src, dst, role, slot, where):
        return pltpu.make_async_remote_copy(
            src_ref=src, dst_ref=dst, send_sem=send_sem.at[role], recv_sem=recv_sem.at[slot],
            device_id=where, device_id_type=MESH,
        )

    corner = {NE: 0, NW: 1, SE: 2, SW: 3}

    def to_rows(role, slot, where):
        return send(row_out.at[0 if role == NORTH else 1], row_in.at[0 if slot == NORTH else 1], role, slot, where)

    def to_corner(role, slot, where, fold=False):
        src = fold_out if fold else strip_out.at[:, 8:16, :] if role in (NE, NW) else strip_out.at[:, 0:8, :]
        return send(src, corner_in.at[corner[slot]], role, slot, where)

    side_sends = [
        send(strip_out, strip_in.at[0], WEST, EAST, (west, lat)),
        send(strip_out, strip_in.at[1], EAST, WEST, (east, lat)),
    ]
    north_sends = [
        to_rows(NORTH, SOUTH, north[0][1]),
        to_corner(NE, SW, north[1][1]),
        to_corner(NW, SE, north[2][1]),
    ]
    south_sends = [
        to_rows(SOUTH, NORTH, south[0][1]),
        to_corner(SE, NW, south[1][1]),
        to_corner(SW, NE, south[2][1]),
    ]
    fold_sends = [
        to_rows(NORTH, NORTH, folded[0][1]),
        to_corner(NE, NE, folded[1][1], True),
        to_corner(NW, NW, folded[2][1], True),
    ]
    ne_local = pltpu.make_async_copy(fold_out, corner_in.at[corner[NE]], send_sem.at[NE])
    nw_local = pltpu.make_async_copy(fold_out, corner_in.at[corner[NW]], send_sem.at[NW])

    @pl.when(jnp.logical_not(at_south))
    def _():
        for copy in south_sends:
            copy.start()

    @pl.when(jnp.logical_not(at_north))
    def _():
        for copy in north_sends:
            copy.start()

    @pl.when(at_north)
    def _():
        fold_sends[0].start()
        for copy, local, own in ((fold_sends[1], ne_local, ne_self), (fold_sends[2], nw_local, nw_self)):
            @pl.when(own)
            def _():
                local.start()

            @pl.when(jnp.logical_not(own))
            def _():
                copy.start()

    for copy in side_sends:
        copy.start()

    main = dict(
        t=[tr.at[0], tr.at[1]], u=u, v=v, f=floor,
        density=lambda pair: haline_coef * pair[1] - thermal_coef * pair[0],
    )
    names = dict(low=low, mx=mx, mn=mn, ax=ax, ay=ay, az=az, rin=rin, rout=rout, adv=adv)
    main.update({name: [ref.at[0], ref.at[1]] for name, ref in names.items()})

    outs = (t_out, s_out)

    stage_flux(main, [(8, 16, 0, 16)])
    stage_ratio(main, [(8, 16, 0, 16)])
    stage_limit(main, [(8, 16, 0, 16)])

    def emit_inner(k, wi, m, val):
        outs[m][k, 4:12, :] = val[4:12]

    stage_diffuse(main, [(8, 16, 4, 12)], emit_inner)

    @pl.when(at_south)
    def _():
        row_in[1] = jnp.zeros(row_in.shape[1:], jnp.float32)

    @pl.when(jnp.logical_not(at_south))
    def _():
        north_sends[0].wait_recv()

    @pl.when(jnp.logical_not(at_north))
    def _():
        south_sends[0].wait_recv()

    @pl.when(at_north)
    def _():
        fold_sends[0].wait_recv()

    for slot, row in ((1, 4), (0, 24)):
        for g, (a, b) in enumerate(fields):
            for k in range(nk):
                a[k, row : row + 4, :] = row_in[slot, g * nk + k, 0:4, :]
                b[k, row : row + 4, :] = row_in[slot, g * nk + k, 4:8, :]
        floor[row : row + 4, :] = row_in[slot, 2 * nk, 0:4, :]

    stage_flux(main, [(4, 8, 1, 5), (20, 8, 3, 7)])
    stage_ratio(main, [(4, 8, 2, 6), (20, 8, 2, 6)])
    stage_limit(main, [(4, 8, 3, 7), (20, 8, 1, 5)])

    def emit_outer(k, wi, m, val):
        if wi == 0:
            outs[m][k, 0:4, :] = val[4:8]
        else:
            outs[m][k, 12:16, :] = val[4:8]

    stage_diffuse(main, [(4, 8, 4, 8), (16, 8, 4, 8)], emit_outer)

    @pl.when(at_south)
    def _():
        corner_in[corner[SE]] = jnp.zeros(corner_in.shape[1:], jnp.float32)
        corner_in[corner[SW]] = jnp.zeros(corner_in.shape[1:], jnp.float32)

    @pl.when(jnp.logical_not(at_south))
    def _():
        for copy in north_sends[1:]:
            copy.wait_recv()
        for copy in south_sends:
            copy.wait_send()

    @pl.when(jnp.logical_not(at_north))
    def _():
        for copy in south_sends[1:]:
            copy.wait_recv()
        for copy in north_sends:
            copy.wait_send()

    @pl.when(at_north)
    def _():
        fold_sends[0].wait_send()
        for copy, local, own in ((fold_sends[1], ne_local, ne_self), (fold_sends[2], nw_local, nw_self)):
            @pl.when(own)
            def _():
                local.wait()

            @pl.when(jnp.logical_not(own))
            def _():
                copy.wait()

    for copy in side_sends:
        copy.wait()

    strip_tile(0)
    strip_tile(24)
    halo = jnp.logical_and(p >= 12, p < 20)
    from_east = lax.rem(lane8, 8) >= 4
    for row, east_ref, west_ref, at in (
        (0, corner_in.at[corner[SE]], corner_in.at[corner[SW]], 0),
        (8, strip_in.at[0], strip_in.at[1], 0),
        (16, strip_in.at[0], strip_in.at[1], 8),
        (24, corner_in.at[corner[NE]], corner_in.at[corner[NW]], 0),
    ):
        rows = slice(row, row + 8)
        for k in range(half + 1):
            x = jnp.where(from_east, east_ref[k, at : at + 8, :], west_ref[k, at : at + 8, :])
            if k == half:
                e_floor[rows, :] = jnp.where(halo, x, e_floor[rows, :])
                continue
            for level, y in ((k, x), (k + half, pltpu.roll(x, 96, 1))):
                e_tr[level, rows, :] = jnp.where(halo, y, e_tr[level, rows, :])
                e_u[level, rows, :] = jnp.where(halo, pltpu.roll(y, 120, 1), e_u[level, rows, :])
                e_v[level, rows, :] = jnp.where(halo, pltpu.roll(y, 112, 1), e_v[level, rows, :])

    def strip_density(one):
        x = one[0]
        low_half = lane_iota(x.shape[0]) < 64
        own = jnp.where(low_half, -thermal_coef, haline_coef)
        other = jnp.where(low_half, haline_coef, -thermal_coef)
        return own * x + other * pltpu.roll(x, 64, 1)

    strips = dict(t=[e_tr], u=e_u, v=e_v, f=e_floor, density=strip_density)
    names = dict(low=e_low, mx=e_mx, mn=e_mn, ax=e_ax, ay=e_ay, az=e_az, rin=e_rin, rout=e_rout, adv=e_adv)
    strips.update({name: [ref] for name, ref in names.items()})
    stage_flux(strips, [(4, 24, 0, 24)])
    stage_ratio(strips, [(4, 24, 0, 24)])
    stage_limit(strips, [(4, 24, 0, 24)])

    def emit_strip(k, wi, m, val):
        e_res[k] = val[4:20]

    stage_diffuse(strips, [(4, 24, 4, 20)], emit_strip)


def finish(t_ref, s_ref, e_res, t_hbm, s_hbm, t_buf, s_buf, sem):
    lane16 = lane_iota(16)
    rim = jnp.logical_or(lane16 < 4, lane16 >= 124)
    copies = []
    for m, (ref, buf, out) in enumerate(((t_ref, t_buf, t_hbm), (s_ref, s_buf, s_hbm))):
        back = jnp.where(lane16 < 4, lane16 + 20, jnp.where(lane16 >= 124, lane16 - 116, 0)) + 64 * m
        for k in range(ref.shape[0]):
            buf[k] = jnp.where(rim, jnp.take_along_axis(e_res[k], back, axis=1), ref[k])
        copies.append(pltpu.make_async_copy(buf, out, sem.at[m]))
        copies[-1].start()
    for copy in copies:
        copy.wait()


def on_device(t, s, u, v, flag, point, count):
    nk = t.shape[0]
    f32 = jnp.float32
    vm = lambda *shape: pltpu.VMEM(shape, f32)
    big = lambda: vm(2, nk, 32, 128)
    one = lambda: vm(nk, 32, 128)
    whole = pl.BlockSpec(memory_space=pltpu.VMEM)
    hbm = pl.BlockSpec(memory_space=pltpu.HBM)
    part = pltpu.VMEM(t.shape, f32)
    main_t, main_s, strips = pl.pallas_call(
        kernel,
        out_shape=(part, part, part),
        in_specs=[hbm] * 7,
        out_specs=(whole, whole, whole),
        scratch_shapes=[
            pltpu.VMEM(flag.shape, flag.dtype), pltpu.VMEM(point.shape, point.dtype), pltpu.VMEM(count.shape, count.dtype),
            big(), one(), one(), vm(32, 128),
            *[big() for _ in range(9)],
            one(), one(), one(), vm(32, 128),
            *[one() for _ in range(9)],
            vm(2, 2 * nk + 1, 8, 128), vm(2, 2 * nk + 1, 8, 128),
            vm(nk // 2 + 1, 16, 128), vm(nk // 2 + 1, 8, 128),
            vm(2, nk // 2 + 1, 16, 128), vm(4, nk // 2 + 1, 8, 128),
            pltpu.SemaphoreType.DMA((7,)), pltpu.SemaphoreType.DMA((8,)), pltpu.SemaphoreType.DMA((8,)),
        ],
        compiler_params=pltpu.CompilerParams(
            collective_id=0, has_side_effects=True, vmem_limit_bytes=60 * 1024 * 1024
        ),
    )(t, s, u, v, flag, point, count)
    result = jax.ShapeDtypeStruct(t.shape, f32)
    return pl.pallas_call(
        finish,
        out_shape=(result, result),
        in_specs=[whole] * 3,
        out_specs=(hbm, hbm),
        scratch_shapes=[vm(*t.shape), vm(*t.shape), pltpu.SemaphoreType.DMA((2,))],
        compiler_params=pltpu.CompilerParams(vmem_limit_bytes=4 * 1024 * 1024),
    )(main_t, main_s, strips)


def solution(mesh):
    grid = P(None, "lat", "lon")
    flat = P("lat", "lon")
    return jax.shard_map(
        on_device, mesh=mesh, in_specs=(grid,) * 4 + (flat,) * 3, out_specs=(grid, grid), check_vma=False
    )
```

```python
import functools

import jax
import jax.numpy as jnp
from jax import lax
from jax.experimental import pallas as pl
from jax.experimental.pallas import tpu as pltpu
from jax.sharding import PartitionSpec as P

time_step = 0.5
diffusivity = 0.1
strat_floor = 0.5
slope_limit = 2.0
thermal_coef = 0.2
haline_coef = 0.8

MESH = pl.DeviceIdType.MESH
INF = float("inf")
TINY = 1e-37
FACE_SCALE = 0.25 * time_step
DIFF_SCALE = 0.25 * time_step * diffusivity

EAST, WEST, NORTH, SOUTH, NE, NW, SE, SW = range(8)


def east_of(x):
    return pltpu.roll(x, x.shape[1] - 1, 1)


def west_of(x):
    return pltpu.roll(x, 1, 1)


def south_of(x):
    return pltpu.roll(x, 1, 0)


def lane_iota(rows):
    return lax.broadcasted_iota(jnp.int32, (rows, 128), 1)


def upper_lanes(rows):
    return lax.rem(lane_iota(rows), 64) < 32


def to_upper(x):
    return jnp.where(upper_lanes(x.shape[0]), pltpu.roll(x, 96, 1), 0.0)


def to_lower(x):
    return jnp.where(upper_lanes(x.shape[0]), 0.0, pltpu.roll(x, 32, 1))


def above(z, ref, k, r0, n):
    if not z["split"]:
        return ref[jnp.maximum(k - 1, 0), r0 : r0 + n, :]
    if k > 0:
        return ref[k - 1, r0 : r0 + n, :]
    last = z["u"].shape[0] - 1
    return jnp.where(upper_lanes(n), ref[0, r0 : r0 + n, :], pltpu.roll(ref[last, r0 : r0 + n, :], 32, 1))


def below(z, ref, k, r0, n):
    last = z["u"].shape[0] - 1
    if not z["split"]:
        return ref[jnp.minimum(k + 1, last), r0 : r0 + n, :]
    if k < last:
        return ref[k + 1, r0 : r0 + n, :]
    return jnp.where(upper_lanes(n), pltpu.roll(ref[0, r0 : r0 + n, :], 96, 1), ref[last, r0 : r0 + n, :])


def upward(z, body, carry, unroll):
    nk = z["u"].shape[0]
    if z["split"]:
        for k in range(nk - 1, -1, -1):
            carry = body(k, jnp.float32(k), carry)
        return carry

    def step(i, carry):
        k = nk - 1 - i
        return body(k, k.astype(jnp.float32), carry)

    return lax.fori_loop(0, nk, step, carry, unroll=unroll)


def nothing(z, wins):
    return tuple(tuple(jnp.zeros((n, 128), jnp.float32) for _ in z["t"]) for _, n, _, _ in wins)


def stage_flux(z, wins):
    nk = z["u"].shape[0]
    stat = []
    for r0, n, _, _ in wins:
        f = z["f"][r0 : r0 + n, :]
        f_e = jnp.minimum(f, east_of(f))
        f_n = jnp.minimum(f, z["f"][r0 + 1 : r0 + 1 + n, :])
        stat.append((f, f_e, f_n))

    def velocities(k, kk, r0, n, f_e, f_n):
        u = z["u"][k, r0 : r0 + n, :]
        u_e = jnp.where(kk < f_e, FACE_SCALE * (u + east_of(u)), 0.0)
        v = z["v"][k, r0 : r0 + n, :]
        v_n = jnp.where(kk < f_n, FACE_SCALE * (v + z["v"][k, r0 + 1 : r0 + 1 + n, :]), 0.0)
        return u_e, v_n, u_e - west_of(u_e) + v_n - south_of(v_n)

    def body(k, kk, carry):
        out = []
        for (r0, n, lo, hi), (f, f_e, f_n), (w_old, bottoms) in zip(wins, stat, carry):
            u_e, v_n, gain = velocities(k, kk, r0, n, f_e, f_n)
            w = w_old - gain
            abs_u, abs_v, abs_w = jnp.abs(u_e), jnp.abs(v_n), jnp.abs(w)
            wet = kk < f
            tops = []
            for m, t in enumerate(z["t"]):
                c = t[k, r0 : r0 + n, :]
                e = east_of(c)
                nn = t[k, r0 + 1 : r0 + 1 + n, :]
                up = above(z, t, k, r0, n)
                a_e = abs_u * (e - c)
                l_e = u_e * (c + e) - a_e
                a_n = abs_v * (nn - c)
                l_n = v_n * (c + nn) - a_n
                a_t = abs_w * (up - c)
                l_t = w * (c + up) - a_t
                low = c - ((l_e - west_of(l_e)) + (l_n - south_of(l_n)) + (l_t - bottoms[m]))
                low = jnp.where(wet, low, 0.0)
                big = jnp.where(wet, jnp.maximum(c, low), -INF)
                small = jnp.where(wet, jnp.minimum(c, low), INF)
                for name, val in (("ax", a_e), ("ay", a_n), ("az", a_t), ("low", low), ("mx", big), ("mn", small)):
                    z[name][m][k, r0 + lo : r0 + hi, :] = val[lo:hi]
                tops.append(l_t)
            out.append((w, tuple(tops)))
        return tuple(out)

    start = []
    for (r0, n, _, _), (f, f_e, f_n) in zip(wins, stat):
        w = jnp.zeros((n, 128), jnp.float32)
        flows = tuple(w for _ in z["t"])
        if z["split"]:
            for k in range(nk):
                w = w - velocities(k, jnp.float32(k), r0, n, f_e, f_n)[2]
            w = to_upper(w)
            flows = []
            for t in z["t"]:
                up, c = t[nk - 1, r0 : r0 + n, :], below(z, t, nk - 1, r0, n)
                flows.append(w * (c + up) - jnp.abs(w) * (up - c))
        start.append((w, tuple(flows)))
    upward(z, body, tuple(start), nk)


def stage_ratio(z, wins):
    nk = z["u"].shape[0]

    def body(k, kk, carry):
        out = []
        for (r0, n, lo, hi), bottoms in zip(wins, carry):
            tops = []
            for m in range(len(z["t"])):
                def near(ref, pick):
                    c = ref[k, r0 : r0 + n, :]
                    horizontal = pick(pick(east_of(c), west_of(c)), pick(ref[k, r0 + 1 : r0 + 1 + n, :], ref[k, r0 - 1 : r0 - 1 + n, :]))
                    return pick(pick(c, horizontal), pick(above(z, ref, k, r0, n), below(z, ref, k, r0, n)))

                big, small = near(z["mx"][m], jnp.maximum), near(z["mn"][m], jnp.minimum)
                low = z["low"][m][k, r0 : r0 + n, :]
                a_e = z["ax"][m][k, r0 : r0 + n, :]
                a_w = west_of(a_e)
                a_n = z["ay"][m][k, r0 : r0 + n, :]
                a_s = z["ay"][m][k, r0 - 1 : r0 - 1 + n, :]
                a_t, a_b = z["az"][m][k, r0 : r0 + n, :], bottoms[m]
                p_in, p_out = 0.0, 0.0
                for inward, outward in ((a_w, a_e), (a_s, a_n), (a_b, a_t)):
                    p_in = p_in + (jnp.maximum(inward, 0.0) - jnp.minimum(outward, 0.0))
                    p_out = p_out + (jnp.maximum(outward, 0.0) - jnp.minimum(inward, 0.0))
                r_in = jnp.clip((big - low) * pl.reciprocal(jnp.maximum(p_in, TINY)), 0.0, 1.0)
                r_out = jnp.clip((low - small) * pl.reciprocal(jnp.maximum(p_out, TINY)), 0.0, 1.0)
                z["rin"][m][k, r0 + lo : r0 + hi, :] = r_in[lo:hi]
                z["rout"][m][k, r0 + lo : r0 + hi, :] = r_out[lo:hi]
                tops.append(a_t)
            out.append(tuple(tops))
        return tuple(out)

    start = nothing(z, wins)
    if z["split"]:
        start = tuple(tuple(to_upper(a[0, r0 : r0 + n, :]) for a in z["az"]) for r0, n, _, _ in wins)
    upward(z, body, start, nk)


def limited(anti, r_in, r_out, far_in, far_out):
    return anti * jnp.where(anti >= 0, jnp.minimum(far_in, r_out), jnp.minimum(r_in, far_out))


def stage_limit(z, wins):
    nk = z["u"].shape[0]
    stat = [z["f"][r0 : r0 + n, :] for r0, n, _, _ in wins]

    def rise(m, k, r0, n):
        r_in, r_out = z["rin"][m][k, r0 : r0 + n, :], z["rout"][m][k, r0 : r0 + n, :]
        far_in, far_out = above(z, z["rin"][m], k, r0, n), above(z, z["rout"][m], k, r0, n)
        return limited(z["az"][m][k, r0 : r0 + n, :], r_in, r_out, far_in, far_out)

    def body(k, kk, carry):
        out = []
        for (r0, n, lo, hi), f, bottoms in zip(wins, stat, carry):
            tops = []
            for m in range(len(z["t"])):
                r_in, r_out = z["rin"][m][k, r0 : r0 + n, :], z["rout"][m][k, r0 : r0 + n, :]
                f_e = limited(z["ax"][m][k, r0 : r0 + n, :], r_in, r_out, east_of(r_in), east_of(r_out))
                f_n = limited(
                    z["ay"][m][k, r0 : r0 + n, :], r_in, r_out,
                    z["rin"][m][k, r0 + 1 : r0 + 1 + n, :], z["rout"][m][k, r0 + 1 : r0 + 1 + n, :],
                )
                f_t = rise(m, k, r0, n)
                low = z["low"][m][k, r0 : r0 + n, :]
                new = low - ((f_e - west_of(f_e)) + (f_n - south_of(f_n)) + (f_t - bottoms[m]))
                new = jnp.where(kk < f, new, 0.0)
                z["adv"][m][k, r0 + lo : r0 + hi, :] = new[lo:hi]
                tops.append(f_t)
            out.append(tuple(tops))
        return tuple(out)

    start = nothing(z, wins)
    if z["split"]:
        start = tuple(tuple(to_upper(rise(m, 0, r0, n)) for m in range(len(z["t"]))) for r0, n, _, _ in wins)
    upward(z, body, start, nk)


def clip_slope(x):
    return jnp.clip(x, -slope_limit, slope_limit)


def stage_diffuse(z, wins, emit):
    nk = z["u"].shape[0]
    dens = z["density"]
    nt = len(z["t"])
    stat = []
    for r0, n, _, _ in wins:
        f = z["f"][r0 : r0 + n, :]
        far_e, far_n = east_of(f), z["f"][r0 + 1 : r0 + 1 + n, :]
        stat.append((f, far_e, far_n, jnp.minimum(f, far_e), jnp.minimum(f, far_n)))

    def inverse(grads):
        return pl.reciprocal(jnp.maximum(-dens(grads), strat_floor))

    def vertical(k, kk, r0, n, f, far_n):
        gz = [jnp.where(kk < f, above(z, a, k, r0, n) - a[k, r0 : r0 + n, :], 0.0) for a in z["adv"]]
        gz_n = [jnp.where(kk < far_n, above(z, a, k, r0 + 1, n) - a[k, r0 + 1 : r0 + 1 + n, :], 0.0) for a in z["adv"]]
        inv = inverse(gz)
        return inv, east_of(inv), inverse(gz_n), tuple(gz), tuple(east_of(g) for g in gz), tuple(gz_n)

    def body(k, kk, carry):
        out = []
        for wi, ((r0, n, _, _), (f, far_e, far_n, f_e, f_n), old) in enumerate(zip(wins, stat, carry)):
            if not z["split"]:
                not_top = (k >= 1).astype(jnp.float32)
            elif k == 0:
                not_top = jnp.where(upper_lanes(n), 0.0, 1.0)
            here = [a[k, r0 : r0 + n, :] for a in z["adv"]]
            north = [a[k, r0 + 1 : r0 + 1 + n, :] for a in z["adv"]]
            inv, inv_e, inv_n, gz, gz_e, gz_n = vertical(k, kk, r0, n, f, far_n)
            gx = [jnp.where(kk < f_e, east_of(c) - c, 0.0) for c in here]
            gy = [jnp.where(kk < f_n, b - c, 0.0) for b, c in zip(north, here)]
            rx, ry = dens(gx), dens(gy)
            (o_inv, o_inv_e, o_inv_n, o_gz, o_gz_e, o_gz_n), o_part, o_top = old
            low_here, low_e, low_n = kk + 1.0 < f, kk + 1.0 < far_e, kk + 1.0 < far_n
            s_x = [clip_slope(rx * q) for q in (inv, inv_e, o_inv, o_inv_e)]
            s_y = [clip_slope(ry * q) for q in (inv, inv_n, o_inv, o_inv_n)]
            parts, tops = [], []
            for m in range(nt):
                gx_top, gy_top = gx[m], gy[m]
                if not z["split"] or k == 0:
                    gx_top, gy_top = gx_top * not_top, gy_top * not_top
                hx = (
                    gx_top + s_x[0] * gz[m],
                    gx_top + s_x[1] * gz_e[m],
                    jnp.where(low_here, gx[m], 0.0) + s_x[2] * o_gz[m],
                    jnp.where(low_e, gx[m], 0.0) + s_x[3] * o_gz_e[m],
                )
                hy = (
                    gy_top + s_y[0] * gz[m],
                    gy_top + s_y[1] * gz_n[m],
                    jnp.where(low_here, gy[m], 0.0) + s_y[2] * o_gz[m],
                    jnp.where(low_n, gy[m], 0.0) + s_y[3] * o_gz_n[m],
                )
                flux_e = (hx[0] + hx[1]) + (hx[2] + hx[3])
                flux_n = (hy[0] + hy[1]) + (hy[2] + hy[3])
                top = (s_x[0] * hx[0] + west_of(s_x[1] * hx[1])) + (s_y[0] * hy[0] + south_of(s_y[1] * hy[1]))
                bottom = (s_x[2] * hx[2] + west_of(s_x[3] * hx[3])) + (s_y[2] * hy[2] + south_of(s_y[3] * hy[3]))
                rise = o_top[m] + bottom
                if z["split"] and k == nk - 1:
                    bottom_lower[wi, m] = to_lower(bottom)
                else:
                    done = jnp.where(kk + 1.0 < f, o_part[m] + DIFF_SCALE * rise, 0.0)
                    emit(k + 1 if z["split"] else jnp.minimum(k + 1, nk - 1), wi, m, done)
                parts.append(here[m] + DIFF_SCALE * ((flux_e - west_of(flux_e)) + (flux_n - south_of(flux_n)) - rise))
                tops.append(top)
            out.append(((inv, inv_e, inv_n, gz, gz_e, gz_n), tuple(parts), tuple(tops)))
        return tuple(out)

    bottom_lower = {}
    start = []
    for (r0, n, _, _), (f, _, far_n, *_) in zip(wins, stat):
        x = jnp.zeros((n, 128), jnp.float32)
        xs = tuple(x for _ in range(nt))
        first = (x, x, x, xs, xs, xs)
        if z["split"]:
            first = jax.tree.map(to_upper, vertical(0, jnp.float32(0), r0, n, f, far_n))
        start.append((first, xs, xs))
    last = upward(z, body, tuple(start), nk // 2)
    for wi, ((r0, n, _, _), (f, *_), (_, parts, tops)) in enumerate(zip(wins, stat, last)):
        for m in range(nt):
            top = tops[m]
            if z["split"]:
                top = top + bottom_lower[wi, m]
                late = jnp.where(nk - 1.0 < f, -DIFF_SCALE * to_upper(tops[m]), 0.0)
                emit(nk - 1, wi, m, late, True)
            emit(0, wi, m, jnp.where(0.0 < f, parts[m] + DIFF_SCALE * top, 0.0))


def kernel(
    t_hbm, s_hbm, u_hbm, v_hbm, flag_hbm, point_hbm, count_hbm,
    t_out, s_out, e_res,
    flag_ref, point_ref, count_ref, tr, u, v, floor, low, mx, mn, ax, ay, az, rin, rout, adv,
    e_tr, e_u, e_v, e_floor, e_low, e_mx, e_mn, e_ax, e_ay, e_az, e_rin, e_rout, e_adv,
    row_out, row_in, strip_out, fold_out, strip_in, corner_in,
    load_sem, send_sem, recv_sem,
):
    n_lon, n_lat = lax.axis_size("lon"), lax.axis_size("lat")
    lon, lat = lax.axis_index("lon"), lax.axis_index("lat")
    nk = u.shape[0]
    half = nk // 2
    east, west = lax.rem(lon + 1, n_lon), lax.rem(lon + n_lon - 1, n_lon)
    at_north, at_south = lat == n_lat - 1, lat == 0
    fold_mid = n_lon - 1 - lon
    fold_ne = lax.rem(2 * n_lon - 2 - lon, n_lon)
    fold_nw = lax.rem(n_lon - lon, n_lon)

    side = [(EAST, (east, lat)), (WEST, (west, lat))]
    north = [(NORTH, (lon, lat + 1)), (NE, (east, lat + 1)), (NW, (west, lat + 1))]
    south = [(SOUTH, (lon, lat - 1)), (SE, (east, lat - 1)), (SW, (west, lat - 1))]
    folded = [(NORTH, (fold_mid, lat)), (NE, (fold_ne, lat)), (NW, (fold_nw, lat))]
    ne_self, nw_self = fold_ne == lon, fold_nw == lon
    not_self = {NORTH: True, NE: jnp.logical_not(ne_self), NW: jnp.logical_not(nw_self)}

    barrier = pltpu.get_barrier_semaphore()

    def greet(where):
        pl.semaphore_signal(barrier, inc=1, device_id=where, device_id_type=MESH)

    for _, where in side:
        greet(where)

    @pl.when(jnp.logical_not(at_south))
    def _():
        for _, where in south:
            greet(where)

    @pl.when(jnp.logical_not(at_north))
    def _():
        for _, where in north:
            greet(where)

    @pl.when(at_north)
    def _():
        greet(folded[0][1])

        @pl.when(jnp.logical_not(ne_self))
        def _():
            greet(folded[1][1])

        @pl.when(jnp.logical_not(nw_self))
        def _():
            greet(folded[2][1])

    loads = [
        pltpu.make_async_copy(src, dst.at[:, 8:24, :], load_sem.at[i])
        for i, (src, dst) in enumerate(((t_hbm, tr.at[0]), (s_hbm, tr.at[1]), (u_hbm, u), (v_hbm, v)))
    ]
    loads += [
        pltpu.make_async_copy(src, dst, load_sem.at[4 + i])
        for i, (src, dst) in enumerate(((flag_hbm, flag_ref), (point_hbm, point_ref), (count_hbm, count_ref)))
    ]
    for copy in loads:
        copy.start()
    for copy in loads:
        copy.wait()
    floor[8:24, :] = (count_ref[...] * point_ref[...] * flag_ref[...]).astype(jnp.float32)

    fields = ((tr.at[0], tr.at[1]), (u, v))
    for g, (a, b) in enumerate(fields):
        for k in range(nk):
            row_out[1, g * nk + k, 0:4, :] = a[k, 8:12, :]
            row_out[1, g * nk + k, 4:8, :] = b[k, 8:12, :]
    row_out[1, 2 * nk, 0:4, :] = floor[8:12, :]

    @pl.when(jnp.logical_not(at_north))
    def _():
        for g, (a, b) in enumerate(fields):
            for k in range(nk):
                row_out[0, g * nk + k, 0:4, :] = a[k, 20:24, :]
                row_out[0, g * nk + k, 4:8, :] = b[k, 20:24, :]
        row_out[0, 2 * nk, 0:4, :] = floor[20:24, :]

    lane8, sub8 = lane_iota(8), lax.broadcasted_iota(jnp.int32, (8, 128), 0)

    @pl.when(at_north)
    def _():
        def turned(x):
            x = jnp.take_along_axis(x, 127 - lane8, axis=1)
            return jnp.take_along_axis(x, 7 - sub8, axis=0)

        for g, (a, b) in enumerate(fields):
            sign = 1.0 if g == 0 else -1.0
            for k in range(nk):
                row_out[0, g * nk + k, 0:4, :] = sign * turned(a[k, 16:24, :])[0:4]
                row_out[0, g * nk + k, 4:8, :] = sign * turned(b[k, 16:24, :])[0:4]
        row_out[0, 2 * nk, 0:4, :] = turned(floor[16:24, :])[0:4]

    p = lax.rem(lane8, 32)
    shift = jnp.where(p < 12, 116, jnp.where(p < 16, -12, jnp.where(p < 20, 108, -20)))
    strip_idx = lax.rem(p + shift + 128, 128)
    first, upper = lane8 < 64, upper_lanes(8)

    def strip_tile(row):
        rows = slice(row, row + 8)

        def gather(x):
            return jnp.take_along_axis(x, strip_idx, axis=1)

        def halves(ref, k):
            return jnp.where(upper, gather(ref[k, rows, :]), gather(ref[k + half, rows, :]))

        for k in range(half):
            e_tr[k, rows, :] = jnp.where(first, halves(tr.at[0], k), halves(tr.at[1], k))
            e_u[k, rows, :] = halves(u, k)
            e_v[k, rows, :] = halves(v, k)
        e_floor[rows, :] = gather(floor[rows, :]) - jnp.where(upper, 0.0, float(half))

    q_t = jnp.logical_and(p >= 12, p < 20)
    q_u = jnp.logical_and(p >= 20, p < 28)
    for row in (8, 16):
        strip_tile(row)
        rows = slice(row, row + 8)
        for k in range(half):
            strip_out[k, row - 8 : row, :] = jnp.where(
                q_t, e_tr[k, rows, :],
                jnp.where(q_u, pltpu.roll(e_u[k, rows, :], 8, 1), pltpu.roll(e_v[k, rows, :], 16, 1)),
            )
        strip_out[half, row - 8 : row, :] = e_floor[rows, :]

    @pl.when(at_north)
    def _():
        group_idx = lax.rem(lane8 + 7 - 2 * lax.rem(lane8 + 4, 8) + 128, 128)
        sign = jnp.where(q_t, 1.0, -1.0)
        for k in range(half + 1):
            x = jnp.take_along_axis(strip_out[k, 8:16, :], group_idx, axis=1)
            x = jnp.take_along_axis(x, 7 - sub8, axis=0)
            fold_out[k] = x if k == half else x * sign

    n_north = jnp.where(at_north, 3 - ne_self.astype(jnp.int32) - nw_self.astype(jnp.int32), 3)
    pl.semaphore_wait(barrier, 2 + n_north + jnp.where(at_south, 0, 3))

    def send(src, dst, role, slot, where):
        return pltpu.make_async_remote_copy(
            src_ref=src, dst_ref=dst, send_sem=send_sem.at[role], recv_sem=recv_sem.at[slot],
            device_id=where, device_id_type=MESH,
        )

    corner = {NE: 0, NW: 1, SE: 2, SW: 3}

    def to_rows(role, slot, where):
        return send(row_out.at[0 if role == NORTH else 1], row_in.at[0 if slot == NORTH else 1], role, slot, where)

    def to_corner(role, slot, where, fold=False):
        src = fold_out if fold else strip_out.at[:, 8:16, :] if role in (NE, NW) else strip_out.at[:, 0:8, :]
        return send(src, corner_in.at[corner[slot]], role, slot, where)

    side_sends = [
        send(strip_out, strip_in.at[0], WEST, EAST, (west, lat)),
        send(strip_out, strip_in.at[1], EAST, WEST, (east, lat)),
    ]
    north_sends = [
        to_rows(NORTH, SOUTH, north[0][1]),
        to_corner(NE, SW, north[1][1]),
        to_corner(NW, SE, north[2][1]),
    ]
    south_sends = [
        to_rows(SOUTH, NORTH, south[0][1]),
        to_corner(SE, NW, south[1][1]),
        to_corner(SW, NE, south[2][1]),
    ]
    fold_sends = [
        to_rows(NORTH, NORTH, folded[0][1]),
        to_corner(NE, NE, folded[1][1], True),
        to_corner(NW, NW, folded[2][1], True),
    ]
    ne_local = pltpu.make_async_copy(fold_out, corner_in.at[corner[NE]], send_sem.at[NE])
    nw_local = pltpu.make_async_copy(fold_out, corner_in.at[corner[NW]], send_sem.at[NW])

    @pl.when(jnp.logical_not(at_south))
    def _():
        for copy in south_sends:
            copy.start()

    @pl.when(jnp.logical_not(at_north))
    def _():
        for copy in north_sends:
            copy.start()

    @pl.when(at_north)
    def _():
        fold_sends[0].start()
        for copy, local, own in ((fold_sends[1], ne_local, ne_self), (fold_sends[2], nw_local, nw_self)):
            @pl.when(own)
            def _():
                local.start()

            @pl.when(jnp.logical_not(own))
            def _():
                copy.start()

    for copy in side_sends:
        copy.start()

    main = dict(
        split=False, t=[tr.at[0], tr.at[1]], u=u, v=v, f=floor,
        density=lambda pair: haline_coef * pair[1] - thermal_coef * pair[0],
    )
    names = dict(low=low, mx=mx, mn=mn, ax=ax, ay=ay, az=az, rin=rin, rout=rout, adv=adv)
    main.update({name: [ref.at[0], ref.at[1]] for name, ref in names.items()})

    outs = (t_out, s_out)

    stage_flux(main, [(8, 16, 0, 16)])
    stage_ratio(main, [(8, 16, 0, 16)])
    stage_limit(main, [(8, 16, 0, 16)])

    def emit_inner(k, wi, m, val):
        outs[m][k, 4:12, :] = val[4:12]

    stage_diffuse(main, [(8, 16, 4, 12)], emit_inner)

    @pl.when(at_south)
    def _():
        row_in[1] = jnp.zeros(row_in.shape[1:], jnp.float32)

    @pl.when(jnp.logical_not(at_south))
    def _():
        north_sends[0].wait_recv()

    @pl.when(jnp.logical_not(at_north))
    def _():
        south_sends[0].wait_recv()

    @pl.when(at_north)
    def _():
        fold_sends[0].wait_recv()

    for slot, row in ((1, 4), (0, 24)):
        for g, (a, b) in enumerate(fields):
            for k in range(nk):
                a[k, row : row + 4, :] = row_in[slot, g * nk + k, 0:4, :]
                b[k, row : row + 4, :] = row_in[slot, g * nk + k, 4:8, :]
        floor[row : row + 4, :] = row_in[slot, 2 * nk, 0:4, :]

    stage_flux(main, [(4, 8, 1, 5), (20, 8, 3, 7)])
    stage_ratio(main, [(4, 8, 2, 6), (20, 8, 2, 6)])
    stage_limit(main, [(4, 8, 3, 7), (20, 8, 1, 5)])

    def emit_outer(k, wi, m, val):
        if wi == 0:
            outs[m][k, 0:4, :] = val[4:8]
        else:
            outs[m][k, 12:16, :] = val[4:8]

    stage_diffuse(main, [(4, 8, 4, 8), (16, 8, 4, 8)], emit_outer)

    @pl.when(at_south)
    def _():
        corner_in[corner[SE]] = jnp.zeros(corner_in.shape[1:], jnp.float32)
        corner_in[corner[SW]] = jnp.zeros(corner_in.shape[1:], jnp.float32)

    @pl.when(jnp.logical_not(at_south))
    def _():
        for copy in north_sends[1:]:
            copy.wait_recv()
        for copy in south_sends:
            copy.wait_send()

    @pl.when(jnp.logical_not(at_north))
    def _():
        for copy in south_sends[1:]:
            copy.wait_recv()
        for copy in north_sends:
            copy.wait_send()

    @pl.when(at_north)
    def _():
        fold_sends[0].wait_send()
        for copy, local, own in ((fold_sends[1], ne_local, ne_self), (fold_sends[2], nw_local, nw_self)):
            @pl.when(own)
            def _():
                local.wait()

            @pl.when(jnp.logical_not(own))
            def _():
                copy.wait()

    for copy in side_sends:
        copy.wait()

    strip_tile(0)
    strip_tile(24)
    from_east = lax.rem(lane8, 8) >= 4
    for row, east_ref, west_ref, at in (
        (0, corner_in.at[corner[SE]], corner_in.at[corner[SW]], 0),
        (8, strip_in.at[0], strip_in.at[1], 0),
        (16, strip_in.at[0], strip_in.at[1], 8),
        (24, corner_in.at[corner[NE]], corner_in.at[corner[NW]], 0),
    ):
        rows = slice(row, row + 8)
        for k in range(half + 1):
            x = jnp.where(from_east, east_ref[k, at : at + 8, :], west_ref[k, at : at + 8, :])
            if k == half:
                e_floor[rows, :] = jnp.where(q_t, x, e_floor[rows, :])
                continue
            e_tr[k, rows, :] = jnp.where(q_t, x, e_tr[k, rows, :])
            e_u[k, rows, :] = jnp.where(q_t, pltpu.roll(x, 120, 1), e_u[k, rows, :])
            e_v[k, rows, :] = jnp.where(q_t, pltpu.roll(x, 112, 1), e_v[k, rows, :])

    def strip_density(one):
        x = one[0]
        low_half = lane_iota(x.shape[0]) < 64
        own = jnp.where(low_half, -thermal_coef, haline_coef)
        other = jnp.where(low_half, haline_coef, -thermal_coef)
        return own * x + other * pltpu.roll(x, 64, 1)

    strips = dict(split=True, t=[e_tr], u=e_u, v=e_v, f=e_floor, density=strip_density)
    names = dict(low=e_low, mx=e_mx, mn=e_mn, ax=e_ax, ay=e_ay, az=e_az, rin=e_rin, rout=e_rout, adv=e_adv)
    strips.update({name: [ref] for name, ref in names.items()})
    stage_flux(strips, [(4, 24, 0, 24)])
    stage_ratio(strips, [(4, 24, 0, 24)])
    stage_limit(strips, [(4, 24, 0, 24)])

    def emit_strip(k, wi, m, val, add=False):
        e_res[k] = e_res[k] + val[4:20] if add else val[4:20]

    stage_diffuse(strips, [(4, 24, 4, 20)], emit_strip)


def finish(t_ref, s_ref, e_res, t_hbm, s_hbm, t_buf, s_buf, sem):
    lane16 = lane_iota(16)
    rim = jnp.logical_or(lane16 < 4, lane16 >= 124)
    copies = []
    for m, (ref, buf, out) in enumerate(((t_ref, t_buf, t_hbm), (s_ref, s_buf, s_hbm))):
        back = jnp.where(lane16 < 4, lane16 + 20, jnp.where(lane16 >= 124, lane16 - 116, 0)) + 64 * m
        half = e_res.shape[0]
        for k in range(ref.shape[0]):
            edge = jnp.take_along_axis(e_res[k % half], back + 32 * (k // half), axis=1)
            buf[k] = jnp.where(rim, edge, ref[k])
        copies.append(pltpu.make_async_copy(buf, out, sem.at[m]))
        copies[-1].start()
    for copy in copies:
        copy.wait()


def on_device(t, s, u, v, flag, point, count):
    nk = t.shape[0]
    f32 = jnp.float32
    vm = lambda *shape: pltpu.VMEM(shape, f32)
    big = lambda: vm(2, nk, 32, 128)
    one = lambda: vm(nk, 32, 128)
    whole = pl.BlockSpec(memory_space=pltpu.VMEM)
    hbm = pl.BlockSpec(memory_space=pltpu.HBM)
    part = pltpu.VMEM(t.shape, f32)
    main_t, main_s, strips = pl.pallas_call(
        kernel,
        out_shape=(part, part, pltpu.VMEM((nk // 2, *t.shape[1:]), f32)),
        in_specs=[hbm] * 7,
        out_specs=(whole, whole, whole),
        scratch_shapes=[
            pltpu.VMEM(flag.shape, flag.dtype), pltpu.VMEM(point.shape, point.dtype), pltpu.VMEM(count.shape, count.dtype),
            big(), one(), one(), vm(32, 128),
            *[big() for _ in range(9)],
            *[vm(nk // 2, 32, 128) for _ in range(3)], vm(32, 128),
            *[vm(nk // 2, 32, 128) for _ in range(9)],
            vm(2, 2 * nk + 1, 8, 128), vm(2, 2 * nk + 1, 8, 128),
            vm(nk // 2 + 1, 16, 128), vm(nk // 2 + 1, 8, 128),
            vm(2, nk // 2 + 1, 16, 128), vm(4, nk // 2 + 1, 8, 128),
            pltpu.SemaphoreType.DMA((7,)), pltpu.SemaphoreType.DMA((8,)), pltpu.SemaphoreType.DMA((8,)),
        ],
        compiler_params=pltpu.CompilerParams(
            collective_id=0, has_side_effects=True, vmem_limit_bytes=60 * 1024 * 1024
        ),
    )(t, s, u, v, flag, point, count)
    result = jax.ShapeDtypeStruct(t.shape, f32)
    return pl.pallas_call(
        finish,
        out_shape=(result, result),
        in_specs=[whole] * 3,
        out_specs=(hbm, hbm),
        scratch_shapes=[vm(*t.shape), vm(*t.shape), pltpu.SemaphoreType.DMA((2,))],
        compiler_params=pltpu.CompilerParams(vmem_limit_bytes=4 * 1024 * 1024),
    )(main_t, main_s, strips)


def solution(mesh):
    grid = P(None, "lat", "lon")
    flat = P("lat", "lon")
    return jax.shard_map(
        on_device, mesh=mesh, in_specs=(grid,) * 4 + (flat,) * 3, out_specs=(grid, grid), check_vma=False
    )
```

```python
import functools

import jax
import jax.numpy as jnp
from jax import lax
from jax.experimental import pallas as pl
from jax.experimental.pallas import tpu as pltpu
from jax.sharding import PartitionSpec as P

time_step = 0.5
diffusivity = 0.1
strat_floor = 0.5
slope_limit = 2.0
thermal_coef = 0.2
haline_coef = 0.8

MESH = pl.DeviceIdType.MESH
INF = float("inf")
TINY = 1e-37
FACE_SCALE = 0.25 * time_step
DIFF_SCALE = 0.25 * time_step * diffusivity

EAST, WEST, NORTH, SOUTH, CORNER_NORTH, CORNER_SOUTH = range(6)


def east_of(x):
    return pltpu.roll(x, x.shape[1] - 1, 1)


def west_of(x):
    return pltpu.roll(x, 1, 1)


def south_of(x):
    return pltpu.roll(x, 1, 0)


def lane_iota(rows):
    return lax.broadcasted_iota(jnp.int32, (rows, 128), 1)


def upper_lanes(rows):
    return lax.rem(lane_iota(rows), 64) < 32


def to_upper(x):
    return jnp.where(upper_lanes(x.shape[0]), pltpu.roll(x, 96, 1), 0.0)


def to_lower(x):
    return jnp.where(upper_lanes(x.shape[0]), 0.0, pltpu.roll(x, 32, 1))


def above(z, ref, k, r0, n):
    if not z["split"]:
        return ref[jnp.maximum(k - 1, 0), r0 : r0 + n, :]
    if k > 0:
        return ref[k - 1, r0 : r0 + n, :]
    last = z["u"].shape[0] - 1
    return jnp.where(upper_lanes(n), ref[0, r0 : r0 + n, :], pltpu.roll(ref[last, r0 : r0 + n, :], 32, 1))


def below(z, ref, k, r0, n):
    last = z["u"].shape[0] - 1
    if not z["split"]:
        return ref[jnp.minimum(k + 1, last), r0 : r0 + n, :]
    if k < last:
        return ref[k + 1, r0 : r0 + n, :]
    return jnp.where(upper_lanes(n), pltpu.roll(ref[0, r0 : r0 + n, :], 96, 1), ref[last, r0 : r0 + n, :])


def upward(z, body, carry, unroll):
    nk = z["u"].shape[0]
    if z["split"]:
        for k in range(nk - 1, -1, -1):
            carry = body(k, jnp.float32(k), carry)
        return carry

    def step(i, carry):
        k = nk - 1 - i
        return body(k, k.astype(jnp.float32), carry)

    return lax.fori_loop(0, nk, step, carry, unroll=unroll)


def nothing(z, wins):
    return tuple(tuple(jnp.zeros((n, 128), jnp.float32) for _ in z["t"]) for _, n, _, _ in wins)


def stage_flux(z, wins):
    nk = z["u"].shape[0]
    stat = []
    for r0, n, _, _ in wins:
        f = z["f"][r0 : r0 + n, :]
        f_e = jnp.minimum(f, east_of(f))
        f_n = jnp.minimum(f, z["f"][r0 + 1 : r0 + 1 + n, :])
        stat.append((f, f_e, f_n))

    def velocities(k, kk, r0, n, f_e, f_n):
        u = z["u"][k, r0 : r0 + n, :]
        u_e = jnp.where(kk < f_e, FACE_SCALE * (u + east_of(u)), 0.0)
        v = z["v"][k, r0 : r0 + n, :]
        v_n = jnp.where(kk < f_n, FACE_SCALE * (v + z["v"][k, r0 + 1 : r0 + 1 + n, :]), 0.0)
        return u_e, v_n, u_e - west_of(u_e) + v_n - south_of(v_n)

    def body(k, kk, carry):
        out = []
        for (r0, n, lo, hi), (f, f_e, f_n), (w_old, bottoms) in zip(wins, stat, carry):
            u_e, v_n, gain = velocities(k, kk, r0, n, f_e, f_n)
            w = w_old - gain
            abs_u, abs_v, abs_w = jnp.abs(u_e), jnp.abs(v_n), jnp.abs(w)
            wet = kk < f
            tops = []
            for m, t in enumerate(z["t"]):
                c = t[k, r0 : r0 + n, :]
                e = east_of(c)
                nn = t[k, r0 + 1 : r0 + 1 + n, :]
                up = above(z, t, k, r0, n)
                a_e = abs_u * (e - c)
                l_e = u_e * (c + e) - a_e
                a_n = abs_v * (nn - c)
                l_n = v_n * (c + nn) - a_n
                a_t = abs_w * (up - c)
                l_t = w * (c + up) - a_t
                low = c - ((l_e - west_of(l_e)) + (l_n - south_of(l_n)) + (l_t - bottoms[m]))
                low = jnp.where(wet, low, 0.0)
                big = jnp.where(wet, jnp.maximum(c, low), -INF)
                small = jnp.where(wet, jnp.minimum(c, low), INF)
                for name, val in (("ax", a_e), ("ay", a_n), ("az", a_t), ("low", low), ("mx", big), ("mn", small)):
                    z[name][m][k, r0 + lo : r0 + hi, :] = val[lo:hi]
                tops.append(l_t)
            out.append((w, tuple(tops)))
        return tuple(out)

    start = []
    for (r0, n, _, _), (f, f_e, f_n) in zip(wins, stat):
        w = jnp.zeros((n, 128), jnp.float32)
        flows = tuple(w for _ in z["t"])
        if z["split"]:
            for k in range(nk):
                w = w - velocities(k, jnp.float32(k), r0, n, f_e, f_n)[2]
            w = to_upper(w)
            flows = []
            for t in z["t"]:
                up, c = t[nk - 1, r0 : r0 + n, :], below(z, t, nk - 1, r0, n)
                flows.append(w * (c + up) - jnp.abs(w) * (up - c))
        start.append((w, tuple(flows)))
    upward(z, body, tuple(start), nk)


def stage_ratio(z, wins):
    nk = z["u"].shape[0]

    def body(k, kk, carry):
        out = []
        for (r0, n, lo, hi), bottoms in zip(wins, carry):
            tops = []
            for m in range(len(z["t"])):
                def near(ref, pick):
                    c = ref[k, r0 : r0 + n, :]
                    horizontal = pick(pick(east_of(c), west_of(c)), pick(ref[k, r0 + 1 : r0 + 1 + n, :], ref[k, r0 - 1 : r0 - 1 + n, :]))
                    return pick(pick(c, horizontal), pick(above(z, ref, k, r0, n), below(z, ref, k, r0, n)))

                big, small = near(z["mx"][m], jnp.maximum), near(z["mn"][m], jnp.minimum)
                low = z["low"][m][k, r0 : r0 + n, :]
                a_e = z["ax"][m][k, r0 : r0 + n, :]
                a_w = west_of(a_e)
                a_n = z["ay"][m][k, r0 : r0 + n, :]
                a_s = z["ay"][m][k, r0 - 1 : r0 - 1 + n, :]
                a_t, a_b = z["az"][m][k, r0 : r0 + n, :], bottoms[m]
                p_in, p_out = 0.0, 0.0
                for inward, outward in ((a_w, a_e), (a_s, a_n), (a_b, a_t)):
                    p_in = p_in + (jnp.maximum(inward, 0.0) - jnp.minimum(outward, 0.0))
                    p_out = p_out + (jnp.maximum(outward, 0.0) - jnp.minimum(inward, 0.0))
                r_in = jnp.clip((big - low) * pl.reciprocal(jnp.maximum(p_in, TINY)), 0.0, 1.0)
                r_out = jnp.clip((low - small) * pl.reciprocal(jnp.maximum(p_out, TINY)), 0.0, 1.0)
                z["rin"][m][k, r0 + lo : r0 + hi, :] = r_in[lo:hi]
                z["rout"][m][k, r0 + lo : r0 + hi, :] = r_out[lo:hi]
                tops.append(a_t)
            out.append(tuple(tops))
        return tuple(out)

    start = nothing(z, wins)
    if z["split"]:
        start = tuple(tuple(to_upper(a[0, r0 : r0 + n, :]) for a in z["az"]) for r0, n, _, _ in wins)
    upward(z, body, start, nk)


def limited(anti, r_in, r_out, far_in, far_out):
    return anti * jnp.where(anti >= 0, jnp.minimum(far_in, r_out), jnp.minimum(r_in, far_out))


def stage_limit(z, wins):
    nk = z["u"].shape[0]
    stat = [z["f"][r0 : r0 + n, :] for r0, n, _, _ in wins]

    def rise(m, k, r0, n):
        r_in, r_out = z["rin"][m][k, r0 : r0 + n, :], z["rout"][m][k, r0 : r0 + n, :]
        far_in, far_out = above(z, z["rin"][m], k, r0, n), above(z, z["rout"][m], k, r0, n)
        return limited(z["az"][m][k, r0 : r0 + n, :], r_in, r_out, far_in, far_out)

    def body(k, kk, carry):
        out = []
        for (r0, n, lo, hi), f, bottoms in zip(wins, stat, carry):
            tops = []
            for m in range(len(z["t"])):
                r_in, r_out = z["rin"][m][k, r0 : r0 + n, :], z["rout"][m][k, r0 : r0 + n, :]
                f_e = limited(z["ax"][m][k, r0 : r0 + n, :], r_in, r_out, east_of(r_in), east_of(r_out))
                f_n = limited(
                    z["ay"][m][k, r0 : r0 + n, :], r_in, r_out,
                    z["rin"][m][k, r0 + 1 : r0 + 1 + n, :], z["rout"][m][k, r0 + 1 : r0 + 1 + n, :],
                )
                f_t = rise(m, k, r0, n)
                low = z["low"][m][k, r0 : r0 + n, :]
                new = low - ((f_e - west_of(f_e)) + (f_n - south_of(f_n)) + (f_t - bottoms[m]))
                new = jnp.where(kk < f, new, 0.0)
                z["adv"][m][k, r0 + lo : r0 + hi, :] = new[lo:hi]
                tops.append(f_t)
            out.append(tuple(tops))
        return tuple(out)

    start = nothing(z, wins)
    if z["split"]:
        start = tuple(tuple(to_upper(rise(m, 0, r0, n)) for m in range(len(z["t"]))) for r0, n, _, _ in wins)
    upward(z, body, start, nk)


def clip_slope(x):
    return jnp.clip(x, -slope_limit, slope_limit)


def stage_diffuse(z, wins, emit):
    nk = z["u"].shape[0]
    dens = z["density"]
    nt = len(z["t"])
    stat = []
    for r0, n, _, _ in wins:
        f = z["f"][r0 : r0 + n, :]
        far_e, far_n = east_of(f), z["f"][r0 + 1 : r0 + 1 + n, :]
        stat.append((f, far_e, far_n, jnp.minimum(f, far_e), jnp.minimum(f, far_n)))

    def inverse(grads):
        return pl.reciprocal(jnp.maximum(-dens(grads), strat_floor))

    def vertical(k, kk, r0, n, f, far_n):
        gz = [jnp.where(kk < f, above(z, a, k, r0, n) - a[k, r0 : r0 + n, :], 0.0) for a in z["adv"]]
        gz_n = [jnp.where(kk < far_n, above(z, a, k, r0 + 1, n) - a[k, r0 + 1 : r0 + 1 + n, :], 0.0) for a in z["adv"]]
        inv = inverse(gz)
        return inv, east_of(inv), inverse(gz_n), tuple(gz), tuple(east_of(g) for g in gz), tuple(gz_n)

    def body(k, kk, carry):
        out = []
        for wi, ((r0, n, _, _), (f, far_e, far_n, f_e, f_n), old) in enumerate(zip(wins, stat, carry)):
            if not z["split"]:
                not_top = (k >= 1).astype(jnp.float32)
            elif k == 0:
                not_top = jnp.where(upper_lanes(n), 0.0, 1.0)
            here = [a[k, r0 : r0 + n, :] for a in z["adv"]]
            north = [a[k, r0 + 1 : r0 + 1 + n, :] for a in z["adv"]]
            inv, inv_e, inv_n, gz, gz_e, gz_n = vertical(k, kk, r0, n, f, far_n)
            gx = [jnp.where(kk < f_e, east_of(c) - c, 0.0) for c in here]
            gy = [jnp.where(kk < f_n, b - c, 0.0) for b, c in zip(north, here)]
            rx, ry = dens(gx), dens(gy)
            (o_inv, o_inv_e, o_inv_n, o_gz, o_gz_e, o_gz_n), o_part, o_top = old
            low_here, low_e, low_n = kk + 1.0 < f, kk + 1.0 < far_e, kk + 1.0 < far_n
            s_x = [clip_slope(rx * q) for q in (inv, inv_e, o_inv, o_inv_e)]
            s_y = [clip_slope(ry * q) for q in (inv, inv_n, o_inv, o_inv_n)]
            parts, tops = [], []
            for m in range(nt):
                gx_top, gy_top = gx[m], gy[m]
                if not z["split"] or k == 0:
                    gx_top, gy_top = gx_top * not_top, gy_top * not_top
                hx = (
                    gx_top + s_x[0] * gz[m],
                    gx_top + s_x[1] * gz_e[m],
                    jnp.where(low_here, gx[m], 0.0) + s_x[2] * o_gz[m],
                    jnp.where(low_e, gx[m], 0.0) + s_x[3] * o_gz_e[m],
                )
                hy = (
                    gy_top + s_y[0] * gz[m],
                    gy_top + s_y[1] * gz_n[m],
                    jnp.where(low_here, gy[m], 0.0) + s_y[2] * o_gz[m],
                    jnp.where(low_n, gy[m], 0.0) + s_y[3] * o_gz_n[m],
                )
                flux_e = (hx[0] + hx[1]) + (hx[2] + hx[3])
                flux_n = (hy[0] + hy[1]) + (hy[2] + hy[3])
                top = (s_x[0] * hx[0] + west_of(s_x[1] * hx[1])) + (s_y[0] * hy[0] + south_of(s_y[1] * hy[1]))
                bottom = (s_x[2] * hx[2] + west_of(s_x[3] * hx[3])) + (s_y[2] * hy[2] + south_of(s_y[3] * hy[3]))
                rise = o_top[m] + bottom
                if z["split"] and k == nk - 1:
                    bottom_lower[wi, m] = to_lower(bottom)
                else:
                    done = jnp.where(kk + 1.0 < f, o_part[m] + DIFF_SCALE * rise, 0.0)
                    emit(k + 1 if z["split"] else jnp.minimum(k + 1, nk - 1), wi, m, done)
                parts.append(here[m] + DIFF_SCALE * ((flux_e - west_of(flux_e)) + (flux_n - south_of(flux_n)) - rise))
                tops.append(top)
            out.append(((inv, inv_e, inv_n, gz, gz_e, gz_n), tuple(parts), tuple(tops)))
        return tuple(out)

    bottom_lower = {}
    start = []
    for (r0, n, _, _), (f, _, far_n, *_) in zip(wins, stat):
        x = jnp.zeros((n, 128), jnp.float32)
        xs = tuple(x for _ in range(nt))
        first = (x, x, x, xs, xs, xs)
        if z["split"]:
            first = jax.tree.map(to_upper, vertical(0, jnp.float32(0), r0, n, f, far_n))
        start.append((first, xs, xs))
    last = upward(z, body, tuple(start), nk // 2)
    for wi, ((r0, n, _, _), (f, *_), (_, parts, tops)) in enumerate(zip(wins, stat, last)):
        for m in range(nt):
            top = tops[m]
            if z["split"]:
                top = top + bottom_lower[wi, m]
                late = jnp.where(nk - 1.0 < f, -DIFF_SCALE * to_upper(tops[m]), 0.0)
                emit(nk - 1, wi, m, late, True)
            emit(0, wi, m, jnp.where(0.0 < f, parts[m] + DIFF_SCALE * top, 0.0))


def kernel(
    t_hbm, s_hbm, u_hbm, v_hbm, flag_hbm, point_hbm, count_hbm,
    t_out, s_out, e_res,
    flag_ref, point_ref, count_ref, tr, u, v, floor, low, mx, mn, ax, ay, az, rin, rout, adv,
    e_tr, e_u, e_v, e_floor, e_low, e_mx, e_mn, e_ax, e_ay, e_az, e_rin, e_rout, e_adv,
    row_out, row_in, strip_out, strip_in, side, fold_out, corner_in,
    load_sem, send_sem, recv_sem,
):
    n_lon, n_lat = lax.axis_size("lon"), lax.axis_size("lat")
    lon, lat = lax.axis_index("lon"), lax.axis_index("lat")
    nk = u.shape[0]
    half = nk // 2
    east, west = lax.rem(lon + 1, n_lon), lax.rem(lon + n_lon - 1, n_lon)
    at_north, at_south = lat == n_lat - 1, lat == 0
    to_east, to_west = (east, lat), (west, lat)
    to_north, to_south, to_fold = (lon, lat + 1), (lon, lat - 1), (n_lon - 1 - lon, lat)

    barrier = pltpu.get_barrier_semaphore()

    def greet(where):
        pl.semaphore_signal(barrier, inc=1, device_id=where, device_id_type=MESH)

    greet(to_east)
    greet(to_west)

    @pl.when(jnp.logical_not(at_south))
    def _():
        greet(to_south)

    @pl.when(jnp.logical_not(at_north))
    def _():
        greet(to_north)

    @pl.when(at_north)
    def _():
        greet(to_fold)

    loads = [
        pltpu.make_async_copy(src, dst.at[:, 8:24, :], load_sem.at[i])
        for i, (src, dst) in enumerate(((t_hbm, tr.at[0]), (s_hbm, tr.at[1]), (u_hbm, u), (v_hbm, v)))
    ]
    loads += [
        pltpu.make_async_copy(src, dst, load_sem.at[4 + i])
        for i, (src, dst) in enumerate(((flag_hbm, flag_ref), (point_hbm, point_ref), (count_hbm, count_ref)))
    ]
    for copy in loads:
        copy.start()
    for copy in loads:
        copy.wait()
    floor[8:24, :] = (count_ref[...] * point_ref[...] * flag_ref[...]).astype(jnp.float32)

    fields = ((tr.at[0], tr.at[1]), (u, v))
    for g, (a, b) in enumerate(fields):
        for k in range(nk):
            row_out[1, g * nk + k, 0:4, :] = a[k, 8:12, :]
            row_out[1, g * nk + k, 4:8, :] = b[k, 8:12, :]
    row_out[1, 2 * nk, 0:4, :] = floor[8:12, :]

    @pl.when(jnp.logical_not(at_north))
    def _():
        for g, (a, b) in enumerate(fields):
            for k in range(nk):
                row_out[0, g * nk + k, 0:4, :] = a[k, 20:24, :]
                row_out[0, g * nk + k, 4:8, :] = b[k, 20:24, :]
        row_out[0, 2 * nk, 0:4, :] = floor[20:24, :]

    lane8, sub8 = lane_iota(8), lax.broadcasted_iota(jnp.int32, (8, 128), 0)

    @pl.when(at_north)
    def _():
        def turned(x):
            x = jnp.take_along_axis(x, 127 - lane8, axis=1)
            return jnp.take_along_axis(x, 7 - sub8, axis=0)

        for g, (a, b) in enumerate(fields):
            sign = 1.0 if g == 0 else -1.0
            for k in range(nk):
                row_out[0, g * nk + k, 0:4, :] = sign * turned(a[k, 16:24, :])[0:4]
                row_out[0, g * nk + k, 4:8, :] = sign * turned(b[k, 16:24, :])[0:4]
        row_out[0, 2 * nk, 0:4, :] = turned(floor[16:24, :])[0:4]

    p = lax.rem(lane8, 32)
    shift = jnp.where(p < 12, 116, jnp.where(p < 16, -12, jnp.where(p < 20, 108, -20)))
    strip_idx = lax.rem(p + shift + 128, 128)
    first, upper = lane8 < 64, upper_lanes(8)

    def strip_tile(row):
        rows = slice(row, row + 8)

        def gather(x):
            return jnp.take_along_axis(x, strip_idx, axis=1)

        def halves(ref, k):
            return jnp.where(upper, gather(ref[k, rows, :]), gather(ref[k + half, rows, :]))

        for k in range(half):
            e_tr[k, rows, :] = jnp.where(first, halves(tr.at[0], k), halves(tr.at[1], k))
            e_u[k, rows, :] = halves(u, k)
            e_v[k, rows, :] = halves(v, k)
        e_floor[rows, :] = gather(floor[rows, :]) - jnp.where(upper, 0.0, float(half))

    q_t = jnp.logical_and(p >= 12, p < 20)
    q_u = jnp.logical_and(p >= 20, p < 28)
    for row in (8, 16):
        strip_tile(row)
        rows = slice(row, row + 8)
        for k in range(half):
            strip_out[k, row - 8 : row, :] = jnp.where(
                q_t, e_tr[k, rows, :],
                jnp.where(q_u, pltpu.roll(e_u[k, rows, :], 8, 1), pltpu.roll(e_v[k, rows, :], 16, 1)),
            )
        strip_out[half, row - 8 : row, :] = e_floor[rows, :]

    pl.semaphore_wait(barrier, jnp.where(at_south, 3, 4))

    def send(src, dst, role, slot, where):
        return pltpu.make_async_remote_copy(
            src_ref=src, dst_ref=dst, send_sem=send_sem.at[role], recv_sem=recv_sem.at[slot],
            device_id=where, device_id_type=MESH,
        )

    rows_north = send(row_out.at[0], row_in.at[1], NORTH, SOUTH, to_north)
    rows_fold = send(row_out.at[0], row_in.at[0], NORTH, NORTH, to_fold)
    rows_south = send(row_out.at[1], row_in.at[0], SOUTH, NORTH, to_south)
    strip_west = send(strip_out, strip_in.at[0], WEST, EAST, to_west)
    strip_east = send(strip_out, strip_in.at[1], EAST, WEST, to_east)
    corner_north = send(side.at[:, 8:16, :], corner_in.at[1], CORNER_NORTH, CORNER_SOUTH, to_north)
    corner_fold = send(fold_out, corner_in.at[0], CORNER_NORTH, CORNER_NORTH, to_fold)
    corner_south = send(side.at[:, 0:8, :], corner_in.at[0], CORNER_SOUTH, CORNER_NORTH, to_south)

    strip_west.start()
    strip_east.start()

    @pl.when(jnp.logical_not(at_south))
    def _():
        rows_south.start()

    @pl.when(jnp.logical_not(at_north))
    def _():
        rows_north.start()

    @pl.when(at_north)
    def _():
        rows_fold.start()

    main = dict(
        split=False, t=[tr.at[0], tr.at[1]], u=u, v=v, f=floor,
        density=lambda pair: haline_coef * pair[1] - thermal_coef * pair[0],
    )
    names = dict(low=low, mx=mx, mn=mn, ax=ax, ay=ay, az=az, rin=rin, rout=rout, adv=adv)
    main.update({name: [ref.at[0], ref.at[1]] for name, ref in names.items()})

    outs = (t_out, s_out)

    stage_flux(main, [(8, 16, 0, 16)])
    stage_ratio(main, [(8, 16, 0, 16)])
    stage_limit(main, [(8, 16, 0, 16)])

    def emit_inner(k, wi, m, val):
        outs[m][k, 4:12, :] = val[4:12]

    stage_diffuse(main, [(8, 16, 4, 12)], emit_inner)

    strip_west.wait()
    strip_east.wait()
    from_east = lax.rem(lane8, 8) >= 4
    for k in range(half + 1):
        for at in (0, 8):
            rows = slice(at, at + 8)
            side[k, rows, :] = jnp.where(from_east, strip_in[0, k, rows, :], strip_in[1, k, rows, :])

    @pl.when(jnp.logical_not(at_south))
    def _():
        corner_south.start()

    @pl.when(jnp.logical_not(at_north))
    def _():
        corner_north.start()

    @pl.when(at_north)
    def _():
        group_idx = lax.rem(lane8 + 7 - 2 * lax.rem(lane8 + 4, 8) + 128, 128)
        sign = jnp.where(q_t, 1.0, -1.0)
        for k in range(half + 1):
            x = jnp.take_along_axis(side[k, 8:16, :], group_idx, axis=1)
            x = jnp.take_along_axis(x, 7 - sub8, axis=0)
            fold_out[k] = x if k == half else x * sign
        corner_fold.start()

    def strip_halo(row, ref, at):
        rows = slice(row, row + 8)
        for k in range(half + 1):
            x = ref[k, at : at + 8, :]
            if k == half:
                e_floor[rows, :] = jnp.where(q_t, x, e_floor[rows, :])
                continue
            e_tr[k, rows, :] = jnp.where(q_t, x, e_tr[k, rows, :])
            e_u[k, rows, :] = jnp.where(q_t, pltpu.roll(x, 120, 1), e_u[k, rows, :])
            e_v[k, rows, :] = jnp.where(q_t, pltpu.roll(x, 112, 1), e_v[k, rows, :])

    strip_halo(8, side, 0)
    strip_halo(16, side, 8)

    @pl.when(at_south)
    def _():
        row_in[1] = jnp.zeros(row_in.shape[1:], jnp.float32)
        corner_in[1] = jnp.zeros(corner_in.shape[1:], jnp.float32)

    @pl.when(jnp.logical_not(at_south))
    def _():
        rows_south.wait_send()
        rows_north.wait_recv()

    @pl.when(jnp.logical_not(at_north))
    def _():
        rows_north.wait_send()
        rows_south.wait_recv()

    @pl.when(at_north)
    def _():
        rows_fold.wait()

    for slot, row in ((1, 4), (0, 24)):
        for g, (a, b) in enumerate(fields):
            for k in range(nk):
                a[k, row : row + 4, :] = row_in[slot, g * nk + k, 0:4, :]
                b[k, row : row + 4, :] = row_in[slot, g * nk + k, 4:8, :]
        floor[row : row + 4, :] = row_in[slot, 2 * nk, 0:4, :]

    stage_flux(main, [(4, 8, 1, 5), (20, 8, 3, 7)])
    stage_ratio(main, [(4, 8, 2, 6), (20, 8, 2, 6)])
    stage_limit(main, [(4, 8, 3, 7), (20, 8, 1, 5)])

    def emit_outer(k, wi, m, val):
        if wi == 0:
            outs[m][k, 0:4, :] = val[4:8]
        else:
            outs[m][k, 12:16, :] = val[4:8]

    stage_diffuse(main, [(4, 8, 4, 8), (16, 8, 4, 8)], emit_outer)

    strip_tile(0)
    strip_tile(24)

    @pl.when(jnp.logical_not(at_south))
    def _():
        corner_south.wait_send()
        corner_north.wait_recv()

    @pl.when(jnp.logical_not(at_north))
    def _():
        corner_north.wait_send()
        corner_south.wait_recv()

    @pl.when(at_north)
    def _():
        corner_fold.wait()

    strip_halo(0, corner_in.at[1], 0)
    strip_halo(24, corner_in.at[0], 0)

    def strip_density(one):
        x = one[0]
        low_half = lane_iota(x.shape[0]) < 64
        own = jnp.where(low_half, -thermal_coef, haline_coef)
        other = jnp.where(low_half, haline_coef, -thermal_coef)
        return own * x + other * pltpu.roll(x, 64, 1)

    strips = dict(split=True, t=[e_tr], u=e_u, v=e_v, f=e_floor, density=strip_density)
    names = dict(low=e_low, mx=e_mx, mn=e_mn, ax=e_ax, ay=e_ay, az=e_az, rin=e_rin, rout=e_rout, adv=e_adv)
    strips.update({name: [ref] for name, ref in names.items()})
    stage_flux(strips, [(4, 24, 0, 24)])
    stage_ratio(strips, [(4, 24, 0, 24)])
    stage_limit(strips, [(4, 24, 0, 24)])

    def emit_strip(k, wi, m, val, add=False):
        e_res[k] = e_res[k] + val[4:20] if add else val[4:20]

    stage_diffuse(strips, [(4, 24, 4, 20)], emit_strip)


def finish(t_ref, s_ref, e_res, t_hbm, s_hbm, t_buf, s_buf, sem):
    lane16 = lane_iota(16)
    rim = jnp.logical_or(lane16 < 4, lane16 >= 124)
    copies = []
    for m, (ref, buf, out) in enumerate(((t_ref, t_buf, t_hbm), (s_ref, s_buf, s_hbm))):
        back = jnp.where(lane16 < 4, lane16 + 20, jnp.where(lane16 >= 124, lane16 - 116, 0)) + 64 * m
        half = e_res.shape[0]
        for k in range(ref.shape[0]):
            edge = jnp.take_along_axis(e_res[k % half], back + 32 * (k // half), axis=1)
            buf[k] = jnp.where(rim, edge, ref[k])
        copies.append(pltpu.make_async_copy(buf, out, sem.at[m]))
        copies[-1].start()
    for copy in copies:
        copy.wait()


def on_device(t, s, u, v, flag, point, count):
    nk = t.shape[0]
    f32 = jnp.float32
    vm = lambda *shape: pltpu.VMEM(shape, f32)
    big = lambda: vm(2, nk, 32, 128)
    one = lambda: vm(nk, 32, 128)
    whole = pl.BlockSpec(memory_space=pltpu.VMEM)
    hbm = pl.BlockSpec(memory_space=pltpu.HBM)
    part = pltpu.VMEM(t.shape, f32)
    main_t, main_s, strips = pl.pallas_call(
        kernel,
        out_shape=(part, part, pltpu.VMEM((nk // 2, *t.shape[1:]), f32)),
        in_specs=[hbm] * 7,
        out_specs=(whole, whole, whole),
        scratch_shapes=[
            pltpu.VMEM(flag.shape, flag.dtype), pltpu.VMEM(point.shape, point.dtype), pltpu.VMEM(count.shape, count.dtype),
            big(), one(), one(), vm(32, 128),
            *[big() for _ in range(9)],
            *[vm(nk // 2, 32, 128) for _ in range(3)], vm(32, 128),
            *[vm(nk // 2, 32, 128) for _ in range(9)],
            vm(2, 2 * nk + 1, 8, 128), vm(2, 2 * nk + 1, 8, 128),
            vm(nk // 2 + 1, 16, 128), vm(2, nk // 2 + 1, 16, 128), vm(nk // 2 + 1, 16, 128),
            vm(nk // 2 + 1, 8, 128), vm(2, nk // 2 + 1, 8, 128),
            pltpu.SemaphoreType.DMA((7,)), pltpu.SemaphoreType.DMA((6,)), pltpu.SemaphoreType.DMA((6,)),
        ],
        compiler_params=pltpu.CompilerParams(
            collective_id=0, has_side_effects=True, vmem_limit_bytes=60 * 1024 * 1024
        ),
    )(t, s, u, v, flag, point, count)
    result = jax.ShapeDtypeStruct(t.shape, f32)
    return pl.pallas_call(
        finish,
        out_shape=(result, result),
        in_specs=[whole] * 3,
        out_specs=(hbm, hbm),
        scratch_shapes=[vm(*t.shape), vm(*t.shape), pltpu.SemaphoreType.DMA((2,))],
        compiler_params=pltpu.CompilerParams(vmem_limit_bytes=4 * 1024 * 1024),
    )(main_t, main_s, strips)


def solution(mesh):
    grid = P(None, "lat", "lon")
    flat = P("lat", "lon")
    return jax.shard_map(
        on_device, mesh=mesh, in_specs=(grid,) * 4 + (flat,) * 3, out_specs=(grid, grid), check_vma=False
    )
```

```python
import functools

import jax
import jax.numpy as jnp
from jax import lax
from jax.experimental import pallas as pl
from jax.experimental.pallas import tpu as pltpu
from jax.sharding import PartitionSpec as P

time_step = 0.5
diffusivity = 0.1
strat_floor = 0.5
slope_limit = 2.0
thermal_coef = 0.2
haline_coef = 0.8

MESH = pl.DeviceIdType.MESH
INF = float("inf")
TINY = 1e-37
FACE_SCALE = 0.25 * time_step
DIFF_SCALE = 0.25 * time_step * diffusivity

EAST, WEST, NORTH, SOUTH, NE, NW, SE, SW = range(8)
CORNER = {NE: 0, NW: 1, SE: 2, SW: 3}


def east_of(x):
    return pltpu.roll(x, x.shape[1] - 1, 1)


def west_of(x):
    return pltpu.roll(x, 1, 1)


def south_of(x):
    return pltpu.roll(x, 1, 0)


def lane_iota(rows):
    return lax.broadcasted_iota(jnp.int32, (rows, 128), 1)


def upper_lanes(rows):
    return lax.rem(lane_iota(rows), 64) < 32


def to_upper(x):
    return jnp.where(upper_lanes(x.shape[0]), pltpu.roll(x, 96, 1), 0.0)


def to_lower(x):
    return jnp.where(upper_lanes(x.shape[0]), 0.0, pltpu.roll(x, 32, 1))


def above(z, ref, k, r0, n):
    if not z["split"]:
        return ref[jnp.maximum(k - 1, 0), r0 : r0 + n, :]
    if k > 0:
        return ref[k - 1, r0 : r0 + n, :]
    last = z["u"].shape[0] - 1
    return jnp.where(upper_lanes(n), ref[0, r0 : r0 + n, :], pltpu.roll(ref[last, r0 : r0 + n, :], 32, 1))


def below(z, ref, k, r0, n):
    last = z["u"].shape[0] - 1
    if not z["split"]:
        return ref[jnp.minimum(k + 1, last), r0 : r0 + n, :]
    if k < last:
        return ref[k + 1, r0 : r0 + n, :]
    return jnp.where(upper_lanes(n), pltpu.roll(ref[0, r0 : r0 + n, :], 96, 1), ref[last, r0 : r0 + n, :])


def upward(z, body, carry):
    nk = z["u"].shape[0]
    if z["split"]:
        for k in range(nk - 1, -1, -1):
            carry = body(k, jnp.float32(k), carry)
        return carry

    def step(i, carry):
        k = nk - 1 - i
        return body(k, k.astype(jnp.float32), carry)

    return lax.fori_loop(0, nk, step, carry, unroll=nk // 2)


def nothing(z, wins):
    return tuple(tuple(jnp.zeros((n, 128), jnp.float32) for _ in z["t"]) for _, n, _, _ in wins)


def stage_flux(z, wins):
    nk = z["u"].shape[0]
    stat = []
    for r0, n, _, _ in wins:
        f = z["f"][r0 : r0 + n, :]
        f_e = jnp.minimum(f, east_of(f))
        f_n = jnp.minimum(f, z["f"][r0 + 1 : r0 + 1 + n, :])
        stat.append((f, f_e, f_n))

    def velocities(k, kk, r0, n, f_e, f_n):
        u = z["u"][k, r0 : r0 + n, :]
        u_e = jnp.where(kk < f_e, FACE_SCALE * (u + east_of(u)), 0.0)
        v = z["v"][k, r0 : r0 + n, :]
        v_n = jnp.where(kk < f_n, FACE_SCALE * (v + z["v"][k, r0 + 1 : r0 + 1 + n, :]), 0.0)
        return u_e, v_n, u_e - west_of(u_e) + v_n - south_of(v_n)

    def body(k, kk, carry):
        out = []
        for (r0, n, lo, hi), (f, f_e, f_n), (w_old, bottoms) in zip(wins, stat, carry):
            u_e, v_n, gain = velocities(k, kk, r0, n, f_e, f_n)
            w = w_old - gain
            abs_u, abs_v, abs_w = jnp.abs(u_e), jnp.abs(v_n), jnp.abs(w)
            wet = kk < f
            tops = []
            for m, t in enumerate(z["t"]):
                c = t[k, r0 : r0 + n, :]
                e = east_of(c)
                nn = t[k, r0 + 1 : r0 + 1 + n, :]
                up = above(z, t, k, r0, n)
                a_e = abs_u * (e - c)
                l_e = u_e * (c + e) - a_e
                a_n = abs_v * (nn - c)
                l_n = v_n * (c + nn) - a_n
                a_t = abs_w * (up - c)
                l_t = w * (c + up) - a_t
                low = c - ((l_e - west_of(l_e)) + (l_n - south_of(l_n)) + (l_t - bottoms[m]))
                low = jnp.where(wet, low, 0.0)
                big = jnp.where(wet, jnp.maximum(c, low), -INF)
                small = jnp.where(wet, jnp.minimum(c, low), INF)
                for name, val in (("ax", a_e), ("ay", a_n), ("az", a_t), ("low", low), ("mx", big), ("mn", small)):
                    z[name][m][k, r0 + lo : r0 + hi, :] = val[lo:hi]
                tops.append(l_t)
            out.append((w, tuple(tops)))
        return tuple(out)

    start = []
    for (r0, n, _, _), (f, f_e, f_n) in zip(wins, stat):
        w = jnp.zeros((n, 128), jnp.float32)
        flows = tuple(w for _ in z["t"])
        if z["split"]:
            for k in range(nk):
                w = w - velocities(k, jnp.float32(k), r0, n, f_e, f_n)[2]
            w = to_upper(w)
            flows = []
            for t in z["t"]:
                up, c = t[nk - 1, r0 : r0 + n, :], below(z, t, nk - 1, r0, n)
                flows.append(w * (c + up) - jnp.abs(w) * (up - c))
        start.append((w, tuple(flows)))
    upward(z, body, tuple(start))


def stage_ratio(z, wins):
    nk = z["u"].shape[0]

    def body(k, kk, carry):
        out = []
        for (r0, n, lo, hi), bottoms in zip(wins, carry):
            tops = []
            for m in range(len(z["t"])):
                def near(ref, pick):
                    c = ref[k, r0 : r0 + n, :]
                    horizontal = pick(pick(east_of(c), west_of(c)), pick(ref[k, r0 + 1 : r0 + 1 + n, :], ref[k, r0 - 1 : r0 - 1 + n, :]))
                    return pick(pick(c, horizontal), pick(above(z, ref, k, r0, n), below(z, ref, k, r0, n)))

                big, small = near(z["mx"][m], jnp.maximum), near(z["mn"][m], jnp.minimum)
                low = z["low"][m][k, r0 : r0 + n, :]
                a_e = z["ax"][m][k, r0 : r0 + n, :]
                a_w = west_of(a_e)
                a_n = z["ay"][m][k, r0 : r0 + n, :]
                a_s = z["ay"][m][k, r0 - 1 : r0 - 1 + n, :]
                a_t, a_b = z["az"][m][k, r0 : r0 + n, :], bottoms[m]
                p_in, p_out = 0.0, 0.0
                for inward, outward in ((a_w, a_e), (a_s, a_n), (a_b, a_t)):
                    p_in = p_in + (jnp.maximum(inward, 0.0) - jnp.minimum(outward, 0.0))
                    p_out = p_out + (jnp.maximum(outward, 0.0) - jnp.minimum(inward, 0.0))
                r_in = jnp.clip((big - low) * pl.reciprocal(jnp.maximum(p_in, TINY)), 0.0, 1.0)
                r_out = jnp.clip((low - small) * pl.reciprocal(jnp.maximum(p_out, TINY)), 0.0, 1.0)
                z["rin"][m][k, r0 + lo : r0 + hi, :] = r_in[lo:hi]
                z["rout"][m][k, r0 + lo : r0 + hi, :] = r_out[lo:hi]
                tops.append(a_t)
            out.append(tuple(tops))
        return tuple(out)

    start = nothing(z, wins)
    if z["split"]:
        start = tuple(tuple(to_upper(a[0, r0 : r0 + n, :]) for a in z["az"]) for r0, n, _, _ in wins)
    upward(z, body, start)


def limited(anti, r_in, r_out, far_in, far_out):
    return anti * jnp.where(anti >= 0, jnp.minimum(far_in, r_out), jnp.minimum(r_in, far_out))


def stage_limit(z, wins):
    nk = z["u"].shape[0]
    stat = [z["f"][r0 : r0 + n, :] for r0, n, _, _ in wins]

    def rise(m, k, r0, n):
        r_in, r_out = z["rin"][m][k, r0 : r0 + n, :], z["rout"][m][k, r0 : r0 + n, :]
        far_in, far_out = above(z, z["rin"][m], k, r0, n), above(z, z["rout"][m], k, r0, n)
        return limited(z["az"][m][k, r0 : r0 + n, :], r_in, r_out, far_in, far_out)

    def body(k, kk, carry):
        out = []
        for (r0, n, lo, hi), f, bottoms in zip(wins, stat, carry):
            tops = []
            for m in range(len(z["t"])):
                r_in, r_out = z["rin"][m][k, r0 : r0 + n, :], z["rout"][m][k, r0 : r0 + n, :]
                f_e = limited(z["ax"][m][k, r0 : r0 + n, :], r_in, r_out, east_of(r_in), east_of(r_out))
                f_n = limited(
                    z["ay"][m][k, r0 : r0 + n, :], r_in, r_out,
                    z["rin"][m][k, r0 + 1 : r0 + 1 + n, :], z["rout"][m][k, r0 + 1 : r0 + 1 + n, :],
                )
                f_t = rise(m, k, r0, n)
                low = z["low"][m][k, r0 : r0 + n, :]
                new = low - ((f_e - west_of(f_e)) + (f_n - south_of(f_n)) + (f_t - bottoms[m]))
                new = jnp.where(kk < f, new, 0.0)
                z["adv"][m][k, r0 + lo : r0 + hi, :] = new[lo:hi]
                tops.append(f_t)
            out.append(tuple(tops))
        return tuple(out)

    start = nothing(z, wins)
    if z["split"]:
        start = tuple(tuple(to_upper(rise(m, 0, r0, n)) for m in range(len(z["t"]))) for r0, n, _, _ in wins)
    upward(z, body, start)


def clip_slope(x):
    return jnp.clip(x, -slope_limit, slope_limit)


def stage_diffuse(z, wins, emit):
    nk = z["u"].shape[0]
    dens = z["density"]
    nt = len(z["t"])
    stat = []
    for r0, n, _, _ in wins:
        f = z["f"][r0 : r0 + n, :]
        far_e, far_n = east_of(f), z["f"][r0 + 1 : r0 + 1 + n, :]
        stat.append((f, far_e, far_n, jnp.minimum(f, far_e), jnp.minimum(f, far_n)))

    def inverse(grads):
        return pl.reciprocal(jnp.maximum(-dens(grads), strat_floor))

    def vertical(k, kk, r0, n, f, far_n):
        gz = [jnp.where(kk < f, above(z, a, k, r0, n) - a[k, r0 : r0 + n, :], 0.0) for a in z["adv"]]
        gz_n = [jnp.where(kk < far_n, above(z, a, k, r0 + 1, n) - a[k, r0 + 1 : r0 + 1 + n, :], 0.0) for a in z["adv"]]
        inv = inverse(gz)
        return inv, east_of(inv), inverse(gz_n), tuple(gz), tuple(east_of(g) for g in gz), tuple(gz_n)

    def body(k, kk, carry):
        out = []
        for wi, ((r0, n, _, _), (f, far_e, far_n, f_e, f_n), old) in enumerate(zip(wins, stat, carry)):
            if not z["split"]:
                not_top = (k >= 1).astype(jnp.float32)
            elif k == 0:
                not_top = jnp.where(upper_lanes(n), 0.0, 1.0)
            here = [a[k, r0 : r0 + n, :] for a in z["adv"]]
            north = [a[k, r0 + 1 : r0 + 1 + n, :] for a in z["adv"]]
            inv, inv_e, inv_n, gz, gz_e, gz_n = vertical(k, kk, r0, n, f, far_n)
            gx = [jnp.where(kk < f_e, east_of(c) - c, 0.0) for c in here]
            gy = [jnp.where(kk < f_n, b - c, 0.0) for b, c in zip(north, here)]
            rx, ry = dens(gx), dens(gy)
            (o_inv, o_inv_e, o_inv_n, o_gz, o_gz_e, o_gz_n), o_part, o_top = old
            low_here, low_e, low_n = kk + 1.0 < f, kk + 1.0 < far_e, kk + 1.0 < far_n
            s_x = [clip_slope(rx * q) for q in (inv, inv_e, o_inv, o_inv_e)]
            s_y = [clip_slope(ry * q) for q in (inv, inv_n, o_inv, o_inv_n)]
            parts, tops = [], []
            for m in range(nt):
                gx_top, gy_top = gx[m], gy[m]
                if not z["split"] or k == 0:
                    gx_top, gy_top = gx_top * not_top, gy_top * not_top
                hx = (
                    gx_top + s_x[0] * gz[m],
                    gx_top + s_x[1] * gz_e[m],
                    jnp.where(low_here, gx[m], 0.0) + s_x[2] * o_gz[m],
                    jnp.where(low_e, gx[m], 0.0) + s_x[3] * o_gz_e[m],
                )
                hy = (
                    gy_top + s_y[0] * gz[m],
                    gy_top + s_y[1] * gz_n[m],
                    jnp.where(low_here, gy[m], 0.0) + s_y[2] * o_gz[m],
                    jnp.where(low_n, gy[m], 0.0) + s_y[3] * o_gz_n[m],
                )
                flux_e = (hx[0] + hx[1]) + (hx[2] + hx[3])
                flux_n = (hy[0] + hy[1]) + (hy[2] + hy[3])
                top = (s_x[0] * hx[0] + west_of(s_x[1] * hx[1])) + (s_y[0] * hy[0] + south_of(s_y[1] * hy[1]))
                bottom = (s_x[2] * hx[2] + west_of(s_x[3] * hx[3])) + (s_y[2] * hy[2] + south_of(s_y[3] * hy[3]))
                rise = o_top[m] + bottom
                if z["split"] and k == nk - 1:
                    bottom_lower[wi, m] = to_lower(bottom)
                else:
                    done = jnp.where(kk + 1.0 < f, o_part[m] + DIFF_SCALE * rise, 0.0)
                    emit(k + 1 if z["split"] else jnp.minimum(k + 1, nk - 1), wi, m, done)
                parts.append(here[m] + DIFF_SCALE * ((flux_e - west_of(flux_e)) + (flux_n - south_of(flux_n)) - rise))
                tops.append(top)
            out.append(((inv, inv_e, inv_n, gz, gz_e, gz_n), tuple(parts), tuple(tops)))
        return tuple(out)

    bottom_lower = {}
    start = []
    for (r0, n, _, _), (f, _, far_n, *_) in zip(wins, stat):
        x = jnp.zeros((n, 128), jnp.float32)
        xs = tuple(x for _ in range(nt))
        first = (x, x, x, xs, xs, xs)
        if z["split"]:
            first = jax.tree.map(to_upper, vertical(0, jnp.float32(0), r0, n, f, far_n))
        start.append((first, xs, xs))
    last = upward(z, body, tuple(start))
    for wi, ((r0, n, _, _), (f, *_), (_, parts, tops)) in enumerate(zip(wins, stat, last)):
        for m in range(nt):
            top = tops[m]
            if z["split"]:
                top = top + bottom_lower[wi, m]
                late = jnp.where(nk - 1.0 < f, -DIFF_SCALE * to_upper(tops[m]), 0.0)
                emit(nk - 1, wi, m, late, True)
            emit(0, wi, m, jnp.where(0.0 < f, parts[m] + DIFF_SCALE * top, 0.0))


def kernel(
    t_hbm, s_hbm, u_hbm, v_hbm, flag_hbm, point_hbm, count_hbm,
    t_out, s_out, e_res,
    flag_ref, point_ref, count_ref, tr, u, v, floor, low, mx, mn, ax, ay, az, rin, rout, adv,
    e_tr, e_u, e_v, e_floor, e_low, e_mx, e_mn, e_ax, e_ay, e_az, e_rin, e_rout, e_adv,
    row_out, row_in, strip_out, strip_in, fold_out, corner_in,
    load_sem, send_sem, recv_sem, ready,
):
    n_lon, n_lat = lax.axis_size("lon"), lax.axis_size("lat")
    lon, lat = lax.axis_index("lon"), lax.axis_index("lat")
    nk = u.shape[0]
    half = nk // 2
    east, west = lax.rem(lon + 1, n_lon), lax.rem(lon + n_lon - 1, n_lon)
    at_north, at_south = lat == n_lat - 1, lat == 0
    to_east, to_west = (east, lat), (west, lat)
    to_north, to_south, to_fold = (lon, lat + 1), (lon, lat - 1), (n_lon - 1 - lon, lat)
    fold_ne, fold_nw = lax.rem(2 * n_lon - 2 - lon, n_lon), lax.rem(n_lon - lon, n_lon)
    ne_self, nw_self = fold_ne == lon, fold_nw == lon

    barrier = pltpu.get_barrier_semaphore()

    def greet(where):
        pl.semaphore_signal(barrier, inc=1, device_id=where, device_id_type=MESH)

    greet(to_east)
    greet(to_west)

    @pl.when(jnp.logical_not(at_south))
    def _():
        greet(to_south)

    @pl.when(jnp.logical_not(at_north))
    def _():
        greet(to_north)

    @pl.when(at_north)
    def _():
        greet(to_fold)

    loads = [
        pltpu.make_async_copy(src, dst.at[:, 8:24, :], load_sem.at[i])
        for i, (src, dst) in enumerate(((t_hbm, tr.at[0]), (s_hbm, tr.at[1]), (u_hbm, u), (v_hbm, v)))
    ]
    loads += [
        pltpu.make_async_copy(src, dst, load_sem.at[4 + i])
        for i, (src, dst) in enumerate(((flag_hbm, flag_ref), (point_hbm, point_ref), (count_hbm, count_ref)))
    ]
    for copy in loads:
        copy.start()
    for copy in loads:
        copy.wait()
    floor[8:24, :] = (count_ref[...] * point_ref[...] * flag_ref[...]).astype(jnp.float32)

    lane8, sub8 = lane_iota(8), lax.broadcasted_iota(jnp.int32, (8, 128), 0)

    p = lax.rem(lane8, 32)
    shift = jnp.where(p < 12, 116, jnp.where(p < 16, -12, jnp.where(p < 20, 108, -20)))
    strip_idx = lax.rem(p + shift + 128, 128)
    first, upper = lane8 < 64, upper_lanes(8)

    def strip_tile(row):
        rows = slice(row, row + 8)

        def gather(x):
            return jnp.take_along_axis(x, strip_idx, axis=1)

        def halves(ref, k):
            return jnp.where(upper, gather(ref[k, rows, :]), gather(ref[k + half, rows, :]))

        for k in range(half):
            e_tr[k, rows, :] = jnp.where(first, halves(tr.at[0], k), halves(tr.at[1], k))
            e_u[k, rows, :] = halves(u, k)
            e_v[k, rows, :] = halves(v, k)
        e_floor[rows, :] = gather(floor[rows, :]) - jnp.where(upper, 0.0, float(half))

    q_t = jnp.logical_and(p >= 12, p < 20)
    q_u = jnp.logical_and(p >= 20, p < 28)
    for row in (8, 16):
        strip_tile(row)
        rows = slice(row, row + 8)
        for k in range(half):
            strip_out[k, row - 8 : row, :] = jnp.where(
                q_t, e_tr[k, rows, :],
                jnp.where(q_u, pltpu.roll(e_u[k, rows, :], 8, 1), pltpu.roll(e_v[k, rows, :], 16, 1)),
            )
        strip_out[half, row - 8 : row, :] = e_floor[rows, :]

    pl.semaphore_wait(barrier, jnp.where(at_south, 3, 4))

    pl.semaphore_signal(ready.at[1], inc=1, device_id=to_east, device_id_type=MESH)
    pl.semaphore_signal(ready.at[0], inc=1, device_id=to_west, device_id_type=MESH)

    def send(src, dst, role, slot, where):
        return pltpu.make_async_remote_copy(
            src_ref=src, dst_ref=dst, send_sem=send_sem.at[role], recv_sem=recv_sem.at[slot],
            device_id=where, device_id_type=MESH,
        )

    rows_north = send(row_out.at[0], row_in.at[1], NORTH, SOUTH, to_north)
    rows_fold = send(row_out.at[0], row_in.at[0], NORTH, NORTH, to_fold)
    rows_south = send(row_out.at[1], row_in.at[0], SOUTH, NORTH, to_south)
    strip_west = send(strip_out, strip_in.at[0], WEST, EAST, to_west)
    strip_east = send(strip_out, strip_in.at[1], EAST, WEST, to_east)

    def corner(src, role, slot, where):
        return send(src, corner_in.at[CORNER[slot]], role, slot, where)

    upper_rows, lower_rows = strip_out.at[:, 8:16, :], strip_out.at[:, 0:8, :]
    corners_north = (corner(upper_rows, NE, SW, (east, lat + 1)), corner(upper_rows, NW, SE, (west, lat + 1)))
    corners_south = (corner(lower_rows, SE, NW, (east, lat - 1)), corner(lower_rows, SW, NE, (west, lat - 1)))
    corners_fold = (
        (corner(fold_out, NE, NE, (fold_ne, lat)), pltpu.make_async_copy(fold_out, corner_in.at[CORNER[NE]], send_sem.at[NE]), ne_self),
        (corner(fold_out, NW, NW, (fold_nw, lat)), pltpu.make_async_copy(fold_out, corner_in.at[CORNER[NW]], send_sem.at[NW]), nw_self),
    )

    strip_west.start()
    strip_east.start()

    fields = ((tr.at[0], tr.at[1]), (u, v))
    for side_no, row in ((0, 20), (1, 8)):
        for g, (a, b) in enumerate(fields):
            for k in range(nk):
                row_out[side_no, g * nk + k, 0:4, :] = a[k, row : row + 4, :]
                row_out[side_no, g * nk + k, 4:8, :] = b[k, row : row + 4, :]
        row_out[side_no, 2 * nk, 0:4, :] = floor[row : row + 4, :]

    @pl.when(at_north)
    def _():
        for k in range(2 * nk + 1):
            x = jnp.take_along_axis(row_out[0, k], 127 - lane8, axis=1)
            x = jnp.take_along_axis(x, 3 - lax.rem(sub8, 4) + jnp.where(sub8 < 4, 0, 4), axis=0)
            row_out[0, k] = -x if nk <= k < 2 * nk else x

    @pl.when(jnp.logical_not(at_south))
    def _():
        rows_south.start()

    @pl.when(jnp.logical_not(at_north))
    def _():
        rows_north.start()

    @pl.when(at_north)
    def _():
        rows_fold.start()

    pl.semaphore_wait(ready.at[0], 1)
    pl.semaphore_wait(ready.at[1], 1)

    @pl.when(jnp.logical_not(at_south))
    def _():
        for copy in corners_south:
            copy.start()

    @pl.when(jnp.logical_not(at_north))
    def _():
        for copy in corners_north:
            copy.start()

    @pl.when(at_north)
    def _():
        group_idx = lax.rem(lane8 + 7 - 2 * lax.rem(lane8 + 4, 8) + 128, 128)
        sign = jnp.where(q_t, 1.0, -1.0)
        for k in range(half + 1):
            x = jnp.take_along_axis(strip_out[k, 8:16, :], group_idx, axis=1)
            x = jnp.take_along_axis(x, 7 - sub8, axis=0)
            fold_out[k] = x if k == half else x * sign
        for copy, local, own in corners_fold:
            pl.when(own)(local.start)
            pl.when(jnp.logical_not(own))(copy.start)

    main = dict(
        split=False, t=[tr.at[0], tr.at[1]], u=u, v=v, f=floor,
        density=lambda pair: haline_coef * pair[1] - thermal_coef * pair[0],
    )
    names = dict(low=low, mx=mx, mn=mn, ax=ax, ay=ay, az=az, rin=rin, rout=rout, adv=adv)
    main.update({name: [ref.at[0], ref.at[1]] for name, ref in names.items()})

    outs = (t_out, s_out)

    stage_flux(main, [(8, 16, 0, 16)])
    stage_ratio(main, [(8, 16, 0, 16)])
    stage_limit(main, [(8, 16, 0, 16)])

    def emit_inner(k, wi, m, val):
        outs[m][k, 4:12, :] = val[4:12]

    stage_diffuse(main, [(8, 16, 4, 12)], emit_inner)

    strip_west.wait()
    strip_east.wait()
    from_east = lax.rem(lane8, 8) >= 4

    def strip_halo(row, east_ref, west_ref, at):
        rows = slice(row, row + 8)
        for k in range(half + 1):
            x = jnp.where(from_east, east_ref[k, at : at + 8, :], west_ref[k, at : at + 8, :])
            if k == half:
                e_floor[rows, :] = jnp.where(q_t, x, e_floor[rows, :])
                continue
            e_tr[k, rows, :] = jnp.where(q_t, x, e_tr[k, rows, :])
            e_u[k, rows, :] = jnp.where(q_t, pltpu.roll(x, 120, 1), e_u[k, rows, :])
            e_v[k, rows, :] = jnp.where(q_t, pltpu.roll(x, 112, 1), e_v[k, rows, :])

    strip_halo(8, strip_in.at[0], strip_in.at[1], 0)
    strip_halo(16, strip_in.at[0], strip_in.at[1], 8)

    @pl.when(at_south)
    def _():
        row_in[1] = jnp.zeros(row_in.shape[1:], jnp.float32)
        for slot in (SE, SW):
            corner_in[CORNER[slot]] = jnp.zeros(corner_in.shape[1:], jnp.float32)

    @pl.when(jnp.logical_not(at_south))
    def _():
        rows_south.wait_send()
        rows_north.wait_recv()

    @pl.when(jnp.logical_not(at_north))
    def _():
        rows_north.wait_send()
        rows_south.wait_recv()

    @pl.when(at_north)
    def _():
        rows_fold.wait()

    for slot, row in ((1, 4), (0, 24)):
        for g, (a, b) in enumerate(fields):
            for k in range(nk):
                a[k, row : row + 4, :] = row_in[slot, g * nk + k, 0:4, :]
                b[k, row : row + 4, :] = row_in[slot, g * nk + k, 4:8, :]
        floor[row : row + 4, :] = row_in[slot, 2 * nk, 0:4, :]

    stage_flux(main, [(4, 8, 1, 5), (20, 8, 3, 7)])
    stage_ratio(main, [(4, 8, 2, 6), (20, 8, 2, 6)])
    stage_limit(main, [(4, 8, 3, 7), (20, 8, 1, 5)])

    def emit_outer(k, wi, m, val):
        if wi == 0:
            outs[m][k, 0:4, :] = val[4:8]
        else:
            outs[m][k, 12:16, :] = val[4:8]

    stage_diffuse(main, [(4, 8, 4, 8), (16, 8, 4, 8)], emit_outer)

    strip_tile(0)
    strip_tile(24)

    @pl.when(jnp.logical_not(at_south))
    def _():
        for copy in corners_south:
            copy.wait_send()
        for copy in corners_north:
            copy.wait_recv()

    @pl.when(jnp.logical_not(at_north))
    def _():
        for copy in corners_north:
            copy.wait_send()
        for copy in corners_south:
            copy.wait_recv()

    @pl.when(at_north)
    def _():
        for copy, local, own in corners_fold:
            pl.when(own)(local.wait)
            pl.when(jnp.logical_not(own))(copy.wait)

    strip_halo(0, corner_in.at[CORNER[SE]], corner_in.at[CORNER[SW]], 0)
    strip_halo(24, corner_in.at[CORNER[NE]], corner_in.at[CORNER[NW]], 0)

    def strip_density(one):
        x = one[0]
        low_half = lane_iota(x.shape[0]) < 64
        own = jnp.where(low_half, -thermal_coef, haline_coef)
        other = jnp.where(low_half, haline_coef, -thermal_coef)
        return own * x + other * pltpu.roll(x, 64, 1)

    strips = dict(split=True, t=[e_tr], u=e_u, v=e_v, f=e_floor, density=strip_density)
    names = dict(low=e_low, mx=e_mx, mn=e_mn, ax=e_ax, ay=e_ay, az=e_az, rin=e_rin, rout=e_rout, adv=e_adv)
    strips.update({name: [ref] for name, ref in names.items()})
    stage_flux(strips, [(4, 24, 0, 24)])
    stage_ratio(strips, [(4, 24, 0, 24)])
    stage_limit(strips, [(4, 24, 0, 24)])

    def emit_strip(k, wi, m, val, add=False):
        e_res[k] = e_res[k] + val[4:20] if add else val[4:20]

    stage_diffuse(strips, [(4, 24, 4, 20)], emit_strip)


def finish(t_ref, s_ref, e_res, t_hbm, s_hbm, t_buf, s_buf, sem):
    lane16 = lane_iota(16)
    rim = jnp.logical_or(lane16 < 4, lane16 >= 124)
    copies = []
    for m, (ref, buf, out) in enumerate(((t_ref, t_buf, t_hbm), (s_ref, s_buf, s_hbm))):
        back = jnp.where(lane16 < 4, lane16 + 20, jnp.where(lane16 >= 124, lane16 - 116, 0)) + 64 * m
        half = e_res.shape[0]
        for k in range(ref.shape[0]):
            edge = jnp.take_along_axis(e_res[k % half], back + 32 * (k // half), axis=1)
            buf[k] = jnp.where(rim, edge, ref[k])
        copies.append(pltpu.make_async_copy(buf, out, sem.at[m]))
        copies[-1].start()
    for copy in copies:
        copy.wait()


def on_device(t, s, u, v, flag, point, count):
    nk = t.shape[0]
    f32 = jnp.float32
    vm = lambda *shape: pltpu.VMEM(shape, f32)
    big = lambda: vm(2, nk, 32, 128)
    one = lambda: vm(nk, 32, 128)
    whole = pl.BlockSpec(memory_space=pltpu.VMEM)
    hbm = pl.BlockSpec(memory_space=pltpu.HBM)
    part = pltpu.VMEM(t.shape, f32)
    main_t, main_s, strips = pl.pallas_call(
        kernel,
        out_shape=(part, part, pltpu.VMEM((nk // 2, *t.shape[1:]), f32)),
        in_specs=[hbm] * 7,
        out_specs=(whole, whole, whole),
        scratch_shapes=[
            pltpu.VMEM(flag.shape, flag.dtype), pltpu.VMEM(point.shape, point.dtype), pltpu.VMEM(count.shape, count.dtype),
            big(), one(), one(), vm(32, 128),
            *[big() for _ in range(9)],
            *[vm(nk // 2, 32, 128) for _ in range(3)], vm(32, 128),
            *[vm(nk // 2, 32, 128) for _ in range(9)],
            vm(2, 2 * nk + 1, 8, 128), vm(2, 2 * nk + 1, 8, 128),
            vm(nk // 2 + 1, 16, 128), vm(2, nk // 2 + 1, 16, 128),
            vm(nk // 2 + 1, 8, 128), vm(4, nk // 2 + 1, 8, 128),
            pltpu.SemaphoreType.DMA((7,)), pltpu.SemaphoreType.DMA((8,)), pltpu.SemaphoreType.DMA((8,)),
            pltpu.SemaphoreType.REGULAR((2,)),
        ],
        compiler_params=pltpu.CompilerParams(
            collective_id=0, has_side_effects=True, vmem_limit_bytes=60 * 1024 * 1024
        ),
    )(t, s, u, v, flag, point, count)
    result = jax.ShapeDtypeStruct(t.shape, f32)
    return pl.pallas_call(
        finish,
        out_shape=(result, result),
        in_specs=[whole] * 3,
        out_specs=(hbm, hbm),
        scratch_shapes=[vm(*t.shape), vm(*t.shape), pltpu.SemaphoreType.DMA((2,))],
        compiler_params=pltpu.CompilerParams(vmem_limit_bytes=4 * 1024 * 1024),
    )(main_t, main_s, strips)


def solution(mesh):
    grid = P(None, "lat", "lon")
    flat = P("lat", "lon")
    return jax.shard_map(
        on_device, mesh=mesh, in_specs=(grid,) * 4 + (flat,) * 3, out_specs=(grid, grid), check_vma=False
    )
```

```python
import functools

import jax
import jax.numpy as jnp
from jax import lax
from jax.experimental import pallas as pl
from jax.experimental.pallas import tpu as pltpu
from jax.sharding import PartitionSpec as P

time_step = 0.5
diffusivity = 0.1
strat_floor = 0.5
slope_limit = 2.0
thermal_coef = 0.2
haline_coef = 0.8

MESH = pl.DeviceIdType.MESH
INF = float("inf")
TINY = 1e-37
FACE_SCALE = 0.25 * time_step
DIFF_SCALE = 0.25 * time_step * diffusivity

EAST, WEST, NORTH, SOUTH, NE, NW, SE, SW = range(8)
CORNER = {NE: 0, NW: 1, SE: 2, SW: 3}


def east_of(x):
    return pltpu.roll(x, x.shape[1] - 1, 1)


def west_of(x):
    return pltpu.roll(x, 1, 1)


def south_of(x):
    return pltpu.roll(x, 1, 0)


def lane_iota(rows):
    return lax.broadcasted_iota(jnp.int32, (rows, 128), 1)


def upper_lanes(rows):
    return lax.rem(lane_iota(rows), 64) < 32


def to_upper(x):
    return jnp.where(upper_lanes(x.shape[0]), pltpu.roll(x, 96, 1), 0.0)


def to_lower(x):
    return jnp.where(upper_lanes(x.shape[0]), 0.0, pltpu.roll(x, 32, 1))


def above(z, ref, k, r0, n):
    if not z["split"]:
        return ref[jnp.maximum(k - 1, 0), r0 : r0 + n, :]
    if k > 0:
        return ref[k - 1, r0 : r0 + n, :]
    last = z["u"].shape[0] - 1
    return jnp.where(upper_lanes(n), ref[0, r0 : r0 + n, :], pltpu.roll(ref[last, r0 : r0 + n, :], 32, 1))


def below(z, ref, k, r0, n):
    last = z["u"].shape[0] - 1
    if not z["split"]:
        return ref[jnp.minimum(k + 1, last), r0 : r0 + n, :]
    if k < last:
        return ref[k + 1, r0 : r0 + n, :]
    return jnp.where(upper_lanes(n), pltpu.roll(ref[0, r0 : r0 + n, :], 96, 1), ref[last, r0 : r0 + n, :])


def upward(z, body, carry):
    nk = z["u"].shape[0]
    if z["split"]:
        for k in range(nk - 1, -1, -1):
            carry = body(k, jnp.float32(k), carry)
        return carry

    def step(i, carry):
        k = nk - 1 - i
        return body(k, k.astype(jnp.float32), carry)

    return lax.fori_loop(0, nk, step, carry, unroll=nk // 2)


def nothing(z, wins):
    return tuple(tuple(jnp.zeros((n, 128), jnp.float32) for _ in z["t"]) for _, n, _, _ in wins)


def stage_flux(z, wins):
    nk = z["u"].shape[0]
    stat = []
    for r0, n, _, _ in wins:
        f = z["f"][r0 : r0 + n, :]
        f_e = jnp.minimum(f, east_of(f))
        f_n = jnp.minimum(f, z["f"][r0 + 1 : r0 + 1 + n, :])
        stat.append((f, f_e, f_n))

    def velocities(k, kk, r0, n, f_e, f_n):
        u = z["u"][k, r0 : r0 + n, :]
        u_e = jnp.where(kk < f_e, FACE_SCALE * (u + east_of(u)), 0.0)
        v = z["v"][k, r0 : r0 + n, :]
        v_n = jnp.where(kk < f_n, FACE_SCALE * (v + z["v"][k, r0 + 1 : r0 + 1 + n, :]), 0.0)
        return u_e, v_n, u_e - west_of(u_e) + v_n - south_of(v_n)

    def body(k, kk, carry):
        out = []
        for (r0, n, lo, hi), (f, f_e, f_n), (w_old, bottoms) in zip(wins, stat, carry):
            u_e, v_n, gain = velocities(k, kk, r0, n, f_e, f_n)
            w = w_old - gain
            abs_u, abs_v, abs_w = jnp.abs(u_e), jnp.abs(v_n), jnp.abs(w)
            wet = kk < f
            tops = []
            for m, t in enumerate(z["t"]):
                c = t[k, r0 : r0 + n, :]
                e = east_of(c)
                nn = t[k, r0 + 1 : r0 + 1 + n, :]
                up = above(z, t, k, r0, n)
                a_e = abs_u * (e - c)
                l_e = u_e * (c + e) - a_e
                a_n = abs_v * (nn - c)
                l_n = v_n * (c + nn) - a_n
                a_t = abs_w * (up - c)
                l_t = w * (c + up) - a_t
                low = c - ((l_e - west_of(l_e)) + (l_n - south_of(l_n)) + (l_t - bottoms[m]))
                low = jnp.where(wet, low, 0.0)
                big = jnp.where(wet, jnp.maximum(c, low), -INF)
                small = jnp.where(wet, jnp.minimum(c, low), INF)
                for name, val in (("ax", a_e), ("ay", a_n), ("az", a_t), ("low", low), ("mx", big), ("mn", small)):
                    z[name][m][k, r0 + lo : r0 + hi, :] = val[lo:hi]
                tops.append(l_t)
            out.append((w, tuple(tops)))
        return tuple(out)

    start = []
    for (r0, n, _, _), (f, f_e, f_n) in zip(wins, stat):
        w = jnp.zeros((n, 128), jnp.float32)
        flows = tuple(w for _ in z["t"])
        if z["split"]:
            for k in range(nk):
                w = w - velocities(k, jnp.float32(k), r0, n, f_e, f_n)[2]
            w = to_upper(w)
            flows = []
            for t in z["t"]:
                up, c = t[nk - 1, r0 : r0 + n, :], below(z, t, nk - 1, r0, n)
                flows.append(w * (c + up) - jnp.abs(w) * (up - c))
        start.append((w, tuple(flows)))
    upward(z, body, tuple(start))


def stage_ratio(z, wins):
    nk = z["u"].shape[0]

    def body(k, kk, carry):
        out = []
        for (r0, n, lo, hi), bottoms in zip(wins, carry):
            tops = []
            for m in range(len(z["t"])):
                def near(ref, pick):
                    c = ref[k, r0 : r0 + n, :]
                    horizontal = pick(pick(east_of(c), west_of(c)), pick(ref[k, r0 + 1 : r0 + 1 + n, :], ref[k, r0 - 1 : r0 - 1 + n, :]))
                    return pick(pick(c, horizontal), pick(above(z, ref, k, r0, n), below(z, ref, k, r0, n)))

                big, small = near(z["mx"][m], jnp.maximum), near(z["mn"][m], jnp.minimum)
                low = z["low"][m][k, r0 : r0 + n, :]
                a_e = z["ax"][m][k, r0 : r0 + n, :]
                a_w = west_of(a_e)
                a_n = z["ay"][m][k, r0 : r0 + n, :]
                a_s = z["ay"][m][k, r0 - 1 : r0 - 1 + n, :]
                a_t, a_b = z["az"][m][k, r0 : r0 + n, :], bottoms[m]
                p_in, p_out = 0.0, 0.0
                for inward, outward in ((a_w, a_e), (a_s, a_n), (a_b, a_t)):
                    p_in = p_in + (jnp.maximum(inward, 0.0) - jnp.minimum(outward, 0.0))
                    p_out = p_out + (jnp.maximum(outward, 0.0) - jnp.minimum(inward, 0.0))
                r_in = jnp.clip((big - low) * pl.reciprocal(jnp.maximum(p_in, TINY)), 0.0, 1.0)
                r_out = jnp.clip((low - small) * pl.reciprocal(jnp.maximum(p_out, TINY)), 0.0, 1.0)
                z["rin"][m][k, r0 + lo : r0 + hi, :] = r_in[lo:hi]
                z["rout"][m][k, r0 + lo : r0 + hi, :] = r_out[lo:hi]
                tops.append(a_t)
            out.append(tuple(tops))
        return tuple(out)

    start = nothing(z, wins)
    if z["split"]:
        start = tuple(tuple(to_upper(a[0, r0 : r0 + n, :]) for a in z["az"]) for r0, n, _, _ in wins)
    upward(z, body, start)


def limited(anti, r_in, r_out, far_in, far_out):
    return anti * jnp.where(anti >= 0, jnp.minimum(far_in, r_out), jnp.minimum(r_in, far_out))


def stage_limit(z, wins):
    nk = z["u"].shape[0]
    stat = [z["f"][r0 : r0 + n, :] for r0, n, _, _ in wins]

    def rise(m, k, r0, n):
        r_in, r_out = z["rin"][m][k, r0 : r0 + n, :], z["rout"][m][k, r0 : r0 + n, :]
        far_in, far_out = above(z, z["rin"][m], k, r0, n), above(z, z["rout"][m], k, r0, n)
        return limited(z["az"][m][k, r0 : r0 + n, :], r_in, r_out, far_in, far_out)

    def body(k, kk, carry):
        out = []
        for (r0, n, lo, hi), f, bottoms in zip(wins, stat, carry):
            tops = []
            for m in range(len(z["t"])):
                r_in, r_out = z["rin"][m][k, r0 : r0 + n, :], z["rout"][m][k, r0 : r0 + n, :]
                f_e = limited(z["ax"][m][k, r0 : r0 + n, :], r_in, r_out, east_of(r_in), east_of(r_out))
                f_n = limited(
                    z["ay"][m][k, r0 : r0 + n, :], r_in, r_out,
                    z["rin"][m][k, r0 + 1 : r0 + 1 + n, :], z["rout"][m][k, r0 + 1 : r0 + 1 + n, :],
                )
                f_t = rise(m, k, r0, n)
                low = z["low"][m][k, r0 : r0 + n, :]
                new = low - ((f_e - west_of(f_e)) + (f_n - south_of(f_n)) + (f_t - bottoms[m]))
                new = jnp.where(kk < f, new, 0.0)
                z["adv"][m][k, r0 + lo : r0 + hi, :] = new[lo:hi]
                tops.append(f_t)
            out.append(tuple(tops))
        return tuple(out)

    start = nothing(z, wins)
    if z["split"]:
        start = tuple(tuple(to_upper(rise(m, 0, r0, n)) for m in range(len(z["t"]))) for r0, n, _, _ in wins)
    upward(z, body, start)


def clip_slope(x):
    return jnp.clip(x, -slope_limit, slope_limit)


def stage_diffuse(z, wins, emit):
    nk = z["u"].shape[0]
    dens = z["density"]
    nt = len(z["t"])
    stat = []
    for r0, n, _, _ in wins:
        f = z["f"][r0 : r0 + n, :]
        far_e, far_n = east_of(f), z["f"][r0 + 1 : r0 + 1 + n, :]
        stat.append((f, far_e, far_n, jnp.minimum(f, far_e), jnp.minimum(f, far_n)))

    def inverse(grads):
        return pl.reciprocal(jnp.maximum(-dens(grads), strat_floor))

    def vertical(k, kk, r0, n, f, far_n):
        gz = [jnp.where(kk < f, above(z, a, k, r0, n) - a[k, r0 : r0 + n, :], 0.0) for a in z["adv"]]
        gz_n = [jnp.where(kk < far_n, above(z, a, k, r0 + 1, n) - a[k, r0 + 1 : r0 + 1 + n, :], 0.0) for a in z["adv"]]
        inv = inverse(gz)
        return inv, east_of(inv), inverse(gz_n), tuple(gz), tuple(east_of(g) for g in gz), tuple(gz_n)

    def body(k, kk, carry):
        out = []
        for wi, ((r0, n, _, _), (f, far_e, far_n, f_e, f_n), old) in enumerate(zip(wins, stat, carry)):
            if not z["split"]:
                not_top = (k >= 1).astype(jnp.float32)
            elif k == 0:
                not_top = jnp.where(upper_lanes(n), 0.0, 1.0)
            here = [a[k, r0 : r0 + n, :] for a in z["adv"]]
            north = [a[k, r0 + 1 : r0 + 1 + n, :] for a in z["adv"]]
            inv, inv_e, inv_n, gz, gz_e, gz_n = vertical(k, kk, r0, n, f, far_n)
            gx = [jnp.where(kk < f_e, east_of(c) - c, 0.0) for c in here]
            gy = [jnp.where(kk < f_n, b - c, 0.0) for b, c in zip(north, here)]
            rx, ry = dens(gx), dens(gy)
            (o_inv, o_inv_e, o_inv_n, o_gz, o_gz_e, o_gz_n), o_part, o_top = old
            low_here, low_e, low_n = kk + 1.0 < f, kk + 1.0 < far_e, kk + 1.0 < far_n
            s_x = [clip_slope(rx * q) for q in (inv, inv_e, o_inv, o_inv_e)]
            s_y = [clip_slope(ry * q) for q in (inv, inv_n, o_inv, o_inv_n)]
            parts, tops = [], []
            for m in range(nt):
                gx_top, gy_top = gx[m], gy[m]
                if not z["split"] or k == 0:
                    gx_top, gy_top = gx_top * not_top, gy_top * not_top
                hx = (
                    gx_top + s_x[0] * gz[m],
                    gx_top + s_x[1] * gz_e[m],
                    jnp.where(low_here, gx[m], 0.0) + s_x[2] * o_gz[m],
                    jnp.where(low_e, gx[m], 0.0) + s_x[3] * o_gz_e[m],
                )
                hy = (
                    gy_top + s_y[0] * gz[m],
                    gy_top + s_y[1] * gz_n[m],
                    jnp.where(low_here, gy[m], 0.0) + s_y[2] * o_gz[m],
                    jnp.where(low_n, gy[m], 0.0) + s_y[3] * o_gz_n[m],
                )
                flux_e = (hx[0] + hx[1]) + (hx[2] + hx[3])
                flux_n = (hy[0] + hy[1]) + (hy[2] + hy[3])
                top = (s_x[0] * hx[0] + west_of(s_x[1] * hx[1])) + (s_y[0] * hy[0] + south_of(s_y[1] * hy[1]))
                bottom = (s_x[2] * hx[2] + west_of(s_x[3] * hx[3])) + (s_y[2] * hy[2] + south_of(s_y[3] * hy[3]))
                rise = o_top[m] + bottom
                if z["split"] and k == nk - 1:
                    bottom_lower[wi, m] = to_lower(bottom)
                else:
                    done = jnp.where(kk + 1.0 < f, o_part[m] + DIFF_SCALE * rise, 0.0)
                    emit(k + 1 if z["split"] else jnp.minimum(k + 1, nk - 1), wi, m, done)
                parts.append(here[m] + DIFF_SCALE * ((flux_e - west_of(flux_e)) + (flux_n - south_of(flux_n)) - rise))
                tops.append(top)
            out.append(((inv, inv_e, inv_n, gz, gz_e, gz_n), tuple(parts), tuple(tops)))
        return tuple(out)

    bottom_lower = {}
    start = []
    for (r0, n, _, _), (f, _, far_n, *_) in zip(wins, stat):
        x = jnp.zeros((n, 128), jnp.float32)
        xs = tuple(x for _ in range(nt))
        first = (x, x, x, xs, xs, xs)
        if z["split"]:
            first = jax.tree.map(to_upper, vertical(0, jnp.float32(0), r0, n, f, far_n))
        start.append((first, xs, xs))
    last = upward(z, body, tuple(start))
    for wi, ((r0, n, _, _), (f, *_), (_, parts, tops)) in enumerate(zip(wins, stat, last)):
        for m in range(nt):
            top = tops[m]
            if z["split"]:
                top = top + bottom_lower[wi, m]
                late = jnp.where(nk - 1.0 < f, -DIFF_SCALE * to_upper(tops[m]), 0.0)
                emit(nk - 1, wi, m, late, True)
            emit(0, wi, m, jnp.where(0.0 < f, parts[m] + DIFF_SCALE * top, 0.0))


def kernel(
    t_hbm, s_hbm, u_hbm, v_hbm, flag_hbm, point_hbm, count_hbm,
    t_out, s_out, e_res,
    flag_ref, point_ref, count_ref, tr, u, v, floor, low, mx, mn, ax, ay, az, rin, rout, adv,
    e_tr, e_u, e_v, e_floor, e_low, e_mx, e_mn, e_ax, e_ay, e_az, e_rin, e_rout, e_adv,
    row_out, row_in, strip_out, strip_in, fold_out, corner_in,
    load_sem, send_sem, recv_sem, ready,
):
    n_lon, n_lat = lax.axis_size("lon"), lax.axis_size("lat")
    lon, lat = lax.axis_index("lon"), lax.axis_index("lat")
    nk = u.shape[0]
    half = nk // 2
    east, west = lax.rem(lon + 1, n_lon), lax.rem(lon + n_lon - 1, n_lon)
    at_north, at_south = lat == n_lat - 1, lat == 0
    to_east, to_west = (east, lat), (west, lat)
    to_north, to_south, to_fold = (lon, lat + 1), (lon, lat - 1), (n_lon - 1 - lon, lat)
    fold_ne, fold_nw = lax.rem(2 * n_lon - 2 - lon, n_lon), lax.rem(n_lon - lon, n_lon)
    ne_self, nw_self = fold_ne == lon, fold_nw == lon

    barrier = pltpu.get_barrier_semaphore()

    def greet(where):
        pl.semaphore_signal(barrier, inc=1, device_id=where, device_id_type=MESH)

    greet(to_east)
    greet(to_west)

    @pl.when(jnp.logical_not(at_south))
    def _():
        greet(to_south)

    @pl.when(jnp.logical_not(at_north))
    def _():
        greet(to_north)

    @pl.when(at_north)
    def _():
        greet(to_fold)

    loads = [
        pltpu.make_async_copy(src, dst.at[:, 8:24, :], load_sem.at[i])
        for i, (src, dst) in enumerate(((t_hbm, tr.at[0]), (s_hbm, tr.at[1]), (u_hbm, u), (v_hbm, v)))
    ]
    loads += [
        pltpu.make_async_copy(src, dst, load_sem.at[4 + i])
        for i, (src, dst) in enumerate(((flag_hbm, flag_ref), (point_hbm, point_ref), (count_hbm, count_ref)))
    ]
    for copy in loads:
        copy.start()
    for copy in loads:
        copy.wait()
    floor[8:24, :] = (count_ref[...] * point_ref[...] * flag_ref[...]).astype(jnp.float32)

    lane8, sub8 = lane_iota(8), lax.broadcasted_iota(jnp.int32, (8, 128), 0)

    p = lax.rem(lane8, 32)
    shift = jnp.where(p < 12, 116, jnp.where(p < 16, -12, jnp.where(p < 20, 108, -20)))
    strip_idx = lax.rem(p + shift + 128, 128)
    first, upper = lane8 < 64, upper_lanes(8)

    def strip_tile(row):
        rows = slice(row, row + 8)

        def gather(x):
            return jnp.take_along_axis(x, strip_idx, axis=1)

        def halves(ref, k):
            return jnp.where(upper, gather(ref[k, rows, :]), gather(ref[k + half, rows, :]))

        for k in range(half):
            e_tr[k, rows, :] = jnp.where(first, halves(tr.at[0], k), halves(tr.at[1], k))
            e_u[k, rows, :] = halves(u, k)
            e_v[k, rows, :] = halves(v, k)
        e_floor[rows, :] = gather(floor[rows, :]) - jnp.where(upper, 0.0, float(half))

    q_t = jnp.logical_and(p >= 12, p < 20)
    q_u = jnp.logical_and(p >= 20, p < 28)
    for row in (8, 16):
        strip_tile(row)
        rows = slice(row, row + 8)
        for k in range(half):
            strip_out[k, row - 8 : row, :] = jnp.where(
                q_t, e_tr[k, rows, :],
                jnp.where(q_u, pltpu.roll(e_u[k, rows, :], 8, 1), pltpu.roll(e_v[k, rows, :], 16, 1)),
            )
        strip_out[half, row - 8 : row, :] = e_floor[rows, :]

    pl.semaphore_wait(barrier, jnp.where(at_south, 3, 4))

    def tell(slot, where):
        pl.semaphore_signal(ready.at[slot], inc=1, device_id=where, device_id_type=MESH)

    pl.when(jnp.logical_not(at_south))(lambda: tell(0, to_south))
    pl.when(jnp.logical_not(at_north))(lambda: tell(1, to_north))
    pl.when(at_north)(lambda: tell(0, to_fold))

    def send(src, dst, role, slot, where):
        return pltpu.make_async_remote_copy(
            src_ref=src, dst_ref=dst, send_sem=send_sem.at[role], recv_sem=recv_sem.at[slot],
            device_id=where, device_id_type=MESH,
        )

    rows_north = send(row_out.at[0], row_in.at[1], NORTH, SOUTH, to_north)
    rows_fold = send(row_out.at[0], row_in.at[0], NORTH, NORTH, to_fold)
    rows_south = send(row_out.at[1], row_in.at[0], SOUTH, NORTH, to_south)
    strip_west = send(strip_out, strip_in.at[0], WEST, EAST, to_west)
    strip_east = send(strip_out, strip_in.at[1], EAST, WEST, to_east)

    def corner(src, role, slot, where):
        return send(src, corner_in.at[CORNER[slot]], role, slot, where)

    upper_rows, lower_rows = strip_out.at[:, 8:16, :], strip_out.at[:, 0:8, :]
    corners_north = (corner(upper_rows, NE, SW, (east, lat + 1)), corner(upper_rows, NW, SE, (west, lat + 1)))
    corners_south = (corner(lower_rows, SE, NW, (east, lat - 1)), corner(lower_rows, SW, NE, (west, lat - 1)))
    corners_fold = (
        (corner(fold_out, NE, NE, (fold_ne, lat)), pltpu.make_async_copy(fold_out, corner_in.at[CORNER[NE]], send_sem.at[NE]), ne_self),
        (corner(fold_out, NW, NW, (fold_nw, lat)), pltpu.make_async_copy(fold_out, corner_in.at[CORNER[NW]], send_sem.at[NW]), nw_self),
    )

    strip_west.start()
    strip_east.start()

    fields = ((tr.at[0], tr.at[1]), (u, v))
    for side_no, row in ((0, 20), (1, 8)):
        for g, (a, b) in enumerate(fields):
            for k in range(nk):
                row_out[side_no, g * nk + k, 0:4, :] = a[k, row : row + 4, :]
                row_out[side_no, g * nk + k, 4:8, :] = b[k, row : row + 4, :]
        row_out[side_no, 2 * nk, 0:4, :] = floor[row : row + 4, :]

    @pl.when(at_north)
    def _():
        for k in range(2 * nk + 1):
            x = jnp.take_along_axis(row_out[0, k], 127 - lane8, axis=1)
            x = jnp.take_along_axis(x, 3 - lax.rem(sub8, 4) + jnp.where(sub8 < 4, 0, 4), axis=0)
            row_out[0, k] = -x if nk <= k < 2 * nk else x

    @pl.when(jnp.logical_not(at_south))
    def _():
        rows_south.start()

    @pl.when(jnp.logical_not(at_north))
    def _():
        rows_north.start()

    @pl.when(at_north)
    def _():
        rows_fold.start()

    @pl.when(jnp.logical_not(at_south))
    def _():
        pl.semaphore_wait(ready.at[1], 1)
        for copy in corners_south:
            copy.start()

    pl.semaphore_wait(ready.at[0], 1)

    @pl.when(jnp.logical_not(at_north))
    def _():
        for copy in corners_north:
            copy.start()

    @pl.when(at_north)
    def _():
        group_idx = lax.rem(lane8 + 7 - 2 * lax.rem(lane8 + 4, 8) + 128, 128)
        sign = jnp.where(q_t, 1.0, -1.0)
        for k in range(half + 1):
            x = jnp.take_along_axis(strip_out[k, 8:16, :], group_idx, axis=1)
            x = jnp.take_along_axis(x, 7 - sub8, axis=0)
            fold_out[k] = x if k == half else x * sign
        for copy, local, own in corners_fold:
            pl.when(own)(local.start)
            pl.when(jnp.logical_not(own))(copy.start)

    main = dict(
        split=False, t=[tr.at[0], tr.at[1]], u=u, v=v, f=floor,
        density=lambda pair: haline_coef * pair[1] - thermal_coef * pair[0],
    )
    names = dict(low=low, mx=mx, mn=mn, ax=ax, ay=ay, az=az, rin=rin, rout=rout, adv=adv)
    main.update({name: [ref.at[0], ref.at[1]] for name, ref in names.items()})

    outs = (t_out, s_out)

    stage_flux(main, [(8, 16, 0, 16)])
    stage_ratio(main, [(8, 16, 0, 16)])
    stage_limit(main, [(8, 16, 0, 16)])

    def emit_inner(k, wi, m, val):
        outs[m][k, 4:12, :] = val[4:12]

    stage_diffuse(main, [(8, 16, 4, 12)], emit_inner)

    strip_west.wait()
    strip_east.wait()
    from_east = lax.rem(lane8, 8) >= 4

    def strip_halo(row, east_ref, west_ref, at):
        rows = slice(row, row + 8)
        for k in range(half + 1):
            x = jnp.where(from_east, east_ref[k, at : at + 8, :], west_ref[k, at : at + 8, :])
            if k == half:
                e_floor[rows, :] = jnp.where(q_t, x, e_floor[rows, :])
                continue
            e_tr[k, rows, :] = jnp.where(q_t, x, e_tr[k, rows, :])
            e_u[k, rows, :] = jnp.where(q_t, pltpu.roll(x, 120, 1), e_u[k, rows, :])
            e_v[k, rows, :] = jnp.where(q_t, pltpu.roll(x, 112, 1), e_v[k, rows, :])

    strip_halo(8, strip_in.at[0], strip_in.at[1], 0)
    strip_halo(16, strip_in.at[0], strip_in.at[1], 8)

    @pl.when(at_south)
    def _():
        row_in[1] = jnp.zeros(row_in.shape[1:], jnp.float32)
        for slot in (SE, SW):
            corner_in[CORNER[slot]] = jnp.zeros(corner_in.shape[1:], jnp.float32)

    @pl.when(jnp.logical_not(at_south))
    def _():
        rows_south.wait_send()
        rows_north.wait_recv()

    @pl.when(jnp.logical_not(at_north))
    def _():
        rows_north.wait_send()
        rows_south.wait_recv()

    @pl.when(at_north)
    def _():
        rows_fold.wait()

    for slot, row in ((1, 4), (0, 24)):
        for g, (a, b) in enumerate(fields):
            for k in range(nk):
                a[k, row : row + 4, :] = row_in[slot, g * nk + k, 0:4, :]
                b[k, row : row + 4, :] = row_in[slot, g * nk + k, 4:8, :]
        floor[row : row + 4, :] = row_in[slot, 2 * nk, 0:4, :]

    stage_flux(main, [(4, 8, 1, 5), (20, 8, 3, 7)])
    stage_ratio(main, [(4, 8, 2, 6), (20, 8, 2, 6)])
    stage_limit(main, [(4, 8, 3, 7), (20, 8, 1, 5)])

    def emit_outer(k, wi, m, val):
        if wi == 0:
            outs[m][k, 0:4, :] = val[4:8]
        else:
            outs[m][k, 12:16, :] = val[4:8]

    stage_diffuse(main, [(4, 8, 4, 8), (16, 8, 4, 8)], emit_outer)

    strip_tile(0)
    strip_tile(24)

    @pl.when(jnp.logical_not(at_south))
    def _():
        for copy in corners_south:
            copy.wait_send()
        for copy in corners_north:
            copy.wait_recv()

    @pl.when(jnp.logical_not(at_north))
    def _():
        for copy in corners_north:
            copy.wait_send()
        for copy in corners_south:
            copy.wait_recv()

    @pl.when(at_north)
    def _():
        for copy, local, own in corners_fold:
            pl.when(own)(local.wait)
            pl.when(jnp.logical_not(own))(copy.wait)

    strip_halo(0, corner_in.at[CORNER[SE]], corner_in.at[CORNER[SW]], 0)
    strip_halo(24, corner_in.at[CORNER[NE]], corner_in.at[CORNER[NW]], 0)

    def strip_density(one):
        x = one[0]
        low_half = lane_iota(x.shape[0]) < 64
        own = jnp.where(low_half, -thermal_coef, haline_coef)
        other = jnp.where(low_half, haline_coef, -thermal_coef)
        return own * x + other * pltpu.roll(x, 64, 1)

    strips = dict(split=True, t=[e_tr], u=e_u, v=e_v, f=e_floor, density=strip_density)
    names = dict(low=e_low, mx=e_mx, mn=e_mn, ax=e_ax, ay=e_ay, az=e_az, rin=e_rin, rout=e_rout, adv=e_adv)
    strips.update({name: [ref] for name, ref in names.items()})
    stage_flux(strips, [(4, 24, 0, 24)])
    stage_ratio(strips, [(4, 24, 0, 24)])
    stage_limit(strips, [(4, 24, 0, 24)])

    def emit_strip(k, wi, m, val, add=False):
        e_res[k] = e_res[k] + val[4:20] if add else val[4:20]

    stage_diffuse(strips, [(4, 24, 4, 20)], emit_strip)


def finish(t_ref, s_ref, e_res, t_hbm, s_hbm, t_buf, s_buf, sem):
    lane16 = lane_iota(16)
    rim = jnp.logical_or(lane16 < 4, lane16 >= 124)
    copies = []
    for m, (ref, buf, out) in enumerate(((t_ref, t_buf, t_hbm), (s_ref, s_buf, s_hbm))):
        back = jnp.where(lane16 < 4, lane16 + 20, jnp.where(lane16 >= 124, lane16 - 116, 0)) + 64 * m
        half = e_res.shape[0]
        for k in range(ref.shape[0]):
            edge = jnp.take_along_axis(e_res[k % half], back + 32 * (k // half), axis=1)
            buf[k] = jnp.where(rim, edge, ref[k])
        copies.append(pltpu.make_async_copy(buf, out, sem.at[m]))
        copies[-1].start()
    for copy in copies:
        copy.wait()


def on_device(t, s, u, v, flag, point, count):
    nk = t.shape[0]
    f32 = jnp.float32
    vm = lambda *shape: pltpu.VMEM(shape, f32)
    big = lambda: vm(2, nk, 32, 128)
    one = lambda: vm(nk, 32, 128)
    whole = pl.BlockSpec(memory_space=pltpu.VMEM)
    hbm = pl.BlockSpec(memory_space=pltpu.HBM)
    part = pltpu.VMEM(t.shape, f32)
    main_t, main_s, strips = pl.pallas_call(
        kernel,
        out_shape=(part, part, pltpu.VMEM((nk // 2, *t.shape[1:]), f32)),
        in_specs=[hbm] * 7,
        out_specs=(whole, whole, whole),
        scratch_shapes=[
            pltpu.VMEM(flag.shape, flag.dtype), pltpu.VMEM(point.shape, point.dtype), pltpu.VMEM(count.shape, count.dtype),
            big(), one(), one(), vm(32, 128),
            *[big() for _ in range(9)],
            *[vm(nk // 2, 32, 128) for _ in range(3)], vm(32, 128),
            *[vm(nk // 2, 32, 128) for _ in range(9)],
            vm(2, 2 * nk + 1, 8, 128), vm(2, 2 * nk + 1, 8, 128),
            vm(nk // 2 + 1, 16, 128), vm(2, nk // 2 + 1, 16, 128),
            vm(nk // 2 + 1, 8, 128), vm(4, nk // 2 + 1, 8, 128),
            pltpu.SemaphoreType.DMA((7,)), pltpu.SemaphoreType.DMA((8,)), pltpu.SemaphoreType.DMA((8,)),
            pltpu.SemaphoreType.REGULAR((2,)),
        ],
        compiler_params=pltpu.CompilerParams(
            collective_id=0, has_side_effects=True, vmem_limit_bytes=60 * 1024 * 1024
        ),
    )(t, s, u, v, flag, point, count)
    result = jax.ShapeDtypeStruct(t.shape, f32)
    return pl.pallas_call(
        finish,
        out_shape=(result, result),
        in_specs=[whole] * 3,
        out_specs=(hbm, hbm),
        scratch_shapes=[vm(*t.shape), vm(*t.shape), pltpu.SemaphoreType.DMA((2,))],
        compiler_params=pltpu.CompilerParams(vmem_limit_bytes=4 * 1024 * 1024),
    )(main_t, main_s, strips)


def solution(mesh):
    grid = P(None, "lat", "lon")
    flat = P("lat", "lon")
    return jax.shard_map(
        on_device, mesh=mesh, in_specs=(grid,) * 4 + (flat,) * 3, out_specs=(grid, grid), check_vma=False
    )
```

```python
import functools

import jax
import jax.numpy as jnp
from jax import lax
from jax.experimental import pallas as pl
from jax.experimental.pallas import tpu as pltpu
from jax.sharding import PartitionSpec as P

time_step = 0.5
diffusivity = 0.1
strat_floor = 0.5
slope_limit = 2.0
thermal_coef = 0.2
haline_coef = 0.8

MESH = pl.DeviceIdType.MESH
INF = float("inf")
TINY = 1e-37
FACE_SCALE = 0.25 * time_step
DIFF_SCALE = 0.25 * time_step * diffusivity

EAST, WEST, NORTH, SOUTH, NE, NW, SE, SW = range(8)
CORNER = {NE: 0, NW: 1, SE: 2, SW: 3}


def east_of(x):
    return pltpu.roll(x, x.shape[1] - 1, 1)


def west_of(x):
    return pltpu.roll(x, 1, 1)


def south_of(x):
    return pltpu.roll(x, 1, 0)


def lane_iota(rows):
    return lax.broadcasted_iota(jnp.int32, (rows, 128), 1)


def upper_lanes(rows):
    return lax.rem(lane_iota(rows), 64) < 32


def to_upper(x):
    return jnp.where(upper_lanes(x.shape[0]), pltpu.roll(x, 96, 1), 0.0)


def to_lower(x):
    return jnp.where(upper_lanes(x.shape[0]), 0.0, pltpu.roll(x, 32, 1))


def above(z, ref, k, r0, n):
    if not z["split"]:
        return ref[jnp.maximum(k - 1, 0), r0 : r0 + n, :]
    if k > 0:
        return ref[k - 1, r0 : r0 + n, :]
    last = z["u"].shape[0] - 1
    return jnp.where(upper_lanes(n), ref[0, r0 : r0 + n, :], pltpu.roll(ref[last, r0 : r0 + n, :], 32, 1))


def below(z, ref, k, r0, n):
    last = z["u"].shape[0] - 1
    if not z["split"]:
        return ref[jnp.minimum(k + 1, last), r0 : r0 + n, :]
    if k < last:
        return ref[k + 1, r0 : r0 + n, :]
    return jnp.where(upper_lanes(n), pltpu.roll(ref[0, r0 : r0 + n, :], 96, 1), ref[last, r0 : r0 + n, :])


def upward(z, body, carry):
    nk = z["u"].shape[0]
    if z["split"]:
        for k in range(nk - 1, -1, -1):
            carry = body(k, jnp.float32(k), carry)
        return carry

    def step(i, carry):
        k = nk - 1 - i
        return body(k, k.astype(jnp.float32), carry)

    return lax.fori_loop(0, nk, step, carry, unroll=nk // 2)


def nothing(z, wins):
    return tuple(tuple(jnp.zeros((n, 128), jnp.float32) for _ in z["t"]) for _, n, _, _ in wins)


def stage_flux(z, wins):
    nk = z["u"].shape[0]
    stat = []
    for r0, n, _, _ in wins:
        f = z["f"][r0 : r0 + n, :]
        f_e = jnp.minimum(f, east_of(f))
        f_n = jnp.minimum(f, z["f"][r0 + 1 : r0 + 1 + n, :])
        stat.append((f, f_e, f_n))

    def velocities(k, kk, r0, n, f_e, f_n):
        u = z["u"][k, r0 : r0 + n, :]
        u_e = jnp.where(kk < f_e, FACE_SCALE * (u + east_of(u)), 0.0)
        v = z["v"][k, r0 : r0 + n, :]
        v_n = jnp.where(kk < f_n, FACE_SCALE * (v + z["v"][k, r0 + 1 : r0 + 1 + n, :]), 0.0)
        return u_e, v_n, u_e - west_of(u_e) + v_n - south_of(v_n)

    def body(k, kk, carry):
        out = []
        for (r0, n, lo, hi), (f, f_e, f_n), (w_old, bottoms) in zip(wins, stat, carry):
            u_e, v_n, gain = velocities(k, kk, r0, n, f_e, f_n)
            w = w_old - gain
            abs_u, abs_v, abs_w = jnp.abs(u_e), jnp.abs(v_n), jnp.abs(w)
            wet = kk < f
            tops = []
            for m, t in enumerate(z["t"]):
                c = t[k, r0 : r0 + n, :]
                e = east_of(c)
                nn = t[k, r0 + 1 : r0 + 1 + n, :]
                up = above(z, t, k, r0, n)
                a_e = abs_u * (e - c)
                l_e = u_e * (c + e) - a_e
                a_n = abs_v * (nn - c)
                l_n = v_n * (c + nn) - a_n
                a_t = abs_w * (up - c)
                l_t = w * (c + up) - a_t
                low = c - ((l_e - west_of(l_e)) + (l_n - south_of(l_n)) + (l_t - bottoms[m]))
                low = jnp.where(wet, low, 0.0)
                big = jnp.where(wet, jnp.maximum(c, low), -INF)
                small = jnp.where(wet, jnp.minimum(c, low), INF)
                for name, val in (("ax", a_e), ("ay", a_n), ("az", a_t), ("low", low), ("mx", big), ("mn", small)):
                    z[name][m][k, r0 + lo : r0 + hi, :] = val[lo:hi]
                tops.append(l_t)
            out.append((w, tuple(tops)))
        return tuple(out)

    start = []
    for (r0, n, _, _), (f, f_e, f_n) in zip(wins, stat):
        w = jnp.zeros((n, 128), jnp.float32)
        flows = tuple(w for _ in z["t"])
        if z["split"]:
            for k in range(nk):
                w = w - velocities(k, jnp.float32(k), r0, n, f_e, f_n)[2]
            w = to_upper(w)
            flows = []
            for t in z["t"]:
                up, c = t[nk - 1, r0 : r0 + n, :], below(z, t, nk - 1, r0, n)
                flows.append(w * (c + up) - jnp.abs(w) * (up - c))
        start.append((w, tuple(flows)))
    upward(z, body, tuple(start))


def stage_ratio(z, wins):
    nk = z["u"].shape[0]

    def body(k, kk, carry):
        out = []
        for (r0, n, lo, hi), bottoms in zip(wins, carry):
            tops = []
            for m in range(len(z["t"])):
                def near(ref, pick):
                    c = ref[k, r0 : r0 + n, :]
                    horizontal = pick(pick(east_of(c), west_of(c)), pick(ref[k, r0 + 1 : r0 + 1 + n, :], ref[k, r0 - 1 : r0 - 1 + n, :]))
                    return pick(pick(c, horizontal), pick(above(z, ref, k, r0, n), below(z, ref, k, r0, n)))

                big, small = near(z["mx"][m], jnp.maximum), near(z["mn"][m], jnp.minimum)
                low = z["low"][m][k, r0 : r0 + n, :]
                a_e = z["ax"][m][k, r0 : r0 + n, :]
                a_w = west_of(a_e)
                a_n = z["ay"][m][k, r0 : r0 + n, :]
                a_s = z["ay"][m][k, r0 - 1 : r0 - 1 + n, :]
                a_t, a_b = z["az"][m][k, r0 : r0 + n, :], bottoms[m]
                p_in, p_out = 0.0, 0.0
                for inward, outward in ((a_w, a_e), (a_s, a_n), (a_b, a_t)):
                    p_in = p_in + (jnp.maximum(inward, 0.0) - jnp.minimum(outward, 0.0))
                    p_out = p_out + (jnp.maximum(outward, 0.0) - jnp.minimum(inward, 0.0))
                r_in = jnp.clip((big - low) * pl.reciprocal(jnp.maximum(p_in, TINY)), 0.0, 1.0)
                r_out = jnp.clip((low - small) * pl.reciprocal(jnp.maximum(p_out, TINY)), 0.0, 1.0)
                z["rin"][m][k, r0 + lo : r0 + hi, :] = r_in[lo:hi]
                z["rout"][m][k, r0 + lo : r0 + hi, :] = r_out[lo:hi]
                tops.append(a_t)
            out.append(tuple(tops))
        return tuple(out)

    start = nothing(z, wins)
    if z["split"]:
        start = tuple(tuple(to_upper(a[0, r0 : r0 + n, :]) for a in z["az"]) for r0, n, _, _ in wins)
    upward(z, body, start)


def limited(anti, r_in, r_out, far_in, far_out):
    return anti * jnp.where(anti >= 0, jnp.minimum(far_in, r_out), jnp.minimum(r_in, far_out))


def stage_limit(z, wins):
    nk = z["u"].shape[0]
    stat = [z["f"][r0 : r0 + n, :] for r0, n, _, _ in wins]

    def rise(m, k, r0, n):
        r_in, r_out = z["rin"][m][k, r0 : r0 + n, :], z["rout"][m][k, r0 : r0 + n, :]
        far_in, far_out = above(z, z["rin"][m], k, r0, n), above(z, z["rout"][m], k, r0, n)
        return limited(z["az"][m][k, r0 : r0 + n, :], r_in, r_out, far_in, far_out)

    def body(k, kk, carry):
        out = []
        for (r0, n, lo, hi), f, bottoms in zip(wins, stat, carry):
            tops = []
            for m in range(len(z["t"])):
                r_in, r_out = z["rin"][m][k, r0 : r0 + n, :], z["rout"][m][k, r0 : r0 + n, :]
                f_e = limited(z["ax"][m][k, r0 : r0 + n, :], r_in, r_out, east_of(r_in), east_of(r_out))
                f_n = limited(
                    z["ay"][m][k, r0 : r0 + n, :], r_in, r_out,
                    z["rin"][m][k, r0 + 1 : r0 + 1 + n, :], z["rout"][m][k, r0 + 1 : r0 + 1 + n, :],
                )
                f_t = rise(m, k, r0, n)
                low = z["low"][m][k, r0 : r0 + n, :]
                new = low - ((f_e - west_of(f_e)) + (f_n - south_of(f_n)) + (f_t - bottoms[m]))
                new = jnp.where(kk < f, new, 0.0)
                z["adv"][m][k, r0 + lo : r0 + hi, :] = new[lo:hi]
                tops.append(f_t)
            out.append(tuple(tops))
        return tuple(out)

    start = nothing(z, wins)
    if z["split"]:
        start = tuple(tuple(to_upper(rise(m, 0, r0, n)) for m in range(len(z["t"]))) for r0, n, _, _ in wins)
    upward(z, body, start)


def clip_slope(x):
    return jnp.clip(x, -slope_limit, slope_limit)


def stage_diffuse(z, wins, emit):
    nk = z["u"].shape[0]
    dens = z["density"]
    nt = len(z["t"])
    stat = []
    for r0, n, _, _ in wins:
        f = z["f"][r0 : r0 + n, :]
        far_e, far_n = east_of(f), z["f"][r0 + 1 : r0 + 1 + n, :]
        stat.append((f, far_e, far_n, jnp.minimum(f, far_e), jnp.minimum(f, far_n)))

    def inverse(grads):
        return pl.reciprocal(jnp.maximum(-dens(grads), strat_floor))

    def vertical(k, kk, r0, n, f, far_n):
        gz = [jnp.where(kk < f, above(z, a, k, r0, n) - a[k, r0 : r0 + n, :], 0.0) for a in z["adv"]]
        gz_n = [jnp.where(kk < far_n, above(z, a, k, r0 + 1, n) - a[k, r0 + 1 : r0 + 1 + n, :], 0.0) for a in z["adv"]]
        inv = inverse(gz)
        return inv, east_of(inv), inverse(gz_n), tuple(gz), tuple(east_of(g) for g in gz), tuple(gz_n)

    def body(k, kk, carry):
        out = []
        for wi, ((r0, n, _, _), (f, far_e, far_n, f_e, f_n), old) in enumerate(zip(wins, stat, carry)):
            if not z["split"]:
                not_top = (k >= 1).astype(jnp.float32)
            elif k == 0:
                not_top = jnp.where(upper_lanes(n), 0.0, 1.0)
            here = [a[k, r0 : r0 + n, :] for a in z["adv"]]
            north = [a[k, r0 + 1 : r0 + 1 + n, :] for a in z["adv"]]
            inv, inv_e, inv_n, gz, gz_e, gz_n = vertical(k, kk, r0, n, f, far_n)
            gx = [jnp.where(kk < f_e, east_of(c) - c, 0.0) for c in here]
            gy = [jnp.where(kk < f_n, b - c, 0.0) for b, c in zip(north, here)]
            rx, ry = dens(gx), dens(gy)
            (o_inv, o_inv_e, o_inv_n, o_gz, o_gz_e, o_gz_n), o_part, o_top = old
            low_here, low_e, low_n = kk + 1.0 < f, kk + 1.0 < far_e, kk + 1.0 < far_n
            s_x = [clip_slope(rx * q) for q in (inv, inv_e, o_inv, o_inv_e)]
            s_y = [clip_slope(ry * q) for q in (inv, inv_n, o_inv, o_inv_n)]
            parts, tops = [], []
            for m in range(nt):
                gx_top, gy_top = gx[m], gy[m]
                if not z["split"] or k == 0:
                    gx_top, gy_top = gx_top * not_top, gy_top * not_top
                hx = (
                    gx_top + s_x[0] * gz[m],
                    gx_top + s_x[1] * gz_e[m],
                    jnp.where(low_here, gx[m], 0.0) + s_x[2] * o_gz[m],
                    jnp.where(low_e, gx[m], 0.0) + s_x[3] * o_gz_e[m],
                )
                hy = (
                    gy_top + s_y[0] * gz[m],
                    gy_top + s_y[1] * gz_n[m],
                    jnp.where(low_here, gy[m], 0.0) + s_y[2] * o_gz[m],
                    jnp.where(low_n, gy[m], 0.0) + s_y[3] * o_gz_n[m],
                )
                flux_e = (hx[0] + hx[1]) + (hx[2] + hx[3])
                flux_n = (hy[0] + hy[1]) + (hy[2] + hy[3])
                top = (s_x[0] * hx[0] + west_of(s_x[1] * hx[1])) + (s_y[0] * hy[0] + south_of(s_y[1] * hy[1]))
                bottom = (s_x[2] * hx[2] + west_of(s_x[3] * hx[3])) + (s_y[2] * hy[2] + south_of(s_y[3] * hy[3]))
                rise = o_top[m] + bottom
                if z["split"] and k == nk - 1:
                    bottom_lower[wi, m] = to_lower(bottom)
                else:
                    done = jnp.where(kk + 1.0 < f, o_part[m] + DIFF_SCALE * rise, 0.0)
                    emit(k + 1 if z["split"] else jnp.minimum(k + 1, nk - 1), wi, m, done)
                parts.append(here[m] + DIFF_SCALE * ((flux_e - west_of(flux_e)) + (flux_n - south_of(flux_n)) - rise))
                tops.append(top)
            out.append(((inv, inv_e, inv_n, gz, gz_e, gz_n), tuple(parts), tuple(tops)))
        return tuple(out)

    bottom_lower = {}
    start = []
    for (r0, n, _, _), (f, _, far_n, *_) in zip(wins, stat):
        x = jnp.zeros((n, 128), jnp.float32)
        xs = tuple(x for _ in range(nt))
        first = (x, x, x, xs, xs, xs)
        if z["split"]:
            first = jax.tree.map(to_upper, vertical(0, jnp.float32(0), r0, n, f, far_n))
        start.append((first, xs, xs))
    last = upward(z, body, tuple(start))
    for wi, ((r0, n, _, _), (f, *_), (_, parts, tops)) in enumerate(zip(wins, stat, last)):
        for m in range(nt):
            top = tops[m]
            if z["split"]:
                top = top + bottom_lower[wi, m]
                late = jnp.where(nk - 1.0 < f, -DIFF_SCALE * to_upper(tops[m]), 0.0)
                emit(nk - 1, wi, m, late, True)
            emit(0, wi, m, jnp.where(0.0 < f, parts[m] + DIFF_SCALE * top, 0.0))


def kernel(
    t_hbm, s_hbm, u_hbm, v_hbm, flag_hbm, point_hbm, count_hbm,
    t_out, s_out, e_res,
    flag_ref, point_ref, count_ref, tr, u, v, floor, low, mx, mn, ax, ay, az, rin, rout, adv,
    e_tr, e_u, e_v, e_floor, e_low, e_mx, e_mn, e_ax, e_ay, e_az, e_rin, e_rout, e_adv,
    row_out, row_in, strip_out, strip_in, fold_out, corner_in,
    load_sem, send_sem, recv_sem, ready,
):
    n_lon, n_lat = lax.axis_size("lon"), lax.axis_size("lat")
    lon, lat = lax.axis_index("lon"), lax.axis_index("lat")
    nk = u.shape[0]
    half = nk // 2
    east, west = lax.rem(lon + 1, n_lon), lax.rem(lon + n_lon - 1, n_lon)
    at_north, at_south = lat == n_lat - 1, lat == 0
    to_east, to_west = (east, lat), (west, lat)
    above_lat, below_lat = lax.rem(lat + 1, n_lat), lax.rem(lat + n_lat - 1, n_lat)
    to_north, to_south, to_fold = (lon, above_lat), (lon, below_lat), (n_lon - 1 - lon, lat)
    fold_ne, fold_nw = lax.rem(2 * n_lon - 2 - lon, n_lon), lax.rem(n_lon - lon, n_lon)
    ne_self, nw_self = fold_ne == lon, fold_nw == lon

    barrier = pltpu.get_barrier_semaphore()

    def greet(where):
        pl.semaphore_signal(barrier, inc=1, device_id=where, device_id_type=MESH)

    greet(to_east)
    greet(to_west)

    @pl.when(jnp.logical_not(at_south))
    def _():
        greet(to_south)

    @pl.when(jnp.logical_not(at_north))
    def _():
        greet(to_north)

    @pl.when(at_north)
    def _():
        greet(to_fold)

    loads = [
        pltpu.make_async_copy(src, dst.at[:, 8:24, :], load_sem.at[i])
        for i, (src, dst) in enumerate(((t_hbm, tr.at[0]), (s_hbm, tr.at[1]), (u_hbm, u), (v_hbm, v)))
    ]
    loads += [
        pltpu.make_async_copy(src, dst, load_sem.at[4 + i])
        for i, (src, dst) in enumerate(((flag_hbm, flag_ref), (point_hbm, point_ref), (count_hbm, count_ref)))
    ]
    for copy in loads:
        copy.start()
    for copy in loads:
        copy.wait()
    floor[8:24, :] = (count_ref[...] * point_ref[...] * flag_ref[...]).astype(jnp.float32)

    lane8, sub8 = lane_iota(8), lax.broadcasted_iota(jnp.int32, (8, 128), 0)

    p = lax.rem(lane8, 32)
    shift = jnp.where(p < 12, 116, jnp.where(p < 16, -12, jnp.where(p < 20, 108, -20)))
    strip_idx = lax.rem(p + shift + 128, 128)
    first, upper = lane8 < 64, upper_lanes(8)

    def strip_tile(row):
        rows = slice(row, row + 8)

        def gather(x):
            return jnp.take_along_axis(x, strip_idx, axis=1)

        def halves(ref, k):
            return jnp.where(upper, gather(ref[k, rows, :]), gather(ref[k + half, rows, :]))

        for k in range(half):
            e_tr[k, rows, :] = jnp.where(first, halves(tr.at[0], k), halves(tr.at[1], k))
            e_u[k, rows, :] = halves(u, k)
            e_v[k, rows, :] = halves(v, k)
        e_floor[rows, :] = gather(floor[rows, :]) - jnp.where(upper, 0.0, float(half))

    q_t = jnp.logical_and(p >= 12, p < 20)
    q_u = jnp.logical_and(p >= 20, p < 28)
    for row in (8, 16):
        strip_tile(row)
        rows = slice(row, row + 8)
        for k in range(half):
            strip_out[k, row - 8 : row, :] = jnp.where(
                q_t, e_tr[k, rows, :],
                jnp.where(q_u, pltpu.roll(e_u[k, rows, :], 8, 1), pltpu.roll(e_v[k, rows, :], 16, 1)),
            )
        strip_out[half, row - 8 : row, :] = e_floor[rows, :]

    pl.semaphore_wait(barrier, jnp.where(at_south, 3, 4))

    def tell(slot, where):
        pl.semaphore_signal(ready.at[slot], inc=1, device_id=where, device_id_type=MESH)

    pl.when(jnp.logical_not(at_south))(lambda: tell(0, to_south))
    pl.when(jnp.logical_not(at_north))(lambda: tell(1, to_north))
    pl.when(at_north)(lambda: tell(0, to_fold))

    def send(src, dst, role, slot, where):
        return pltpu.make_async_remote_copy(
            src_ref=src, dst_ref=dst, send_sem=send_sem.at[role], recv_sem=recv_sem.at[slot],
            device_id=where, device_id_type=MESH,
        )

    rows_north = send(row_out.at[0], row_in.at[1], NORTH, SOUTH, to_north)
    rows_fold = send(row_out.at[0], row_in.at[0], NORTH, NORTH, to_fold)
    rows_south = send(row_out.at[1], row_in.at[0], SOUTH, NORTH, to_south)
    strip_west = send(strip_out, strip_in.at[0], WEST, EAST, to_west)
    strip_east = send(strip_out, strip_in.at[1], EAST, WEST, to_east)

    def corner(src, role, slot, where):
        return send(src, corner_in.at[CORNER[slot]], role, slot, where)

    upper_rows, lower_rows = strip_out.at[:, 8:16, :], strip_out.at[:, 0:8, :]
    corners_north = (corner(upper_rows, NE, SW, (east, above_lat)), corner(upper_rows, NW, SE, (west, above_lat)))
    corners_south = (corner(lower_rows, SE, NW, (east, below_lat)), corner(lower_rows, SW, NE, (west, below_lat)))
    corners_fold = (
        (corner(fold_out, NE, NE, (fold_ne, lat)), pltpu.make_async_copy(fold_out, corner_in.at[CORNER[NE]], send_sem.at[NE]), ne_self),
        (corner(fold_out, NW, NW, (fold_nw, lat)), pltpu.make_async_copy(fold_out, corner_in.at[CORNER[NW]], send_sem.at[NW]), nw_self),
    )

    strip_west.start()
    strip_east.start()

    fields = ((tr.at[0], tr.at[1]), (u, v))
    for side_no, row in ((0, 20), (1, 8)):
        for g, (a, b) in enumerate(fields):
            for k in range(nk):
                row_out[side_no, g * nk + k, 0:4, :] = a[k, row : row + 4, :]
                row_out[side_no, g * nk + k, 4:8, :] = b[k, row : row + 4, :]
        row_out[side_no, 2 * nk, 0:4, :] = floor[row : row + 4, :]

    @pl.when(at_north)
    def _():
        for k in range(2 * nk + 1):
            x = jnp.take_along_axis(row_out[0, k], 127 - lane8, axis=1)
            x = jnp.take_along_axis(x, 3 - lax.rem(sub8, 4) + jnp.where(sub8 < 4, 0, 4), axis=0)
            row_out[0, k] = -x if nk <= k < 2 * nk else x

    @pl.when(jnp.logical_not(at_south))
    def _():
        rows_south.start()

    @pl.when(jnp.logical_not(at_north))
    def _():
        rows_north.start()

    @pl.when(at_north)
    def _():
        rows_fold.start()

    @pl.when(jnp.logical_not(at_south))
    def _():
        pl.semaphore_wait(ready.at[1], 1)
        for copy in corners_south:
            copy.start()

    pl.semaphore_wait(ready.at[0], 1)

    @pl.when(jnp.logical_not(at_north))
    def _():
        for copy in corners_north:
            copy.start()

    @pl.when(at_north)
    def _():
        group_idx = lax.rem(lane8 + 7 - 2 * lax.rem(lane8 + 4, 8) + 128, 128)
        sign = jnp.where(q_t, 1.0, -1.0)
        for k in range(half + 1):
            x = jnp.take_along_axis(strip_out[k, 8:16, :], group_idx, axis=1)
            x = jnp.take_along_axis(x, 7 - sub8, axis=0)
            fold_out[k] = x if k == half else x * sign
        for copy, local, own in corners_fold:
            pl.when(own)(local.start)
            pl.when(jnp.logical_not(own))(copy.start)

    main = dict(
        split=False, t=[tr.at[0], tr.at[1]], u=u, v=v, f=floor,
        density=lambda pair: haline_coef * pair[1] - thermal_coef * pair[0],
    )
    names = dict(low=low, mx=mx, mn=mn, ax=ax, ay=ay, az=az, rin=rin, rout=rout, adv=adv)
    main.update({name: [ref.at[0], ref.at[1]] for name, ref in names.items()})

    outs = (t_out, s_out)

    stage_flux(main, [(8, 16, 0, 16)])
    stage_ratio(main, [(8, 16, 0, 16)])
    stage_limit(main, [(8, 16, 0, 16)])

    def emit_inner(k, wi, m, val):
        outs[m][k, 4:12, :] = val[4:12]

    stage_diffuse(main, [(8, 16, 4, 12)], emit_inner)

    strip_west.wait()
    strip_east.wait()
    from_east = lax.rem(lane8, 8) >= 4

    def strip_halo(row, east_ref, west_ref, at):
        rows = slice(row, row + 8)
        for k in range(half + 1):
            x = jnp.where(from_east, east_ref[k, at : at + 8, :], west_ref[k, at : at + 8, :])
            if k == half:
                e_floor[rows, :] = jnp.where(q_t, x, e_floor[rows, :])
                continue
            e_tr[k, rows, :] = jnp.where(q_t, x, e_tr[k, rows, :])
            e_u[k, rows, :] = jnp.where(q_t, pltpu.roll(x, 120, 1), e_u[k, rows, :])
            e_v[k, rows, :] = jnp.where(q_t, pltpu.roll(x, 112, 1), e_v[k, rows, :])

    strip_halo(8, strip_in.at[0], strip_in.at[1], 0)
    strip_halo(16, strip_in.at[0], strip_in.at[1], 8)

    @pl.when(at_south)
    def _():
        row_in[1] = jnp.zeros(row_in.shape[1:], jnp.float32)
        for slot in (SE, SW):
            corner_in[CORNER[slot]] = jnp.zeros(corner_in.shape[1:], jnp.float32)

    @pl.when(jnp.logical_not(at_south))
    def _():
        rows_south.wait_send()
        rows_north.wait_recv()

    @pl.when(jnp.logical_not(at_north))
    def _():
        rows_north.wait_send()
        rows_south.wait_recv()

    @pl.when(at_north)
    def _():
        rows_fold.wait()

    for slot, row in ((1, 4), (0, 24)):
        for g, (a, b) in enumerate(fields):
            for k in range(nk):
                a[k, row : row + 4, :] = row_in[slot, g * nk + k, 0:4, :]
                b[k, row : row + 4, :] = row_in[slot, g * nk + k, 4:8, :]
        floor[row : row + 4, :] = row_in[slot, 2 * nk, 0:4, :]

    stage_flux(main, [(4, 8, 1, 5), (20, 8, 3, 7)])
    stage_ratio(main, [(4, 8, 2, 6), (20, 8, 2, 6)])
    stage_limit(main, [(4, 8, 3, 7), (20, 8, 1, 5)])

    def emit_outer(k, wi, m, val):
        if wi == 0:
            outs[m][k, 0:4, :] = val[4:8]
        else:
            outs[m][k, 12:16, :] = val[4:8]

    stage_diffuse(main, [(4, 8, 4, 8), (16, 8, 4, 8)], emit_outer)

    strip_tile(0)
    strip_tile(24)

    @pl.when(jnp.logical_not(at_south))
    def _():
        for copy in corners_south:
            copy.wait_send()
        for copy in corners_north:
            copy.wait_recv()

    @pl.when(jnp.logical_not(at_north))
    def _():
        for copy in corners_north:
            copy.wait_send()
        for copy in corners_south:
            copy.wait_recv()

    @pl.when(at_north)
    def _():
        for copy, local, own in corners_fold:
            pl.when(own)(local.wait)
            pl.when(jnp.logical_not(own))(copy.wait)

    strip_halo(0, corner_in.at[CORNER[SE]], corner_in.at[CORNER[SW]], 0)
    strip_halo(24, corner_in.at[CORNER[NE]], corner_in.at[CORNER[NW]], 0)

    def strip_density(one):
        x = one[0]
        low_half = lane_iota(x.shape[0]) < 64
        own = jnp.where(low_half, -thermal_coef, haline_coef)
        other = jnp.where(low_half, haline_coef, -thermal_coef)
        return own * x + other * pltpu.roll(x, 64, 1)

    strips = dict(split=True, t=[e_tr], u=e_u, v=e_v, f=e_floor, density=strip_density)
    names = dict(low=e_low, mx=e_mx, mn=e_mn, ax=e_ax, ay=e_ay, az=e_az, rin=e_rin, rout=e_rout, adv=e_adv)
    strips.update({name: [ref] for name, ref in names.items()})
    stage_flux(strips, [(4, 24, 0, 24)])
    stage_ratio(strips, [(4, 24, 0, 24)])
    stage_limit(strips, [(4, 24, 0, 24)])

    def emit_strip(k, wi, m, val, add=False):
        e_res[k] = e_res[k] + val[4:20] if add else val[4:20]

    stage_diffuse(strips, [(4, 24, 4, 20)], emit_strip)


def finish(t_ref, s_ref, e_res, t_hbm, s_hbm, t_buf, s_buf, sem):
    lane16 = lane_iota(16)
    rim = jnp.logical_or(lane16 < 4, lane16 >= 124)
    copies = []
    for m, (ref, buf, out) in enumerate(((t_ref, t_buf, t_hbm), (s_ref, s_buf, s_hbm))):
        back = jnp.where(lane16 < 4, lane16 + 20, jnp.where(lane16 >= 124, lane16 - 116, 0)) + 64 * m
        half = e_res.shape[0]
        for k in range(ref.shape[0]):
            edge = jnp.take_along_axis(e_res[k % half], back + 32 * (k // half), axis=1)
            buf[k] = jnp.where(rim, edge, ref[k])
        copies.append(pltpu.make_async_copy(buf, out, sem.at[m]))
        copies[-1].start()
    for copy in copies:
        copy.wait()


def on_device(t, s, u, v, flag, point, count):
    nk = t.shape[0]
    f32 = jnp.float32
    vm = lambda *shape: pltpu.VMEM(shape, f32)
    big = lambda: vm(2, nk, 32, 128)
    one = lambda: vm(nk, 32, 128)
    whole = pl.BlockSpec(memory_space=pltpu.VMEM)
    hbm = pl.BlockSpec(memory_space=pltpu.HBM)
    part = pltpu.VMEM(t.shape, f32)
    main_t, main_s, strips = pl.pallas_call(
        kernel,
        out_shape=(part, part, pltpu.VMEM((nk // 2, *t.shape[1:]), f32)),
        in_specs=[hbm] * 7,
        out_specs=(whole, whole, whole),
        scratch_shapes=[
            pltpu.VMEM(flag.shape, flag.dtype), pltpu.VMEM(point.shape, point.dtype), pltpu.VMEM(count.shape, count.dtype),
            big(), one(), one(), vm(32, 128),
            *[big() for _ in range(9)],
            *[vm(nk // 2, 32, 128) for _ in range(3)], vm(32, 128),
            *[vm(nk // 2, 32, 128) for _ in range(9)],
            vm(2, 2 * nk + 1, 8, 128), vm(2, 2 * nk + 1, 8, 128),
            vm(nk // 2 + 1, 16, 128), vm(2, nk // 2 + 1, 16, 128),
            vm(nk // 2 + 1, 8, 128), vm(4, nk // 2 + 1, 8, 128),
            pltpu.SemaphoreType.DMA((7,)), pltpu.SemaphoreType.DMA((8,)), pltpu.SemaphoreType.DMA((8,)),
            pltpu.SemaphoreType.REGULAR((2,)),
        ],
        compiler_params=pltpu.CompilerParams(
            collective_id=0, has_side_effects=True, vmem_limit_bytes=60 * 1024 * 1024
        ),
    )(t, s, u, v, flag, point, count)
    result = jax.ShapeDtypeStruct(t.shape, f32)
    return pl.pallas_call(
        finish,
        out_shape=(result, result),
        in_specs=[whole] * 3,
        out_specs=(hbm, hbm),
        scratch_shapes=[vm(*t.shape), vm(*t.shape), pltpu.SemaphoreType.DMA((2,))],
        compiler_params=pltpu.CompilerParams(vmem_limit_bytes=4 * 1024 * 1024),
    )(main_t, main_s, strips)


def solution(mesh):
    grid = P(None, "lat", "lon")
    flat = P("lat", "lon")
    return jax.shard_map(
        on_device, mesh=mesh, in_specs=(grid,) * 4 + (flat,) * 3, out_specs=(grid, grid), check_vma=False
    )
```
